32 devices in a mesh: groups: 2 (over x), rows: 8 (over z, y), loop: 2 (over core).
Axes of the slice: x: 2, y: 2, z: 4, core: 2. Of those that a mesh axis runs over, the one named last changes fastest.
Arguments:
- frame_one: bfloat16 [32, 256, 256], P(('groups', 'rows')), parts along dimension 0, may hold values from -12.2 to 12.2
- frame_two: bfloat16 [32, 256, 256], P(('groups', 'rows'), 'loop'), parts along dimension 0, may hold values from -12.2 to 12.2
- context: bfloat16 [32, 256, 128], P(('groups', 'rows')), parts along dimension 0, may hold values from -6 to 6
- carry_hidden: bfloat16 [24576, 128], P(('groups', 'rows')), parts along dimension 0, may hold values from -1 to 1
- carry_flow: bfloat16 [24576, 2], P(('groups', 'rows')), parts along dimension 0, may hold values from -48 to 48
- slot_target: int32 [24576], P(('groups', 'rows')), parts along dimension 0, may hold values from 0 to 4095, as said below
- slot_count: int32 [16], P(('groups', 'rows')), parts along dimension 0, may hold values from 8 to 1536, as said below
- match_weight: bfloat16 [512, 128], replicated, may hold values from -0.25 to 0.25
- offset_weight: float32 [6, 128], replicated, may hold values from -2.5 to 2.5
- gate_weight: bfloat16 [2, 5, 384, 256], replicated, may hold values from -0.125 to 0.125
- state_weight: bfloat16 [2, 5, 384, 128], replicated, may hold values from -0.125 to 0.125
- gru_bias: float32 [2, 384], replicated, may hold values from -3 to 3
- head_weight: bfloat16 [128, 256], replicated, may hold values from -0.5 to 0.5
- delta_weight: bfloat16 [2, 256], replicated, may hold values from -0.375 to 0.375
Outputs:
- hidden_out: float32 [32, 256, 128], P(('groups', 'rows')), parts along dimension 0
- flow_out: float32 [2, 32, 256], P(None, ('groups', 'rows')), parts along dimension 1
The draws below stay inside these ranges and needn't reach their ends.
There are 2 independent parts, one for each index of `groups`. The reference program is written for one: setup_inputs(seed, part) draws one part's arguments, and reference() takes and returns one part's arrays. A program takes and returns all parts, laid end to end along the dimension named above; an argument that names none is the same for every part. Nothing has to cross between parts.
Inputs may be any that keep to these rules, and one draw needn't show every extreme that they name: `slot_target`: over all blocks, the counted slots (the first slot_count[b] of block b of 1536) name every pixel index exactly once, so that every index r of rows, owning pixel indices r * 512 to (r + 1) * 512 - 1, gets exactly 512 counted slots. Of one block's counted slots at most 192 belong to one index of rows, and some block has 192 for every index. Slots past the count hold arbitrary pixel indices. `slot_count`: some block has all 1536 slots counted.
All inputs are finite; a program needn't handle non-finite values.
Results may differ from the reference program's by a relative error of at most 0.0035.
Values may be sent and summed in bfloat16 or wider, within the bound.
No kernel may reach another device: no remote copies, remote signals or barrier semaphores. Data moves between devices by JAX's collectives and lax.ppermute only.
A program may use at most 128 MiB of HBM per device.

```python
import math
import jax
import jax.numpy as jnp
from jax import lax

C = 256
HID = 128
CTX = 128
MOT = 128
FLOWH = 256
TAPS = 5
ITERS = 2
H = 16
W = 256
PIX = 512
CAP = 192
SLOTS = 1536
N_ROWS = 8


def frame_pair(key):
    pixel_count = H * W
    key_perm = jax.random.fold_in(key, 71)
    key_first = jax.random.fold_in(key, 72)
    key_jitter = jax.random.fold_in(key, 73)
    matching = jax.random.permutation(key_perm, pixel_count).astype(jnp.int32)
    first_frame = jnp.clip(jax.random.normal(key_first, (pixel_count, C), jnp.float32), -6.0, 6.0)
    jitter = jnp.clip(jax.random.normal(key_jitter, (pixel_count, C), jnp.float32), -6.0, 6.0)
    second_frame = 0.75 * first_frame[matching] + 0.66 * jitter
    return (first_frame.reshape(H, W, C), second_frame.reshape(H, W, C))


def draw_frame_one(key, part):
    return frame_pair(key)[0].astype(jnp.bfloat16)


def draw_frame_two(key, part):
    return frame_pair(key)[1].astype(jnp.bfloat16)


def share_loads(key, capacity):
    members = jnp.arange(N_ROWS, dtype=jnp.int32)
    chosen = jax.random.randint(jax.random.fold_in(key, 1), (), 0, N_ROWS)
    weights = jax.random.randint(jax.random.fold_in(key, 2), (N_ROWS,), 2, 5)
    weights = jnp.where(members == chosen, 0, weights)
    spare_rows = PIX - (N_ROWS - 1) - capacity
    extra_rows = spare_rows * weights // jnp.sum(weights)
    remain = spare_rows - jnp.sum(extra_rows)
    others = members - (members > chosen).astype(jnp.int32)
    extra_rows = extra_rows + jnp.where((members != chosen) & (others < remain), 1, 0)
    return jnp.where(members == chosen, capacity, 1 + extra_rows).astype(jnp.int32)


def carry_plan(key):
    capacity = CAP
    load_counts = share_loads(jax.random.fold_in(key, 501), capacity)
    starts = jnp.cumsum(load_counts) - load_counts
    dest_orders = jax.vmap(lambda subkey: jax.random.permutation(subkey, PIX))(jax.random.split(jax.random.fold_in(key, 502), N_ROWS)).astype(jnp.int32)
    within = jnp.arange(capacity, dtype=jnp.int32)
    spot_index = jnp.minimum(starts[:, None] + within[None, :], PIX - 1)
    members = jnp.arange(N_ROWS, dtype=jnp.int32)
    picked = dest_orders[members[None, :, None], spot_index[:, None, :]]
    target_grid = (members[None, :, None] * PIX + picked).reshape(N_ROWS, SLOTS)
    counted = jnp.broadcast_to(within[None, None, :] < load_counts[:, None, None], (N_ROWS, N_ROWS, capacity)).reshape(N_ROWS, SLOTS)
    shuffles = jax.vmap(lambda subkey: jax.random.permutation(subkey, SLOTS))(jax.random.split(jax.random.fold_in(key, 503), N_ROWS)).astype(jnp.int32)
    scores = jnp.where(counted, 0, SLOTS) + shuffles
    ordering = jnp.argsort(scores, axis=1)
    sorted_targets = jnp.take_along_axis(target_grid, ordering, axis=1)
    counts = N_ROWS * load_counts
    leftover = jax.random.randint(jax.random.fold_in(key, 504), (N_ROWS, SLOTS), 0, H * W)
    in_count = jnp.arange(SLOTS, dtype=jnp.int32)[None, :] < counts[:, None]
    return (jnp.where(in_count, sorted_targets, leftover).reshape(-1).astype(jnp.int32), counts.astype(jnp.int32))


def draw_slot_target(key, part):
    return carry_plan(key)[0]


def draw_slot_count(key, part):
    return carry_plan(key)[1]


def levels(stream_key, dims, cuts, low, top_value):
    gain, own = 1.0, jax.random.fold_in(stream_key, 6)
    for position, parts in cuts:
        heights = jnp.exp(jax.random.uniform(jax.random.fold_in(own, position), (parts,), jnp.float32, low / len(cuts), top_value / len(cuts)))
        gain = gain * jnp.repeat(heights, dims[position] // parts).reshape([-1 if axis == position else 1 for axis in range(len(dims))])
    return gain


def centred(rng, extent, scale, most, shards=(), held_as=jnp.bfloat16):
    factor_of = levels(rng, extent, shards, -0.22, 0.18) if shards else 1.0
    array = jax.random.normal(rng, extent, jnp.float32) * scale * factor_of
    return jnp.minimum(jnp.maximum(array, -most), most).astype(held_as)


def setup_inputs(seed: int = 0, part: int = 0) -> dict:
    keys = jax.random.split(jax.random.key(seed), 15)
    part_splits = jax.random.split(jax.random.fold_in(keys[14], part), 15)
    frame_one = draw_frame_one(jax.random.fold_in(jax.random.fold_in(keys[14], part), 71), part)
    frame_two = draw_frame_two(jax.random.fold_in(jax.random.fold_in(keys[14], part), 71), part)
    context = centred(part_splits[2], (H, W, CTX), 1.0, 6.0, ((0, 8),))
    carry_hidden = jnp.clip(jax.random.uniform(part_splits[3], (N_ROWS * SLOTS, HID), jnp.float32, -1.0, 1.0) * levels(part_splits[3], (N_ROWS * SLOTS, HID), ((0, 8),), -0.4, 0.0), -1.0, 1.0).astype(jnp.bfloat16)
    carry_flow = centred(part_splits[4], (N_ROWS * SLOTS, 2), 8.0, 48.0, ((0, 8),))
    slot_target = draw_slot_target(jax.random.fold_in(jax.random.fold_in(keys[14], part), 71), part)
    slot_count = draw_slot_count(jax.random.fold_in(jax.random.fold_in(keys[14], part), 71), part)
    match_weight = centred(keys[7], (2 * C, MOT), (2 * C) ** -0.5, 0.25)
    offset_weight = centred(keys[8], (6, MOT), 6 ** -0.5, 2.5, (), jnp.float32)
    gate_weight = centred(keys[9], (2, TAPS, HID + CTX + MOT, 2 * HID), (TAPS * (HID + CTX + MOT)) ** -0.5, 0.125)
    state_weight = centred(keys[10], (2, TAPS, HID + CTX + MOT, HID), (TAPS * (HID + CTX + MOT)) ** -0.5, 0.125)
    gru_bias = centred(keys[11], (2, 3 * HID), 0.5, 3.0, (), jnp.float32)
    head_weight = centred(keys[12], (HID, FLOWH), HID ** -0.5, 0.5)
    delta_weight = centred(keys[13], (2, FLOWH), FLOWH ** -0.5, 0.375)
    return dict(frame_one=frame_one, frame_two=frame_two, context=context, carry_hidden=carry_hidden, carry_flow=carry_flow, slot_target=slot_target, slot_count=slot_count, match_weight=match_weight, offset_weight=offset_weight, gate_weight=gate_weight, state_weight=state_weight, gru_bias=gru_bias, head_weight=head_weight, delta_weight=delta_weight)


offset_scale = 0.03125

def pool_quads(frames):
    values = frames.astype(jnp.float32)
    summed = values[0::2, 0::2] + values[0::2, 1::2] + values[1::2, 0::2] + values[1::2, 1::2]
    return (summed * 0.25).astype(jnp.bfloat16)

def soft_match(scores, key_block, key_rows, key_cols):
    peak_now = lax.optimization_barrier(jnp.max(scores, axis=1))
    expo_terms = jnp.exp(scores - peak_now[:, None])
    weight_sum = lax.optimization_barrier(jnp.sum(expo_terms, axis=1))
    matched = (jnp.dot(expo_terms.astype(jnp.bfloat16), key_block, preferred_element_type=jnp.float32) / weight_sum[:, None]).astype(jnp.bfloat16)
    row_mean = lax.optimization_barrier(jnp.sum(expo_terms * key_rows[None, :], axis=1)) / weight_sum
    col_mean = lax.optimization_barrier(jnp.sum(expo_terms * key_cols[None, :], axis=1)) / weight_sum
    return (matched, row_mean, col_mean)

def conv_along(extended, weights, axis_index, length):
    outcome = None
    for tap_index in range(weights.shape[0]):
        window = lax.slice_in_dim(extended, tap_index, tap_index + length, axis=axis_index)
        product = jnp.dot(window.reshape(-1, window.shape[-1]), weights[tap_index], preferred_element_type=jnp.float32)
        outcome = product if outcome is None else outcome + product
    return outcome

def gated_pass(hidden, inputs, gate_taps, state_taps, bias_row, axis_index):
    hidden_size = hidden.shape[-1]
    rounded = hidden.astype(jnp.bfloat16)
    pad_spec = [(0, 0), (0, 0), (0, 0)]
    pad_spec[axis_index] = (2, 2)
    length = hidden.shape[axis_index]
    extended = jnp.pad(jnp.concatenate([rounded, inputs], axis=2), pad_spec)
    gate_values = jax.nn.sigmoid(conv_along(extended, gate_taps, axis_index, length) + bias_row[:2 * hidden_size])
    update_gate = gate_values[:, :hidden_size]
    reset_gate = gate_values[:, hidden_size:]
    reset_state = (reset_gate * rounded.reshape(-1, hidden_size).astype(jnp.float32)).astype(jnp.bfloat16).reshape(hidden.shape)
    cand_input = jnp.pad(jnp.concatenate([reset_state, inputs], axis=2), pad_spec)
    candidate = jnp.tanh(conv_along(cand_input, state_taps, axis_index, length) + bias_row[2 * hidden_size:])
    mixed = (1.0 - update_gate) * hidden.reshape(-1, hidden_size) + update_gate * candidate
    return mixed.reshape(hidden.shape)

def place_carries(carry_hidden, carry_flow, slot_target, slot_count):
    slot_index = jnp.arange(carry_hidden.shape[0], dtype=jnp.int32)
    counted = slot_index % SLOTS < slot_count[slot_index // SLOTS]
    landing = jnp.where(counted, slot_target, H * W).astype(jnp.int32)
    hidden = jnp.zeros((H * W, HID), jnp.float32).at[landing].set(carry_hidden.astype(jnp.float32), mode='drop')
    flow_field = jnp.zeros((H * W, 2), jnp.float32).at[landing].set(carry_flow.astype(jnp.float32), mode='drop')
    return (hidden, flow_field.T)

def reference(frame_one, frame_two, context, carry_hidden, carry_flow, slot_target, slot_count, match_weight, offset_weight, gate_weight, state_weight, gru_bias, head_weight, delta_weight):
    pixel_count = H * W
    fine_keys = frame_two.reshape(pixel_count, C)
    coarse_keys = pool_quads(frame_two).reshape(pixel_count // 4, C)
    fine_index = jnp.arange(pixel_count, dtype=jnp.int32)
    fine_rows = (fine_index // W).astype(jnp.float32)
    fine_cols = (fine_index % W).astype(jnp.float32)
    coarse_index = jnp.arange(pixel_count // 4, dtype=jnp.int32)
    coarse_rows = (coarse_index // (W // 2) * 2).astype(jnp.float32) + 0.5
    coarse_cols = (coarse_index % (W // 2) * 2).astype(jnp.float32) + 0.5

    def match_block(queries):
        fine_scores = jnp.dot(queries, fine_keys.T, preferred_element_type=jnp.float32) / math.sqrt(C)
        coarse_scores = lax.optimization_barrier(jnp.sum(fine_scores.reshape(-1, H // 2, 2, W // 2, 2), axis=(2, 4))).reshape(-1, pixel_count // 4) * 0.25
        return soft_match(fine_scores, fine_keys, fine_rows, fine_cols) + soft_match(coarse_scores, coarse_keys, coarse_rows, coarse_cols)
    outcome = lax.map(match_block, frame_one)
    matched_zero = outcome[0].reshape(pixel_count, C)
    row_zero = outcome[1].reshape(pixel_count) - fine_rows
    col_zero = outcome[2].reshape(pixel_count) - fine_cols
    matched_one = outcome[3].reshape(pixel_count, C)
    row_one = outcome[4].reshape(pixel_count) - fine_rows
    col_one = outcome[5].reshape(pixel_count) - fine_cols
    base_motion = jnp.dot(jnp.concatenate([matched_zero, matched_one], axis=1), match_weight, preferred_element_type=jnp.float32)
    hidden, flow_field = place_carries(carry_hidden, carry_flow, slot_target, slot_count)
    hidden = hidden.reshape(H, W, HID)
    context_rows = context.reshape(pixel_count, CTX)
    for iteration in range(ITERS):
        features = ((row_zero - flow_field[0]) * offset_scale, (col_zero - flow_field[1]) * offset_scale, (row_one - flow_field[0]) * offset_scale, (col_one - flow_field[1]) * offset_scale, flow_field[0] * offset_scale, flow_field[1] * offset_scale)
        motion = base_motion
        for feature_index in range(6):
            motion = motion + features[feature_index][:, None] * offset_weight[feature_index][None, :]
        motion = jax.nn.relu(motion)
        inputs = jnp.concatenate([context_rows, motion.astype(jnp.bfloat16)], axis=1).reshape(H, W, CTX + MOT)
        hidden = gated_pass(hidden, inputs, gate_weight[0], state_weight[0], gru_bias[0], 1)
        hidden = gated_pass(hidden, inputs, gate_weight[1], state_weight[1], gru_bias[1], 0)
        lifted = jax.nn.relu(jnp.dot(hidden.reshape(pixel_count, HID).astype(jnp.bfloat16), head_weight, preferred_element_type=jnp.float32)).astype(jnp.bfloat16)
        flow_field = flow_field + jnp.dot(delta_weight, lifted.T, preferred_element_type=jnp.float32)
    return (hidden, flow_field.reshape(2, H, W))
```

```python
import functools
import math

import jax
import jax.numpy as jnp
from jax import lax
from jax.experimental import pallas as pl
from jax.experimental.pallas import tpu as pltpu
from jax.sharding import PartitionSpec as P

ITERS = 2
WIN = 32
HALO = 8
TILE = 512
OFFSET_SCALE = 0.03125
F32 = jnp.float32
BF16 = jnp.bfloat16
VMEM = pltpu.VMEM
NT = (((1,), (1,)), ((), ()))


def iota(shape, dim):
    return lax.broadcasted_iota(jnp.int32, shape, dim)


def round_up(value, step):
    return -(-value // step) * step


def dot(a, b):
    return jnp.dot(a, b, preferred_element_type=F32)


def dot_nt(a, b):
    return lax.dot_general(a, b, NT, preferred_element_type=F32)


def vmem_specs(count):
    return [pl.BlockSpec(memory_space=VMEM)] * count


def smem_spec():
    return pl.BlockSpec(memory_space=pltpu.SMEM)


def loop(count, body, carry):
    return lax.fori_loop(0, count, body, carry, unroll=count <= 4)


def call(kernel, out_shape, in_specs, scratch, cost, *args):
    single = not isinstance(out_shape, (tuple, list))
    return pl.pallas_call(
        kernel,
        out_shape=out_shape,
        in_specs=in_specs,
        out_specs=vmem_specs(1)[0] if single else vmem_specs(len(out_shape)),
        scratch_shapes=scratch,
        compiler_params=pltpu.CompilerParams(vmem_limit_bytes=56 * 1024 * 1024),
        cost_estimate=pl.CostEstimate(flops=cost[0], bytes_accessed=cost[1], transcendentals=cost[2]),
    )(*args)


def pack_kernel(dests, cap, pixels, count_ref, target_ref, flow_ref, hidden_ref, out_ref):
    slots = target_ref.shape[1]
    target = target_ref[...]
    counted = iota((1, slots), 1) < count_ref[0]
    owner = target // pixels
    within = target % pixels
    belongs = (iota((dests, slots), 0) == owner) & counted
    member = jnp.where(belongs, 1.0, 0.0)
    upper = jnp.where(iota((128, 128), 0) <= iota((128, 128), 1), 1.0, 0.0).astype(BF16)
    before = jnp.zeros((dests, 1), F32)
    ranks = []
    for start in range(0, slots, 128):
        running = dot(member[:, start : start + 128].astype(BF16), upper) + before
        before = running[:, 127:128]
        ranks.append(running)
    rank = jnp.concatenate(ranks, axis=1) - 1.0
    place_at = jnp.sum(
        jnp.where(belongs, rank + iota((dests, slots), 0).astype(F32) * cap, 0.0), axis=0, keepdims=True
    )
    landing = jnp.where(counted, place_at, -1.0).astype(jnp.int32)
    row = iota((8, slots), 0)
    flow = flow_ref[...]
    side = jnp.where(row == 0, flow[0:1], 0.0)
    side = jnp.where(row == 1, flow[1:2], side)
    side = jnp.where(row == 2, (within // 256).astype(F32), side)
    side = jnp.where(row == 3, (within % 256).astype(F32), side)
    side = jnp.where(row == 4, 1.0, side).astype(BF16)
    hidden = hidden_ref[...]
    rows_hidden = round_up(cap, 16)
    together = max(1, min(dests, 192 // cap))
    for first in range(0, dests, together):
        spots = together * cap
        chosen = jnp.where(iota((spots, slots), 0) + first * cap == landing, 1.0, 0.0).astype(BF16)
        moved = dot(chosen, hidden)
        moved_side = dot_nt(side, chosen)
        for k in range(together):
            out_ref[first + k, 0:cap, :] = moved[k * cap : (k + 1) * cap].astype(BF16)
            for t in range(-(-cap // 128)):
                width = min(128, cap - t * 128)
                piece = moved_side[:, k * cap + t * 128 : k * cap + t * 128 + width]
                if width < 128:
                    piece = jnp.concatenate([piece, jnp.zeros((8, 128 - width), F32)], axis=1)
                base = rows_hidden + 8 * t
                out_ref[first + k, base : base + 8, :] = piece.astype(BF16)


def place_kernel(cap, half_wide, rows_per, where_ref, got_ref, ow_ref, hidden_ref, flow_ref, term_ref, wide_hidden, wide_term):
    half = where_ref[1]
    dests = got_ref.shape[0]
    pixels = flow_ref.shape[1]
    width = pixels // rows_per
    rows_hidden = round_up(cap, 16)
    hidden = jnp.zeros((pixels, 128), F32)
    flow = jnp.zeros((8, pixels), F32)
    for j in range(dests):
        pieces = []
        for t in range(-(-cap // 128)):
            base = rows_hidden + 8 * t
            pieces.append(got_ref[j, base : base + 8, 0 : min(128, cap - t * 128)].astype(F32))
        side = pieces[0] if len(pieces) == 1 else jnp.concatenate(pieces, axis=1)
        place = jnp.where(side[4:5] > 0.5, side[2:3] * 256.0 + side[3:4], -1.0).astype(jnp.int32)
        chosen = jnp.where(iota((pixels, cap), 0) == place, 1.0, 0.0).astype(BF16)
        hidden = hidden + dot(chosen, got_ref[j, 0:cap, :])
        flow = flow + dot_nt(side.astype(BF16), chosen)
    flow_ref[...] = flow
    columns = flow.T
    ow = ow_ref[...]
    term = columns[:, 0:1] * (OFFSET_SCALE * (ow[4:5] - ow[0:1] - ow[2:3])) + columns[:, 1:2] * (
        OFFSET_SCALE * (ow[5:6] - ow[1:2] - ow[3:4])
    )
    start = pl.multiple_of(half * (width // 2), 128)
    for wide, value, out in ((wide_hidden, hidden, hidden_ref), (wide_term, term, term_ref)):
        wide[...] = jnp.zeros_like(wide)
        for r in range(rows_per):
            wide[r, HALO : HALO + width, :] = value[r * width : (r + 1) * width]
            out[r] = wide[r, pl.ds(start, half_wide), :].astype(out.dtype)


def match_kernel(
    count, flip, half_wide, rows_per, where_ref, queries_ref, weight_ref, ow_ref, *refs
):
    key_refs, (keep_ref, send_ref, fine, coarse, scores, mixed, wide) = refs[:count], refs[count:]
    me, half = where_ref[0], where_ref[1]
    pixels, channels = queries_ref.shape
    width = pixels // rows_per
    columns = width // 2
    quarter = columns // 2
    chunks = fine.shape[0]
    shards = chunks * 2
    per_ref = shards // count
    spread = jnp.where(
        iota((columns, columns), 1)
        == jnp.where(iota((columns, columns), 0) < quarter, 2 * iota((columns, columns), 0), 2 * (iota((columns, columns), 0) - quarter) + 1),
        1.0,
        0.0,
    ).astype(BF16)

    def sort_shard(ref, m, shard, lane):
        even, odd = [], []
        for r in range(rows_per):
            parted = dot(spread, ref[m, r])
            even.append(parted[:quarter])
            odd.append(parted[quarter:])
            for p, part in ((0, even[-1]), (1, odd[-1])):
                g = 2 * r + p
                fine[shard, g * 2 * quarter + lane * quarter : g * 2 * quarter + (lane + 1) * quarter, :] = part.astype(BF16)
        pooled = (even[0] + odd[0] + even[1] + odd[1]) * 0.25
        coarse[shard, lane * quarter : (lane + 1) * quarter, :] = pooled.astype(BF16)

    if per_ref == 1:
        for m in range(shards):
            sort_shard(key_refs[m], 0, m // 2, m % 2)
    else:
        def sort_chunk(c, carry):
            for lane in range(2):
                sort_shard(key_refs[0], c * 2 + lane, c, lane)
            return carry

        lax.fori_loop(0, chunks, sort_chunk, 0)

    group = 2 * quarter
    tile = scores.shape[1]
    lane = iota((1, group), 1)
    lane_col = ((lane % quarter) * 2 + half * columns).astype(F32)
    ow = ow_ref[...] * OFFSET_SCALE
    weight = weight_ref[...]

    def lane_row(c):
        arrival = c * 2 + lane // quarter
        shard = lax.bitwise_xor(arrival, me) if flip else arrival
        return (shard * rows_per).astype(F32)

    wide[...] = jnp.zeros_like(wide)

    def one_tile(t, carry):
        first = pl.multiple_of(t * tile, tile)
        queries = queries_ref[pl.ds(first, tile), :] * jnp.asarray(1.0 / math.sqrt(channels), BF16)

        def score(c, peaks):
            values = dot_nt(queries, fine[c])
            scores[c] = values
            parts = [values[:, g * group : (g + 1) * group] for g in range(4)]
            blended = (parts[0] + parts[1] + parts[2] + parts[3]) * 0.25
            high = jnp.maximum(jnp.maximum(parts[0], parts[1]), jnp.maximum(parts[2], parts[3]))
            return jnp.maximum(peaks[0], high), jnp.maximum(peaks[1], blended)

        low = jnp.full((tile, group), -jnp.inf, F32)
        peaks = loop(chunks, score, (low, low))
        peak_fine = jnp.max(peaks[0], axis=1, keepdims=True)
        peak_coarse = jnp.max(peaks[1], axis=1, keepdims=True)

        def absorb(c, so_far):
            total, below, right, rows, c_total, c_rows, acc_fine, acc_coarse = so_far
            parts = [scores[c, :, g * group : (g + 1) * group] for g in range(4)]
            blended = (parts[0] + parts[1] + parts[2] + parts[3]) * 0.25
            expo = [jnp.exp(part - peak_fine) for part in parts]
            c_expo = jnp.exp(blended - peak_coarse)
            lower = expo[2] + expo[3]
            everything = expo[0] + expo[1] + lower
            at = lane_row(c)
            weights = jnp.concatenate([e.astype(BF16) for e in expo], axis=1)
            return (
                total + everything,
                below + lower,
                right + (expo[1] + expo[3]),
                rows + everything * at,
                c_total + c_expo,
                c_rows + c_expo * at,
                acc_fine + dot(weights, fine[c]),
                acc_coarse + dot(c_expo.astype(BF16), coarse[c]),
            )

        zero = jnp.zeros((tile, group), F32)
        blank = jnp.zeros((tile, channels), F32)
        total, below, right, rows, c_total, c_rows, acc_fine, acc_coarse = loop(
            chunks, absorb, (zero, zero, zero, zero, zero, zero, blank, blank)
        )

        def over(value):
            return jnp.sum(value, axis=1, keepdims=True)

        pixel = first + iota((tile, 1), 0)
        own_row = (me * rows_per + pixel // width).astype(F32)
        own_col = (pixel % width).astype(F32)
        fine_sum, coarse_sum = over(total), over(c_total)
        fine_row = over(rows + below) / fine_sum - own_row
        fine_col = over(total * lane_col + right) / fine_sum - own_col
        coarse_row = over(c_rows) / coarse_sum + 0.5 - own_row
        coarse_col = over(c_total * lane_col) / coarse_sum + 0.5 - own_col
        fine_out = dot((acc_fine / fine_sum).astype(BF16), weight[:channels])
        coarse_out = dot((acc_coarse / coarse_sum).astype(BF16), weight[channels:])
        mixed[pl.ds(first, tile), 0:128] = fine_out + fine_row * ow[0:1] + fine_col * ow[1:2]
        mixed[pl.ds(first, tile), 128:256] = coarse_out + coarse_row * ow[2:3] + coarse_col * ow[3:4]
        mixed[pl.ds(first, tile), 256:384] = jnp.where(
            iota((tile, 128), 1) < 64,
            peak_fine + jnp.log(fine_sum),
            peak_coarse + jnp.log(coarse_sum),
        )
        return carry

    lax.fori_loop(0, pixels // tile, one_tile, 0)
    start = pl.multiple_of(half * columns, 128)
    other = pl.multiple_of((1 - half) * columns, 128)
    for r in range(rows_per):
        wide[r, HALO : HALO + width, :] = mixed[r * width : (r + 1) * width, :]
        keep_ref[r] = wide[r, pl.ds(start, half_wide), :]
        send_ref[r] = wide[r, pl.ds(other, half_wide), :]


def merge_kernel(own, keep_ref, got_ref, term_ref, hidden_ref, out_ref):
    dests = out_ref.shape[0]
    for r in range(keep_ref.shape[0]):
        keep, got = keep_ref[r], got_ref[r]
        gap = got[:, 256:384] - keep[:, 256:384]
        share = 1.0 / (1.0 + jnp.exp(gap))
        share_fine, share_coarse = share[:, 0:1], share[:, 64:65]
        base = (
            got[:, 0:128]
            + (keep[:, 0:128] - got[:, 0:128]) * share_fine
            + got[:, 128:256]
            + (keep[:, 128:256] - got[:, 128:256]) * share_coarse
            + term_ref[r]
        )
        hidden = hidden_ref[r].astype(F32)
        for j in range(dests):
            out_ref[j, r * WIN : (r + 1) * WIN, 0:128] = base[j * own : j * own + WIN].astype(BF16)
            out_ref[j, r * WIN : (r + 1) * WIN, 128:256] = hidden[j * own : j * own + WIN].astype(BF16)


def window_kernel(own, half_wide, where_ref, context_ref, out_ref, wide):
    rows_per, width, _ = context_ref.shape
    start = pl.multiple_of(where_ref[1] * (width // 2), 128)
    wide[...] = jnp.zeros_like(wide)
    for r in range(rows_per):
        wide[r, HALO : HALO + width, :] = context_ref[r].astype(F32)
        part = wide[r, pl.ds(start, half_wide), :]
        for j in range(out_ref.shape[0]):
            out_ref[j, r * WIN : (r + 1) * WIN, :] = part[j * own : j * own + WIN].astype(BF16)


def sigmoid(x):
    return 1.0 / (1.0 + jnp.exp(-x))


def update_kernel(
    own, width, where_ref, got_ref, context_ref, ow_ref, gate_ref, state_ref, bias_ref, head_ref, delta_ref,
    out_ref, base, hidden, inputs, states, resets, updates, col_in, col_st, flow, flow_cols,
):
    me, half = where_ref[0], where_ref[1]
    dests, per_dest, _ = got_ref.shape
    rows_per = per_dest // WIN
    count = dests * per_dest
    pad = 2 * WIN
    tiles = count // TILE
    first_col = (half * dests + me) * own - HALO
    column = first_col + iota((TILE, 128), 0) % WIN
    inside = (column >= 0) & (column < width)
    mask = jnp.where(inside, 1.0, 0.0)
    ow = ow_ref[...]
    add_row = OFFSET_SCALE * (ow[4:5] - ow[0:1] - ow[2:3])
    add_col = OFFSET_SCALE * (ow[5:6] - ow[1:2] - ow[3:4])
    bias = bias_ref[...]

    for ref in (inputs, states, resets):
        ref[0:pad, :] = jnp.zeros((pad, ref.shape[1]), BF16)
        ref[pad + count : pad + count + pad, :] = jnp.zeros((pad, ref.shape[1]), BF16)
    for j in range(dests):
        at = j * per_dest
        base[at : at + per_dest, :] = got_ref[j, :, 0:128]
        hidden[at : at + per_dest, :] = got_ref[j, :, 128:256].astype(F32)
        inputs[pad + at : pad + at + per_dest, 0:128] = context_ref[j]
    flow[...] = jnp.zeros_like(flow)
    flow_cols[...] = jnp.zeros_like(flow_cols)

    def each(body):
        def step(t, carry):
            body(pl.multiple_of(t * TILE, TILE))
            return carry

        lax.fori_loop(0, tiles, step, 0, unroll=tiles == 1)

    def shifted(value, tap):
        return value if tap == 2 else pltpu.roll(value, (2 - tap) % TILE, 0)

    def finish(at, update, candidate):
        old = hidden[pl.ds(at, TILE), :]
        hidden[pl.ds(at, TILE), :] = ((1.0 - update) * old + update * candidate) * mask

    for iteration in range(ITERS):

        def columns_pass(at):
            motion = base[pl.ds(at, TILE), :].astype(F32)
            if iteration > 0:
                moved = flow_cols[pl.ds(at, TILE), :]
                motion = (motion + moved[:, 0:1] * add_row + moved[:, 1:2] * add_col) * mask
            motion = jnp.maximum(motion, 0.0)
            inputs[pl.ds(pad + at, TILE), 128:256] = motion.astype(BF16)
            context = inputs[pl.ds(pad + at, TILE), 0:128].astype(F32)
            motion = motion.astype(BF16).astype(F32)
            state = hidden[pl.ds(at, TILE), :].astype(BF16).astype(F32)
            for tap in range(5):
                if iteration == 0:
                    col_in[pl.ds(at, TILE), tap * 256 : tap * 256 + 128] = shifted(context, tap).astype(BF16)
                col_in[pl.ds(at, TILE), tap * 256 + 128 : tap * 256 + 256] = shifted(motion, tap).astype(BF16)
                col_st[:, tap * 128 : (tap + 1) * 128] = shifted(state, tap).astype(BF16)
            gates = dot(col_st[...], gate_ref[0, :, 0:128, :].reshape(640, 256)) + dot(
                col_in[pl.ds(at, TILE), :], gate_ref[0, :, 128:384, :].reshape(1280, 256)
            )
            gates = sigmoid(gates + bias[0:1, 0:256])
            reset = (gates[:, 128:256] * state).astype(BF16).astype(F32)
            for tap in range(5):
                col_st[:, tap * 128 : (tap + 1) * 128] = shifted(reset, tap).astype(BF16)
            candidate = dot(col_st[...], state_ref[0, :, 0:128, :].reshape(640, 128)) + dot(
                col_in[pl.ds(at, TILE), :], state_ref[0, :, 128:384, :].reshape(1280, 128)
            )
            finish(at, gates[:, 0:128], jnp.tanh(candidate + bias[0:1, 256:384]))
            states[pl.ds(pad + at, TILE), :] = hidden[pl.ds(at, TILE), :].astype(BF16)

        def gate_rows(at):
            total = None
            for tap in range(5):
                part = dot(states[pl.ds(at + tap * WIN, TILE), :], gate_ref[1, tap, 0:128, :]) + dot(
                    inputs[pl.ds(at + tap * WIN, TILE), :], gate_ref[1, tap, 128:384, :]
                )
                total = part if total is None else total + part
            gates = sigmoid(total + bias[1:2, 0:256])
            updates[pl.ds(at, TILE), :] = gates[:, 0:128]
            resets[pl.ds(pad + at, TILE), :] = (
                gates[:, 128:256] * states[pl.ds(pad + at, TILE), :].astype(F32)
            ).astype(BF16)

        def state_rows(at):
            total = None
            for tap in range(5):
                part = dot(resets[pl.ds(at + tap * WIN, TILE), :], state_ref[1, tap, 0:128, :]) + dot(
                    inputs[pl.ds(at + tap * WIN, TILE), :], state_ref[1, tap, 128:384, :]
                )
                total = part if total is None else total + part
            finish(at, updates[pl.ds(at, TILE), :], jnp.tanh(total + bias[1:2, 256:384]))
            lifted = jnp.maximum(dot(hidden[pl.ds(at, TILE), :].astype(BF16), head_ref[...]), 0.0).astype(BF16)
            step = dot_nt(delta_ref[...], lifted)
            flow[:, pl.ds(at, TILE)] = flow[:, pl.ds(at, TILE)] + step
            flow_cols[pl.ds(at, TILE), :] = flow_cols[pl.ds(at, TILE), :] + step.T

        each(columns_pass)
        each(gate_rows)
        each(state_rows)

    for j in range(dests):
        for r in range(rows_per):
            at = j * per_dest + r * WIN + HALO
            out_ref[j, r * own : (r + 1) * own, :] = hidden[at : at + own, :]
        moved = flow[:, j * per_dest : (j + 1) * per_dest]
        out_ref[j, rows_per * own : rows_per * own + 8, :] = jnp.concatenate(
            [moved, jnp.zeros((8, 128 - per_dest), F32)], axis=1
        )


def local(
    frame_one,
    frame_two,
    context,
    carry_hidden,
    carry_flow,
    slot_target,
    slot_count,
    match_weight,
    offset_weight,
    gate_weight,
    state_weight,
    gru_bias,
    head_weight,
    delta_weight,
):
    half = lax.axis_index("loop")
    me = lax.axis_index("rows")
    dests = lax.axis_size("rows")
    halves = lax.axis_size("loop")
    rows_per, width, channels = frame_one.shape
    columns = frame_two.shape[1]
    pixels = rows_per * width
    slots, hidden_size = carry_hidden.shape
    cap = slots // dests
    own = columns // dests
    half_wide = round_up(columns - own + WIN, 8)
    padded = columns + half_wide
    here = jnp.stack([me, half]).astype(jnp.int32)

    shard = frame_two.reshape(1, rows_per, columns, channels)
    if dests == 8:

        def swap(value, flip):
            return lax.ppermute(value, "rows", [(i, i ^ flip) for i in range(dests)])

        beside, near, across, wrap = (swap(shard, flip) for flip in (1, 2, 4, 6))
        keys = (shard, beside, near, swap(near, 1), across, swap(across, 1), wrap, swap(wrap, 1))
    else:
        keys = (lax.all_gather(shard, "rows", axis=0, tiled=True),)

    rows_hidden = round_up(cap, 16)
    rows_slot = rows_hidden + round_up(8 * (-(-cap // 128)), 16)
    packed = call(
        functools.partial(pack_kernel, dests, cap, pixels),
        jax.ShapeDtypeStruct((dests, rows_slot, hidden_size), BF16),
        [smem_spec()] + vmem_specs(3),
        [],
        (2 * slots * slots * 128, 1 << 20, 0),
        slot_count,
        slot_target.reshape(1, slots),
        carry_flow.T.astype(F32),
        carry_hidden,
    )
    windows = call(
        functools.partial(window_kernel, own, half_wide),
        jax.ShapeDtypeStruct((dests, rows_per * WIN, hidden_size), BF16),
        [smem_spec()] + vmem_specs(1),
        [pltpu.VMEM((rows_per, padded, 128), F32)],
        (0, 1 << 18, 0),
        here,
        context,
    )
    early = lax.all_to_all(jnp.concatenate([packed, windows], axis=1), "rows", 0, 0, tiled=True)
    ow = jnp.pad(offset_weight, ((0, 2), (0, 0)))
    hidden_wide, flow_first, term = call(
        functools.partial(place_kernel, cap, half_wide, rows_per),
        (
            jax.ShapeDtypeStruct((rows_per, half_wide, 128), BF16),
            jax.ShapeDtypeStruct((8, pixels), F32),
            jax.ShapeDtypeStruct((rows_per, half_wide, 128), F32),
        ),
        [smem_spec()] + vmem_specs(2),
        [pltpu.VMEM((rows_per, padded, 128), F32)] * 2,
        (2 * slots * pixels * 128, 1 << 20, 0),
        here,
        early,
        ow,
    )
    chunks = dests // 2
    tile = 128
    keep, send = call(
        functools.partial(match_kernel, len(keys), len(keys) > 1, half_wide, rows_per),
        (jax.ShapeDtypeStruct((rows_per, half_wide, 384), F32),) * 2,
        [smem_spec()] + vmem_specs(3 + len(keys)),
        [
            pltpu.VMEM((chunks, 4 * columns, channels), BF16),
            pltpu.VMEM((chunks, columns, channels), BF16),
            pltpu.VMEM((chunks, tile, 4 * columns), F32),
            pltpu.VMEM((pixels, 384), F32),
            pltpu.VMEM((rows_per, padded, 384), F32),
        ],
        (4 * pixels * chunks * 4 * columns * channels, 1 << 21, pixels * chunks * 5 * columns),
        here,
        frame_one.reshape(pixels, channels),
        match_weight,
        ow,
        *keys,
    )
    other = lax.ppermute(send, "loop", [(i, (i + 1) % halves) for i in range(halves)])
    sending = call(
        functools.partial(merge_kernel, own),
        jax.ShapeDtypeStruct((dests, rows_per * WIN, 256), BF16),
        vmem_specs(4),
        [],
        (0, 1 << 20, 0),
        keep,
        other,
        term,
        hidden_wide,
    )
    arrived = lax.all_to_all(sending, "rows", 0, 0, tiled=True)
    count = dests * rows_per * WIN
    back_rows = rows_per * own + 8
    outgoing = call(
        functools.partial(update_kernel, own, width),
        jax.ShapeDtypeStruct((dests, back_rows, 128), F32),
        [smem_spec()] + vmem_specs(8),
        [
            pltpu.VMEM((count, 128), BF16),
            pltpu.VMEM((count, 128), F32),
            pltpu.VMEM((count + 4 * WIN, 256), BF16),
            pltpu.VMEM((count + 4 * WIN, 128), BF16),
            pltpu.VMEM((count + 4 * WIN, 128), BF16),
            pltpu.VMEM((count, 128), F32),
            pltpu.VMEM((count, 1280), BF16),
            pltpu.VMEM((TILE, 640), BF16),
            pltpu.VMEM((8, count), F32),
            pltpu.VMEM((count, 8), F32),
        ],
        (16 * count * 5 * 384 * 256, 1 << 22, 8 * count * 384),
        here,
        arrived,
        early[:, rows_slot:, :],
        ow,
        gate_weight,
        state_weight,
        gru_bias,
        head_weight,
        jnp.pad(delta_weight, ((0, 6), (0, 0))),
    )
    back = lax.all_to_all(outgoing, "rows", 0, 0, tiled=True)
    both = lax.all_gather(back, "loop", axis=0)
    cells = both[:, :, : rows_per * own, :].reshape(halves, dests, rows_per, own, hidden_size)
    hidden_out = cells.transpose(2, 0, 1, 3, 4).reshape(rows_per, width, hidden_size)
    moved = both[:, :, rows_per * own : rows_per * own + 2, : rows_per * WIN]
    moved = moved.reshape(halves, dests, 2, rows_per, WIN)[..., HALO : HALO + own]
    moved = moved.transpose(2, 3, 0, 1, 4).reshape(2, rows_per, width)
    flow_out = flow_first[:2].reshape(2, rows_per, width) + moved
    return (hidden_out, flow_out)


def solution(mesh):
    return jax.shard_map(
        local,
        mesh=mesh,
        in_specs=(
            P(("groups", "rows"), None, None),
            P(("groups", "rows"), "loop", None),
            P(("groups", "rows"), None, None),
            P(("groups", "rows"), None),
            P(("groups", "rows"), None),
            P(("groups", "rows")),
            P(("groups", "rows")),
            P(),
            P(),
            P(),
            P(),
            P(),
            P(),
            P(),
        ),
        out_specs=(P(("groups", "rows"), None, None), P(None, ("groups", "rows"), None)),
        check_vma=False,
    )
```

```python
import functools
import math

import jax
import jax.numpy as jnp
from jax import lax
from jax.experimental import pallas as pl
from jax.experimental.pallas import tpu as pltpu
from jax.sharding import PartitionSpec as P

ITERS = 2
WIN = 32
HALO = 8
TILE = 512
OFFSET_SCALE = 0.03125
F32 = jnp.float32
BF16 = jnp.bfloat16
VMEM = pltpu.VMEM
NT = (((1,), (1,)), ((), ()))


def iota(shape, dim):
    return lax.broadcasted_iota(jnp.int32, shape, dim)


def round_up(value, step):
    return -(-value // step) * step


def dot(a, b):
    return jnp.dot(a, b, preferred_element_type=F32)


def dot_nt(a, b):
    return lax.dot_general(a, b, NT, preferred_element_type=F32)


def vmem_specs(count):
    return [pl.BlockSpec(memory_space=VMEM)] * count


def smem_spec():
    return pl.BlockSpec(memory_space=pltpu.SMEM)


def loop(count, body, carry):
    return lax.fori_loop(0, count, body, carry, unroll=count <= 4)


def call(kernel, out_shape, in_specs, scratch, cost, room, *args):
    single = not isinstance(out_shape, (tuple, list))
    return pl.pallas_call(
        kernel,
        out_shape=out_shape,
        in_specs=in_specs,
        out_specs=vmem_specs(1)[0] if single else vmem_specs(len(out_shape)),
        scratch_shapes=scratch,
        compiler_params=pltpu.CompilerParams(vmem_limit_bytes=room * 1024 * 1024),
        cost_estimate=pl.CostEstimate(flops=cost[0], bytes_accessed=cost[1], transcendentals=cost[2]),
    )(*args)


def pack_kernel(dests, cap, pixels, own, half_wide, count_ref, target_ref, flow_ref, hidden_ref, context_ref, out_ref, wide):
    slots = hidden_ref.shape[0]
    target = jnp.concatenate([target_ref[k : k + 1, :] for k in range(slots // 128)], axis=1)
    counted = iota((1, slots), 1) < count_ref[0]
    owner = target // pixels
    within = target % pixels
    belongs = (iota((dests, slots), 0) == owner) & counted
    member = jnp.where(belongs, 1.0, 0.0)
    upper = jnp.where(iota((128, 128), 0) <= iota((128, 128), 1), 1.0, 0.0).astype(BF16)
    before = jnp.zeros((dests, 1), F32)
    ranks = []
    for start in range(0, slots, 128):
        running = dot(member[:, start : start + 128].astype(BF16), upper) + before
        before = running[:, 127:128]
        ranks.append(running)
    rank = jnp.concatenate(ranks, axis=1) - 1.0
    place_at = jnp.sum(
        jnp.where(belongs, rank + iota((dests, slots), 0).astype(F32) * cap, 0.0), axis=0, keepdims=True
    )
    landing = jnp.where(counted, place_at, -1.0).astype(jnp.int32)
    row = iota((8, slots), 0)
    flow = flow_ref[...].astype(F32)
    side = jnp.where(row == 0, flow[0:1], 0.0)
    side = jnp.where(row == 1, flow[1:2], side)
    side = jnp.where(row == 2, (within // 256).astype(F32), side)
    side = jnp.where(row == 3, (within % 256).astype(F32), side)
    side = jnp.where(row == 4, 1.0, side).astype(BF16)
    hidden = hidden_ref[...]
    rows_hidden = round_up(cap, 16)
    together = max(1, min(dests, 192 // cap))
    for first in range(0, dests, together):
        spots = together * cap
        chosen = jnp.where(iota((spots, slots), 0) + first * cap == landing, 1.0, 0.0).astype(BF16)
        moved = dot(chosen, hidden)
        moved_side = dot_nt(side, chosen)
        for k in range(together):
            out_ref[first + k, 0:cap, :] = moved[k * cap : (k + 1) * cap].astype(BF16)
            for t in range(-(-cap // 128)):
                width = min(128, cap - t * 128)
                piece = moved_side[:, k * cap + t * 128 : k * cap + t * 128 + width]
                if width < 128:
                    piece = jnp.concatenate([piece, jnp.zeros((8, 128 - width), F32)], axis=1)
                base = rows_hidden + 8 * t
                out_ref[first + k, base : base + 8, :] = piece.astype(BF16)
    rows_per, width, _ = context_ref.shape
    top = out_ref.shape[1] - rows_per * WIN
    start = pl.multiple_of(lax.axis_index("loop") * (width // 2), 128)
    wide[...] = jnp.zeros_like(wide)
    for r in range(rows_per):
        wide[r, HALO : HALO + width, :] = context_ref[r].astype(F32)
        part = wide[r, pl.ds(start, half_wide), :]
        for j in range(dests):
            out_ref[j, top + r * WIN : top + (r + 1) * WIN, :] = part[j * own : j * own + WIN].astype(BF16)


def place_kernel(cap, half_wide, rows_per, got_ref, ow_ref, hidden_ref, flow_ref, term_ref, wide_hidden, wide_term):
    half = lax.axis_index("loop")
    dests = got_ref.shape[0]
    pixels = flow_ref.shape[1]
    width = pixels // rows_per
    rows_hidden = round_up(cap, 16)
    hidden = jnp.zeros((pixels, 128), F32)
    flow = jnp.zeros((8, pixels), F32)
    for j in range(dests):
        pieces = []
        for t in range(-(-cap // 128)):
            base = rows_hidden + 8 * t
            pieces.append(got_ref[j, base : base + 8, 0 : min(128, cap - t * 128)].astype(F32))
        side = pieces[0] if len(pieces) == 1 else jnp.concatenate(pieces, axis=1)
        place = jnp.where(side[4:5] > 0.5, side[2:3] * 256.0 + side[3:4], -1.0).astype(jnp.int32)
        chosen = jnp.where(iota((pixels, cap), 0) == place, 1.0, 0.0).astype(BF16)
        hidden = hidden + dot(chosen, got_ref[j, 0:cap, :])
        flow = flow + dot_nt(side.astype(BF16), chosen)
    flow_ref[...] = flow
    columns = flow.T
    ow = ow_ref[...]
    term = columns[:, 0:1] * (OFFSET_SCALE * (ow[4:5] - ow[0:1] - ow[2:3])) + columns[:, 1:2] * (
        OFFSET_SCALE * (ow[5:6] - ow[1:2] - ow[3:4])
    )
    start = pl.multiple_of(half * (width // 2), 128)
    for wide, value, out in ((wide_hidden, hidden, hidden_ref), (wide_term, term, term_ref)):
        wide[...] = jnp.zeros_like(wide)
        for r in range(rows_per):
            wide[r, HALO : HALO + width, :] = value[r * width : (r + 1) * width]
            out[r] = wide[r, pl.ds(start, half_wide), :].astype(out.dtype)


def match_kernel(
    count, flip, half_wide, rows_per, queries_ref, weight_ref, ow_ref, *refs
):
    key_refs, (keep_ref, send_ref, fine, coarse, scores, mixed, wide) = refs[:count], refs[count:]
    me, half = lax.axis_index("rows"), lax.axis_index("loop")
    pixels, channels = queries_ref.shape
    width = pixels // rows_per
    columns = width // 2
    quarter = columns // 2
    chunks = fine.shape[0]
    shards = chunks * 2
    per_ref = shards // count
    spread = jnp.where(
        iota((columns, columns), 1)
        == jnp.where(iota((columns, columns), 0) < quarter, 2 * iota((columns, columns), 0), 2 * (iota((columns, columns), 0) - quarter) + 1),
        1.0,
        0.0,
    ).astype(BF16)

    def sort_shard(ref, m, shard, lane):
        even, odd = [], []
        for r in range(rows_per):
            parted = dot(spread, ref[m, r])
            even.append(parted[:quarter])
            odd.append(parted[quarter:])
            for p, part in ((0, even[-1]), (1, odd[-1])):
                g = 2 * r + p
                fine[shard, g * 2 * quarter + lane * quarter : g * 2 * quarter + (lane + 1) * quarter, :] = part.astype(BF16)
        pooled = (even[0] + odd[0] + even[1] + odd[1]) * 0.25
        coarse[shard, lane * quarter : (lane + 1) * quarter, :] = pooled.astype(BF16)

    if per_ref == 1:
        for m in range(shards):
            sort_shard(key_refs[m], 0, m // 2, m % 2)
    else:
        def sort_chunk(c, carry):
            for lane in range(2):
                sort_shard(key_refs[0], c * 2 + lane, c, lane)
            return carry

        lax.fori_loop(0, chunks, sort_chunk, 0)

    group = 2 * quarter
    tile = scores.shape[1]
    lane = iota((1, group), 1)
    lane_col = ((lane % quarter) * 2 + half * columns).astype(F32)
    ow = ow_ref[...] * OFFSET_SCALE
    weight = weight_ref[...]

    def lane_row(c):
        arrival = c * 2 + lane // quarter
        shard = lax.bitwise_xor(arrival, me) if flip else arrival
        return (shard * rows_per).astype(F32)

    wide[...] = jnp.zeros_like(wide)

    def one_tile(t, carry):
        first = pl.multiple_of(t * tile, tile)
        queries = queries_ref[pl.ds(first, tile), :] * jnp.asarray(1.0 / math.sqrt(channels), BF16)

        def score(c, peaks):
            values = dot_nt(queries, fine[c])
            scores[c] = values
            parts = [values[:, g * group : (g + 1) * group] for g in range(4)]
            blended = (parts[0] + parts[1] + parts[2] + parts[3]) * 0.25
            high = jnp.maximum(jnp.maximum(parts[0], parts[1]), jnp.maximum(parts[2], parts[3]))
            return jnp.maximum(peaks[0], high), jnp.maximum(peaks[1], blended)

        low = jnp.full((tile, group), -jnp.inf, F32)
        peaks = loop(chunks, score, (low, low))
        peak_fine = jnp.max(peaks[0], axis=1, keepdims=True)
        peak_coarse = jnp.max(peaks[1], axis=1, keepdims=True)

        def absorb(c, so_far):
            total, below, right, rows, c_total, c_rows, acc_fine, acc_coarse = so_far
            parts = [scores[c, :, g * group : (g + 1) * group] for g in range(4)]
            blended = (parts[0] + parts[1] + parts[2] + parts[3]) * 0.25
            expo = [jnp.exp(part - peak_fine) for part in parts]
            c_expo = jnp.exp(blended - peak_coarse)
            lower = expo[2] + expo[3]
            everything = expo[0] + expo[1] + lower
            at = lane_row(c)
            weights = jnp.concatenate([e.astype(BF16) for e in expo], axis=1)
            return (
                total + everything,
                below + lower,
                right + (expo[1] + expo[3]),
                rows + everything * at,
                c_total + c_expo,
                c_rows + c_expo * at,
                acc_fine + dot(weights, fine[c]),
                acc_coarse + dot(c_expo.astype(BF16), coarse[c]),
            )

        zero = jnp.zeros((tile, group), F32)
        blank = jnp.zeros((tile, channels), F32)
        total, below, right, rows, c_total, c_rows, acc_fine, acc_coarse = loop(
            chunks, absorb, (zero, zero, zero, zero, zero, zero, blank, blank)
        )

        def over(value):
            return jnp.sum(value, axis=1, keepdims=True)

        pixel = first + iota((tile, 1), 0)
        own_row = (me * rows_per + pixel // width).astype(F32)
        own_col = (pixel % width).astype(F32)
        fine_sum, coarse_sum = over(total), over(c_total)
        fine_row = over(rows + below) / fine_sum - own_row
        fine_col = over(total * lane_col + right) / fine_sum - own_col
        coarse_row = over(c_rows) / coarse_sum + 0.5 - own_row
        coarse_col = over(c_total * lane_col) / coarse_sum + 0.5 - own_col
        fine_out = dot((acc_fine / fine_sum).astype(BF16), weight[:channels])
        coarse_out = dot((acc_coarse / coarse_sum).astype(BF16), weight[channels:])
        mixed[pl.ds(first, tile), 0:128] = fine_out + fine_row * ow[0:1] + fine_col * ow[1:2]
        mixed[pl.ds(first, tile), 128:256] = coarse_out + coarse_row * ow[2:3] + coarse_col * ow[3:4]
        mixed[pl.ds(first, tile), 256:384] = jnp.where(
            iota((tile, 128), 1) < 64,
            peak_fine + jnp.log(fine_sum),
            peak_coarse + jnp.log(coarse_sum),
        )
        return carry

    lax.fori_loop(0, pixels // tile, one_tile, 0)
    start = pl.multiple_of(half * columns, 128)
    other = pl.multiple_of((1 - half) * columns, 128)
    for r in range(rows_per):
        wide[r, HALO : HALO + width, :] = mixed[r * width : (r + 1) * width, :]
        keep_ref[r] = wide[r, pl.ds(start, half_wide), :]
        send_ref[r] = wide[r, pl.ds(other, half_wide), :]


def merge_kernel(own, keep_ref, got_ref, term_ref, hidden_ref, out_ref):
    dests = out_ref.shape[0]
    for r in range(keep_ref.shape[0]):
        keep, got = keep_ref[r], got_ref[r]
        gap = got[:, 256:384] - keep[:, 256:384]
        share = 1.0 / (1.0 + jnp.exp(gap))
        share_fine, share_coarse = share[:, 0:1], share[:, 64:65]
        base = (
            got[:, 0:128]
            + (keep[:, 0:128] - got[:, 0:128]) * share_fine
            + got[:, 128:256]
            + (keep[:, 128:256] - got[:, 128:256]) * share_coarse
            + term_ref[r]
        )
        hidden = hidden_ref[r].astype(F32)
        for j in range(dests):
            out_ref[j, r * WIN : (r + 1) * WIN, 0:128] = base[j * own : j * own + WIN].astype(BF16)
            out_ref[j, r * WIN : (r + 1) * WIN, 128:256] = hidden[j * own : j * own + WIN].astype(BF16)


def sigmoid(x):
    return 1.0 / (1.0 + jnp.exp(-x))


def update_kernel(
    own, width, got_ref, context_ref, ow_ref, gate_ref, state_ref, bias_ref, head_ref, delta_ref,
    out_ref, base, hidden, inputs, states, resets, updates, col_in, col_st, flow, flow_cols,
):
    me, half = lax.axis_index("rows"), lax.axis_index("loop")
    dests, per_dest, _ = got_ref.shape
    rows_per = per_dest // WIN
    count = dests * per_dest
    pad = 2 * WIN
    tiles = count // TILE
    first_col = (half * dests + me) * own - HALO
    column = first_col + iota((TILE, 128), 0) % WIN
    inside = (column >= 0) & (column < width)
    mask = jnp.where(inside, 1.0, 0.0)
    ow = ow_ref[...]
    add_row = OFFSET_SCALE * (ow[4:5] - ow[0:1] - ow[2:3])
    add_col = OFFSET_SCALE * (ow[5:6] - ow[1:2] - ow[3:4])
    bias = bias_ref[...]

    for ref in (inputs, states, resets):
        ref[0:pad, :] = jnp.zeros((pad, ref.shape[1]), BF16)
        ref[pad + count : pad + count + pad, :] = jnp.zeros((pad, ref.shape[1]), BF16)
    for j in range(dests):
        at = j * per_dest
        base[at : at + per_dest, :] = got_ref[j, :, 0:128]
        hidden[at : at + per_dest, :] = got_ref[j, :, 128:256].astype(F32)
        inputs[pad + at : pad + at + per_dest, 0:128] = context_ref[j]
    flow[...] = jnp.zeros_like(flow)
    flow_cols[...] = jnp.zeros_like(flow_cols)

    def each(body):
        def step(t, carry):
            body(pl.multiple_of(t * TILE, TILE))
            return carry

        lax.fori_loop(0, tiles, step, 0, unroll=tiles == 1)

    def shifted(value, tap):
        return value if tap == 2 else pltpu.roll(value, (2 - tap) % TILE, 0)

    def finish(at, update, candidate):
        old = hidden[pl.ds(at, TILE), :]
        hidden[pl.ds(at, TILE), :] = ((1.0 - update) * old + update * candidate) * mask

    for iteration in range(ITERS):

        def columns_pass(at):
            motion = base[pl.ds(at, TILE), :].astype(F32)
            if iteration > 0:
                moved = flow_cols[pl.ds(at, TILE), :]
                motion = (motion + moved[:, 0:1] * add_row + moved[:, 1:2] * add_col) * mask
            motion = jnp.maximum(motion, 0.0)
            inputs[pl.ds(pad + at, TILE), 128:256] = motion.astype(BF16)
            context = inputs[pl.ds(pad + at, TILE), 0:128].astype(F32)
            motion = motion.astype(BF16).astype(F32)
            state = hidden[pl.ds(at, TILE), :].astype(BF16).astype(F32)
            for tap in range(5):
                if iteration == 0:
                    col_in[pl.ds(at, TILE), tap * 256 : tap * 256 + 128] = shifted(context, tap).astype(BF16)
                col_in[pl.ds(at, TILE), tap * 256 + 128 : tap * 256 + 256] = shifted(motion, tap).astype(BF16)
                col_st[:, tap * 128 : (tap + 1) * 128] = shifted(state, tap).astype(BF16)
            gates = dot(col_st[...], gate_ref[0, :, 0:128, :].reshape(640, 256)) + dot(
                col_in[pl.ds(at, TILE), :], gate_ref[0, :, 128:384, :].reshape(1280, 256)
            )
            gates = sigmoid(gates + bias[0:1, 0:256])
            reset = (gates[:, 128:256] * state).astype(BF16).astype(F32)
            for tap in range(5):
                col_st[:, tap * 128 : (tap + 1) * 128] = shifted(reset, tap).astype(BF16)
            candidate = dot(col_st[...], state_ref[0, :, 0:128, :].reshape(640, 128)) + dot(
                col_in[pl.ds(at, TILE), :], state_ref[0, :, 128:384, :].reshape(1280, 128)
            )
            finish(at, gates[:, 0:128], jnp.tanh(candidate + bias[0:1, 256:384]))
            states[pl.ds(pad + at, TILE), :] = hidden[pl.ds(at, TILE), :].astype(BF16)

        def gate_rows(at):
            total = None
            for tap in range(5):
                part = dot(states[pl.ds(at + tap * WIN, TILE), :], gate_ref[1, tap, 0:128, :]) + dot(
                    inputs[pl.ds(at + tap * WIN, TILE), :], gate_ref[1, tap, 128:384, :]
                )
                total = part if total is None else total + part
            gates = sigmoid(total + bias[1:2, 0:256])
            updates[pl.ds(at, TILE), :] = gates[:, 0:128]
            resets[pl.ds(pad + at, TILE), :] = (
                gates[:, 128:256] * states[pl.ds(pad + at, TILE), :].astype(F32)
            ).astype(BF16)

        def state_rows(at):
            total = None
            for tap in range(5):
                part = dot(resets[pl.ds(at + tap * WIN, TILE), :], state_ref[1, tap, 0:128, :]) + dot(
                    inputs[pl.ds(at + tap * WIN, TILE), :], state_ref[1, tap, 128:384, :]
                )
                total = part if total is None else total + part
            finish(at, updates[pl.ds(at, TILE), :], jnp.tanh(total + bias[1:2, 256:384]))
            lifted = jnp.maximum(dot(hidden[pl.ds(at, TILE), :].astype(BF16), head_ref[...]), 0.0).astype(BF16)
            step = dot_nt(delta_ref[...], lifted)
            flow[:, pl.ds(at, TILE)] = flow[:, pl.ds(at, TILE)] + step
            flow_cols[pl.ds(at, TILE), :] = flow_cols[pl.ds(at, TILE), :] + step.T

        each(columns_pass)
        each(gate_rows)
        each(state_rows)

    for j in range(dests):
        for r in range(rows_per):
            at = j * per_dest + r * WIN + HALO
            out_ref[j, r * own : (r + 1) * own, :] = hidden[at : at + own, :]
        moved = flow[:, j * per_dest : (j + 1) * per_dest]
        out_ref[j, rows_per * own : rows_per * own + 8, :] = jnp.concatenate(
            [moved, jnp.zeros((8, 128 - per_dest), F32)], axis=1
        )


def local(
    frame_one,
    frame_two,
    context,
    carry_hidden,
    carry_flow,
    slot_target,
    slot_count,
    match_weight,
    offset_weight,
    gate_weight,
    state_weight,
    gru_bias,
    head_weight,
    delta_weight,
):
    dests = lax.axis_size("rows")
    halves = lax.axis_size("loop")
    rows_per, width, channels = frame_one.shape
    columns = frame_two.shape[1]
    pixels = rows_per * width
    slots, hidden_size = carry_hidden.shape
    cap = slots // dests
    own = columns // dests
    half_wide = round_up(columns - own + WIN, 8)
    padded = columns + half_wide
    room = 16 if dests <= 8 else 56

    shard = frame_two.reshape(1, rows_per, columns, channels)
    if dests == 8:

        def swap(value, flip):
            return lax.ppermute(value, "rows", [(i, i ^ flip) for i in range(dests)])

        beside, *others = (swap(shard, flip) for flip in (1, 2, 4, 6))
    else:
        beside, others = lax.all_gather(shard, "rows", axis=0, tiled=True), ()

    rows_hidden = round_up(cap, 16)
    rows_slot = rows_hidden + round_up(8 * (-(-cap // 128)), 16)
    slot_target, beside = lax.optimization_barrier((slot_target, beside))
    packed = call(
        functools.partial(pack_kernel, dests, cap, pixels, own, half_wide),
        jax.ShapeDtypeStruct((dests, rows_slot + rows_per * WIN, hidden_size), BF16),
        [smem_spec()] + vmem_specs(4),
        [pltpu.VMEM((rows_per, padded, 128), F32)],
        (2 * slots * slots * 128, 1 << 20, 0),
        room,
        slot_count,
        slot_target.reshape(slots // 128, 128),
        carry_flow.T,
        carry_hidden,
        context,
    )
    packed, others = lax.optimization_barrier((packed, others))
    early = lax.all_to_all(packed, "rows", 0, 0, tiled=True)
    if others:
        near, across, wrap = others
        keys = (shard, beside, near, swap(near, 1), across, swap(across, 1), wrap, swap(wrap, 1))
    else:
        keys = (beside,)
    ow = jnp.pad(offset_weight, ((0, 2), (0, 0)))
    hidden_wide, flow_first, term = call(
        functools.partial(place_kernel, cap, half_wide, rows_per),
        (
            jax.ShapeDtypeStruct((rows_per, half_wide, 128), BF16),
            jax.ShapeDtypeStruct((8, pixels), F32),
            jax.ShapeDtypeStruct((rows_per, half_wide, 128), F32),
        ),
        vmem_specs(2),
        [pltpu.VMEM((rows_per, padded, 128), F32)] * 2,
        (2 * slots * pixels * 128, 1 << 20, 0),
        room,
        early,
        ow,
    )
    queries = frame_one.reshape(pixels, channels)
    queries, hidden_wide, term = lax.optimization_barrier((queries, hidden_wide, term))
    chunks = dests // 2
    tile = 128
    keep, send = call(
        functools.partial(match_kernel, len(keys), len(keys) > 1, half_wide, rows_per),
        (jax.ShapeDtypeStruct((rows_per, half_wide, 384), F32),) * 2,
        vmem_specs(3 + len(keys)),
        [
            pltpu.VMEM((chunks, 4 * columns, channels), BF16),
            pltpu.VMEM((chunks, columns, channels), BF16),
            pltpu.VMEM((chunks, tile, 4 * columns), F32),
            pltpu.VMEM((pixels, 384), F32),
            pltpu.VMEM((rows_per, padded, 384), F32),
        ],
        (4 * pixels * chunks * 4 * columns * channels, 1 << 21, pixels * chunks * 5 * columns),
        room,
        queries,
        match_weight,
        ow,
        *keys,
    )
    other = lax.ppermute(send, "loop", [(i, (i + 1) % halves) for i in range(halves)])
    sending = call(
        functools.partial(merge_kernel, own),
        jax.ShapeDtypeStruct((dests, rows_per * WIN, 256), BF16),
        vmem_specs(4),
        [],
        (0, 1 << 20, 0),
        room,
        keep,
        other,
        term,
        hidden_wide,
    )
    arrived = lax.all_to_all(sending, "rows", 0, 0, tiled=True)
    count = dests * rows_per * WIN
    back_rows = rows_per * own + 8
    outgoing = call(
        functools.partial(update_kernel, own, width),
        jax.ShapeDtypeStruct((dests, back_rows, 128), F32),
        vmem_specs(8),
        [
            pltpu.VMEM((count, 128), BF16),
            pltpu.VMEM((count, 128), F32),
            pltpu.VMEM((count + 4 * WIN, 256), BF16),
            pltpu.VMEM((count + 4 * WIN, 128), BF16),
            pltpu.VMEM((count + 4 * WIN, 128), BF16),
            pltpu.VMEM((count, 128), F32),
            pltpu.VMEM((count, 1280), BF16),
            pltpu.VMEM((TILE, 640), BF16),
            pltpu.VMEM((8, count), F32),
            pltpu.VMEM((count, 8), F32),
        ],
        (16 * count * 5 * 384 * 256, 1 << 22, 8 * count * 384),
        room,
        arrived,
        early[:, rows_slot:, :],
        ow,
        gate_weight,
        state_weight,
        gru_bias,
        head_weight,
        jnp.pad(delta_weight, ((0, 6), (0, 0))),
    )
    back = lax.all_to_all(outgoing, "rows", 0, 0, tiled=True)
    both = lax.all_gather(back, "loop", axis=0)
    cells = both[:, :, : rows_per * own, :].reshape(halves, dests, rows_per, own, hidden_size)
    hidden_out = cells.transpose(2, 0, 1, 3, 4).reshape(rows_per, width, hidden_size)
    moved = both[:, :, rows_per * own : rows_per * own + 2, : rows_per * WIN]
    moved = moved.reshape(halves, dests, 2, rows_per, WIN)[..., HALO : HALO + own]
    moved = moved.transpose(2, 3, 0, 1, 4).reshape(2, rows_per, width)
    flow_out = flow_first[:2].reshape(2, rows_per, width) + moved
    return (hidden_out, flow_out)


def solution(mesh):
    return jax.shard_map(
        local,
        mesh=mesh,
        in_specs=(
            P(("groups", "rows"), None, None),
            P(("groups", "rows"), "loop", None),
            P(("groups", "rows"), None, None),
            P(("groups", "rows"), None),
            P(("groups", "rows"), None),
            P(("groups", "rows")),
            P(("groups", "rows")),
            P(),
            P(),
            P(),
            P(),
            P(),
            P(),
            P(),
        ),
        out_specs=(P(("groups", "rows"), None, None), P(None, ("groups", "rows"), None)),
        check_vma=False,
    )
```

```python
import functools
import math

import jax
import jax.numpy as jnp
from jax import lax
from jax.experimental import pallas as pl
from jax.experimental.pallas import tpu as pltpu
from jax.sharding import PartitionSpec as P

ITERS = 2
WIN = 32
HALO = 8
TILE = 512
OFFSET_SCALE = 0.03125
F32 = jnp.float32
BF16 = jnp.bfloat16
VMEM = pltpu.VMEM
NT = (((1,), (1,)), ((), ()))


def iota(shape, dim):
    return lax.broadcasted_iota(jnp.int32, shape, dim)


def round_up(value, step):
    return -(-value // step) * step


def dot(a, b):
    return jnp.dot(a, b, preferred_element_type=F32)


def dot_nt(a, b):
    return lax.dot_general(a, b, NT, preferred_element_type=F32)


def vmem_specs(count):
    return [pl.BlockSpec(memory_space=VMEM)] * count


def smem_spec():
    return pl.BlockSpec(memory_space=pltpu.SMEM)


def loop(count, body, carry):
    return lax.fori_loop(0, count, body, carry, unroll=count <= 4)


def call(kernel, out_shape, in_specs, scratch, cost, room, *args):
    single = not isinstance(out_shape, (tuple, list))
    return pl.pallas_call(
        kernel,
        out_shape=out_shape,
        in_specs=in_specs,
        out_specs=vmem_specs(1)[0] if single else vmem_specs(len(out_shape)),
        scratch_shapes=scratch,
        compiler_params=pltpu.CompilerParams(vmem_limit_bytes=room * 1024 * 1024),
        cost_estimate=pl.CostEstimate(flops=cost[0], bytes_accessed=cost[1], transcendentals=cost[2]),
    )(*args)


def pack_kernel(dests, cap, pixels, own, half_wide, count_ref, target_ref, flow_ref, hidden_ref, context_ref, shard_ref, out_ref, pass_ref, wide):
    pass_ref[...] = shard_ref[...]
    slots = hidden_ref.shape[0]
    target = jnp.concatenate([target_ref[k : k + 1, :] for k in range(slots // 128)], axis=1)
    counted = iota((1, slots), 1) < count_ref[0]
    owner = target // pixels
    within = target % pixels
    belongs = (iota((dests, slots), 0) == owner) & counted
    member = jnp.where(belongs, 1.0, 0.0)
    upper = jnp.where(iota((128, 128), 0) <= iota((128, 128), 1), 1.0, 0.0).astype(BF16)
    before = jnp.zeros((dests, 1), F32)
    ranks = []
    for start in range(0, slots, 128):
        running = dot(member[:, start : start + 128].astype(BF16), upper) + before
        before = running[:, 127:128]
        ranks.append(running)
    rank = jnp.concatenate(ranks, axis=1) - 1.0
    place_at = jnp.sum(
        jnp.where(belongs, rank + iota((dests, slots), 0).astype(F32) * cap, 0.0), axis=0, keepdims=True
    )
    landing = jnp.where(counted, place_at, -1.0).astype(jnp.int32)
    row = iota((8, slots), 0)
    flow = flow_ref[...].astype(F32)
    side = jnp.where(row == 0, flow[0:1], 0.0)
    side = jnp.where(row == 1, flow[1:2], side)
    side = jnp.where(row == 2, (within // 256).astype(F32), side)
    side = jnp.where(row == 3, (within % 256).astype(F32), side)
    side = jnp.where(row == 4, 1.0, side).astype(BF16)
    hidden = hidden_ref[...]
    rows_hidden = round_up(cap, 16)
    together = max(1, min(dests, 192 // cap))
    for first in range(0, dests, together):
        spots = together * cap
        chosen = jnp.where(iota((spots, slots), 0) + first * cap == landing, 1.0, 0.0).astype(BF16)
        moved = dot(chosen, hidden)
        moved_side = dot_nt(side, chosen)
        for k in range(together):
            out_ref[first + k, 0:cap, :] = moved[k * cap : (k + 1) * cap].astype(BF16)
            for t in range(-(-cap // 128)):
                width = min(128, cap - t * 128)
                piece = moved_side[:, k * cap + t * 128 : k * cap + t * 128 + width]
                if width < 128:
                    piece = jnp.concatenate([piece, jnp.zeros((8, 128 - width), F32)], axis=1)
                base = rows_hidden + 8 * t
                out_ref[first + k, base : base + 8, :] = piece.astype(BF16)
    rows_per, width, _ = context_ref.shape
    top = out_ref.shape[1] - rows_per * WIN
    start = pl.multiple_of(lax.axis_index("loop") * (width // 2), 128)
    wide[...] = jnp.zeros_like(wide)
    for r in range(rows_per):
        wide[r, HALO : HALO + width, :] = context_ref[r].astype(F32)
        part = wide[r, pl.ds(start, half_wide), :]
        for j in range(dests):
            out_ref[j, top + r * WIN : top + (r + 1) * WIN, :] = part[j * own : j * own + WIN].astype(BF16)


def place_kernel(cap, half_wide, rows_per, got_ref, ow_ref, hidden_ref, flow_ref, term_ref, wide_hidden, wide_term):
    half = lax.axis_index("loop")
    dests = got_ref.shape[0]
    pixels = flow_ref.shape[1]
    width = pixels // rows_per
    rows_hidden = round_up(cap, 16)
    hidden = jnp.zeros((pixels, 128), F32)
    flow = jnp.zeros((8, pixels), F32)
    for j in range(dests):
        pieces = []
        for t in range(-(-cap // 128)):
            base = rows_hidden + 8 * t
            pieces.append(got_ref[j, base : base + 8, 0 : min(128, cap - t * 128)].astype(F32))
        side = pieces[0] if len(pieces) == 1 else jnp.concatenate(pieces, axis=1)
        place = jnp.where(side[4:5] > 0.5, side[2:3] * 256.0 + side[3:4], -1.0).astype(jnp.int32)
        chosen = jnp.where(iota((pixels, cap), 0) == place, 1.0, 0.0).astype(BF16)
        hidden = hidden + dot(chosen, got_ref[j, 0:cap, :])
        flow = flow + dot_nt(side.astype(BF16), chosen)
    flow_ref[...] = flow
    columns = flow.T
    ow = ow_ref[...]
    term = columns[:, 0:1] * (OFFSET_SCALE * (ow[4:5] - ow[0:1] - ow[2:3])) + columns[:, 1:2] * (
        OFFSET_SCALE * (ow[5:6] - ow[1:2] - ow[3:4])
    )
    start = pl.multiple_of(half * (width // 2), 128)
    for wide, value, out in ((wide_hidden, hidden, hidden_ref), (wide_term, term, term_ref)):
        wide[...] = jnp.zeros_like(wide)
        for r in range(rows_per):
            wide[r, HALO : HALO + width, :] = value[r * width : (r + 1) * width]
            out[r] = wide[r, pl.ds(start, half_wide), :].astype(out.dtype)


def match_kernel(
    count, flip, half_wide, rows_per, queries_ref, weight_ref, ow_ref, *refs
):
    key_refs, (keep_ref, send_ref, fine, coarse, scores, mixed, wide) = refs[:count], refs[count:]
    me, half = lax.axis_index("rows"), lax.axis_index("loop")
    pixels, channels = queries_ref.shape
    width = pixels // rows_per
    columns = width // 2
    quarter = columns // 2
    chunks = fine.shape[0]
    shards = chunks * 2
    per_ref = shards // count
    spread = jnp.where(
        iota((columns, columns), 1)
        == jnp.where(iota((columns, columns), 0) < quarter, 2 * iota((columns, columns), 0), 2 * (iota((columns, columns), 0) - quarter) + 1),
        1.0,
        0.0,
    ).astype(BF16)

    def sort_shard(ref, m, shard, lane):
        even, odd = [], []
        for r in range(rows_per):
            parted = dot(spread, ref[m, r])
            even.append(parted[:quarter])
            odd.append(parted[quarter:])
            for p, part in ((0, even[-1]), (1, odd[-1])):
                g = 2 * r + p
                fine[shard, g * 2 * quarter + lane * quarter : g * 2 * quarter + (lane + 1) * quarter, :] = part.astype(BF16)
        pooled = (even[0] + odd[0] + even[1] + odd[1]) * 0.25
        coarse[shard, lane * quarter : (lane + 1) * quarter, :] = pooled.astype(BF16)

    if per_ref == 1:
        for m in range(shards):
            sort_shard(key_refs[m], 0, m // 2, m % 2)
    else:
        def sort_chunk(c, carry):
            for lane in range(2):
                sort_shard(key_refs[0], c * 2 + lane, c, lane)
            return carry

        lax.fori_loop(0, chunks, sort_chunk, 0)

    group = 2 * quarter
    tile = scores.shape[1]
    lane = iota((1, group), 1)
    lane_col = ((lane % quarter) * 2 + half * columns).astype(F32)
    ow = ow_ref[...] * OFFSET_SCALE
    weight = weight_ref[...]

    def lane_row(c):
        arrival = c * 2 + lane // quarter
        shard = lax.bitwise_xor(arrival, me) if flip else arrival
        return (shard * rows_per).astype(F32)

    wide[...] = jnp.zeros_like(wide)

    def one_tile(t, carry):
        first = pl.multiple_of(t * tile, tile)
        queries = queries_ref[pl.ds(first, tile), :] * jnp.asarray(1.0 / math.sqrt(channels), BF16)

        def score(c, peaks):
            values = dot_nt(queries, fine[c])
            scores[c] = values
            parts = [values[:, g * group : (g + 1) * group] for g in range(4)]
            blended = (parts[0] + parts[1] + parts[2] + parts[3]) * 0.25
            high = jnp.maximum(jnp.maximum(parts[0], parts[1]), jnp.maximum(parts[2], parts[3]))
            return jnp.maximum(peaks[0], high), jnp.maximum(peaks[1], blended)

        low = jnp.full((tile, group), -jnp.inf, F32)
        peaks = loop(chunks, score, (low, low))
        peak_fine = jnp.max(peaks[0], axis=1, keepdims=True)
        peak_coarse = jnp.max(peaks[1], axis=1, keepdims=True)

        def absorb(c, so_far):
            total, below, right, rows, c_total, c_rows, acc_fine, acc_coarse = so_far
            parts = [scores[c, :, g * group : (g + 1) * group] for g in range(4)]
            blended = (parts[0] + parts[1] + parts[2] + parts[3]) * 0.25
            expo = [jnp.exp(part - peak_fine) for part in parts]
            c_expo = jnp.exp(blended - peak_coarse)
            lower = expo[2] + expo[3]
            everything = expo[0] + expo[1] + lower
            at = lane_row(c)
            weights = jnp.concatenate([e.astype(BF16) for e in expo], axis=1)
            return (
                total + everything,
                below + lower,
                right + (expo[1] + expo[3]),
                rows + everything * at,
                c_total + c_expo,
                c_rows + c_expo * at,
                acc_fine + dot(weights, fine[c]),
                acc_coarse + dot(c_expo.astype(BF16), coarse[c]),
            )

        zero = jnp.zeros((tile, group), F32)
        blank = jnp.zeros((tile, channels), F32)
        total, below, right, rows, c_total, c_rows, acc_fine, acc_coarse = loop(
            chunks, absorb, (zero, zero, zero, zero, zero, zero, blank, blank)
        )

        def over(value):
            return jnp.sum(value, axis=1, keepdims=True)

        pixel = first + iota((tile, 1), 0)
        own_row = (me * rows_per + pixel // width).astype(F32)
        own_col = (pixel % width).astype(F32)
        fine_sum, coarse_sum = over(total), over(c_total)
        fine_row = over(rows + below) / fine_sum - own_row
        fine_col = over(total * lane_col + right) / fine_sum - own_col
        coarse_row = over(c_rows) / coarse_sum + 0.5 - own_row
        coarse_col = over(c_total * lane_col) / coarse_sum + 0.5 - own_col
        fine_out = dot((acc_fine / fine_sum).astype(BF16), weight[:channels])
        coarse_out = dot((acc_coarse / coarse_sum).astype(BF16), weight[channels:])
        mixed[pl.ds(first, tile), 0:128] = fine_out + fine_row * ow[0:1] + fine_col * ow[1:2]
        mixed[pl.ds(first, tile), 128:256] = coarse_out + coarse_row * ow[2:3] + coarse_col * ow[3:4]
        mixed[pl.ds(first, tile), 256:384] = jnp.where(
            iota((tile, 128), 1) < 64,
            peak_fine + jnp.log(fine_sum),
            peak_coarse + jnp.log(coarse_sum),
        )
        return carry

    lax.fori_loop(0, pixels // tile, one_tile, 0)
    start = pl.multiple_of(half * columns, 128)
    other = pl.multiple_of((1 - half) * columns, 128)
    for r in range(rows_per):
        wide[r, HALO : HALO + width, :] = mixed[r * width : (r + 1) * width, :]
        keep_ref[r] = wide[r, pl.ds(start, half_wide), :]
        send_ref[r] = wide[r, pl.ds(other, half_wide), :]


def merge_kernel(own, keep_ref, got_ref, term_ref, hidden_ref, out_ref):
    dests = out_ref.shape[0]
    for r in range(keep_ref.shape[0]):
        keep, got = keep_ref[r], got_ref[r]
        gap = got[:, 256:384] - keep[:, 256:384]
        share = 1.0 / (1.0 + jnp.exp(gap))
        share_fine, share_coarse = share[:, 0:1], share[:, 64:65]
        base = (
            got[:, 0:128]
            + (keep[:, 0:128] - got[:, 0:128]) * share_fine
            + got[:, 128:256]
            + (keep[:, 128:256] - got[:, 128:256]) * share_coarse
            + term_ref[r]
        )
        hidden = hidden_ref[r].astype(F32)
        for j in range(dests):
            out_ref[j, r * WIN : (r + 1) * WIN, 0:128] = base[j * own : j * own + WIN].astype(BF16)
            out_ref[j, r * WIN : (r + 1) * WIN, 128:256] = hidden[j * own : j * own + WIN].astype(BF16)


def sigmoid(x):
    return 0.5 * jnp.tanh(0.5 * x) + 0.5


def shifted(value, tap):
    return value if tap == 2 else pltpu.roll(value, (2 - tap) % TILE, 0)


def each_tile(count, body):
    def step(t, carry):
        body(pl.multiple_of(t * TILE, TILE))
        return carry

    lax.fori_loop(0, count // TILE, step, 0, unroll=count == TILE)


def fetch(copies, sems, first=0):
    handles = []
    for k, (source, target) in enumerate(copies):
        handles.append(pltpu.make_async_copy(source, target, sems.at[first + k]))
        handles[-1].start()
    return handles


def context_kernel(early_ref, gate_hbm, state_hbm, bias_ref, fixed_ref, gate_ref, state_ref, padded, taps, sems):
    handles = fetch(
        [
            (gate_hbm.at[:, :, pl.ds(128, 128), :], gate_ref),
            (state_hbm.at[:, :, pl.ds(128, 128), :], state_ref),
        ],
        sems,
    )
    dests = early_ref.shape[0]
    count = fixed_ref.shape[1]
    per_dest = count // dests
    first = early_ref.shape[1] - per_dest
    pad = 2 * WIN
    padded[0:pad, :] = jnp.zeros((pad, 128), BF16)
    padded[pad + count : pad + count + pad, :] = jnp.zeros((pad, 128), BF16)
    for j in range(dests):
        padded[pad + j * per_dest : pad + (j + 1) * per_dest, :] = early_ref[j, first : first + per_dest, :]
    for handle in handles:
        handle.wait()
    for p in range(2):

        def one(at):
            for tap in range(5):
                if p == 0:
                    value = shifted(padded[pl.ds(pad + at, TILE), :].astype(F32), tap).astype(BF16)
                else:
                    value = padded[pl.ds(at + tap * WIN, TILE), :]
                taps[:, tap * 128 : (tap + 1) * 128] = value
            gate = gate_ref[p].reshape(640, 256)
            state = state_ref[p].reshape(640, 128)
            fixed_ref[p, pl.ds(at, TILE), 0:256] = dot(taps[...], gate) + bias_ref[p : p + 1, 0:256]
            fixed_ref[p, pl.ds(at, TILE), 256:384] = dot(taps[...], state) + bias_ref[p : p + 1, 256:384]

        each_tile(count, one)


def update_kernel(
    own, width, got_ref, fixed_ref, ow_ref, gate_hbm, state_hbm, head_ref, delta_ref,
    out_ref, base, hidden, motions, states, resets, updates, taps, flow, flow_cols, gate_ref, state_ref, sems,
):
    handles = []
    for p in range(2):
        for source, target in ((gate_hbm, gate_ref), (state_hbm, state_ref)):
            parts = [
                (source.at[p, :, pl.ds(256 * k, 128), :], target.at[p, :, pl.ds(128 * k, 128), :]) for k in range(2)
            ]
            handles.append(fetch(parts, sems, 2 * len(handles)))

    def ready(k):
        for handle in handles[k]:
            handle.wait()

    me, half = lax.axis_index("rows"), lax.axis_index("loop")
    dests, per_dest, _ = got_ref.shape
    rows_per = per_dest // WIN
    count = dests * per_dest
    pad = 2 * WIN
    first_col = (half * dests + me) * own - HALO
    column = first_col + iota((TILE, 128), 0) % WIN
    inside = (column >= 0) & (column < width)
    mask = jnp.where(inside, 1.0, 0.0)
    ow = ow_ref[...]
    add_row = OFFSET_SCALE * (ow[4:5] - ow[0:1] - ow[2:3])
    add_col = OFFSET_SCALE * (ow[5:6] - ow[1:2] - ow[3:4])

    for ref in (motions, states, resets):
        ref[0:pad, :] = jnp.zeros((pad, 128), BF16)
        ref[pad + count : pad + count + pad, :] = jnp.zeros((pad, 128), BF16)
    for j in range(dests):
        at = j * per_dest
        base[at : at + per_dest, :] = got_ref[j, :, 0:128]
        hidden[at : at + per_dest, :] = got_ref[j, :, 128:256].astype(F32)

    def finish(at, update, candidate):
        old = hidden[pl.ds(at, TILE), :]
        new = (old + update * (candidate - old)) * mask
        hidden[pl.ds(at, TILE), :] = new
        return new

    for iteration in range(ITERS):

        def columns_pass(at):
            motion = base[pl.ds(at, TILE), :].astype(F32)
            if iteration > 0:
                moved = flow_cols[pl.ds(at, TILE), :]
                motion = (motion + moved[:, 0:1] * add_row + moved[:, 1:2] * add_col) * mask
            motion = jnp.maximum(motion, 0.0)
            rounded = motion.astype(BF16)
            motions[pl.ds(pad + at, TILE), :] = rounded
            motion = rounded.astype(F32)
            state = hidden[pl.ds(at, TILE), :].astype(BF16).astype(F32)
            for tap in range(5):
                taps[:, tap * 256 : tap * 256 + 128] = shifted(state, tap).astype(BF16)
                taps[:, tap * 256 + 128 : tap * 256 + 256] = shifted(motion, tap).astype(BF16)
            if iteration == 0 and count == TILE:
                ready(0)
            gates = sigmoid(dot(taps[...], gate_ref[0].reshape(1280, 256)) + fixed_ref[0, pl.ds(at, TILE), 0:256])
            reset = (gates[:, 128:256] * state).astype(BF16).astype(F32)
            for tap in range(5):
                taps[:, tap * 256 : tap * 256 + 128] = shifted(reset, tap).astype(BF16)
            if iteration == 0 and count == TILE:
                ready(1)
            candidate = jnp.tanh(dot(taps[...], state_ref[0].reshape(1280, 128)) + fixed_ref[0, pl.ds(at, TILE), 256:384])
            states[pl.ds(pad + at, TILE), :] = finish(at, gates[:, 0:128], candidate).astype(BF16)

        def fill(first, at):
            for tap in range(5):
                taps[:, tap * 256 : tap * 256 + 128] = first[pl.ds(at + tap * WIN, TILE), :]
                taps[:, tap * 256 + 128 : tap * 256 + 256] = motions[pl.ds(at + tap * WIN, TILE), :]

        def gate_rows(at):
            fill(states, at)
            gates = sigmoid(dot(taps[...], gate_ref[1].reshape(1280, 256)) + fixed_ref[1, pl.ds(at, TILE), 0:256])
            updates[pl.ds(at, TILE), :] = gates[:, 0:128]
            resets[pl.ds(pad + at, TILE), :] = (
                gates[:, 128:256] * states[pl.ds(pad + at, TILE), :].astype(F32)
            ).astype(BF16)

        def state_rows(at):
            fill(resets, at)
            candidate = jnp.tanh(dot(taps[...], state_ref[1].reshape(1280, 128)) + fixed_ref[1, pl.ds(at, TILE), 256:384])
            new = finish(at, updates[pl.ds(at, TILE), :], candidate)
            lifted = jnp.maximum(dot(new.astype(BF16), head_ref[...]), 0.0).astype(BF16)
            step = dot_nt(delta_ref[...], lifted)
            if iteration == 0:
                flow[:, pl.ds(at, TILE)] = step
                flow_cols[pl.ds(at, TILE), :] = step.T
            else:
                flow[:, pl.ds(at, TILE)] = flow[:, pl.ds(at, TILE)] + step

        if iteration == 0 and count != TILE:
            ready(0)
            ready(1)
        each_tile(count, columns_pass)
        if iteration == 0:
            ready(2)
            ready(3)
        each_tile(count, gate_rows)
        each_tile(count, state_rows)

    for j in range(dests):
        for r in range(rows_per):
            at = j * per_dest + r * WIN + HALO
            out_ref[j, r * own : (r + 1) * own, :] = hidden[at : at + own, :]
        moved = flow[:, j * per_dest : (j + 1) * per_dest]
        out_ref[j, rows_per * own : rows_per * own + 8, :] = jnp.concatenate(
            [moved, jnp.zeros((8, 128 - per_dest), F32)], axis=1
        )


def local(
    frame_one,
    frame_two,
    context,
    carry_hidden,
    carry_flow,
    slot_target,
    slot_count,
    match_weight,
    offset_weight,
    gate_weight,
    state_weight,
    gru_bias,
    head_weight,
    delta_weight,
):
    dests = lax.axis_size("rows")
    halves = lax.axis_size("loop")
    rows_per, width, channels = frame_one.shape
    columns = frame_two.shape[1]
    pixels = rows_per * width
    slots, hidden_size = carry_hidden.shape
    cap = slots // dests
    own = columns // dests
    half_wide = round_up(columns - own + WIN, 8)
    padded = columns + half_wide
    room = 16 if dests <= 8 else 56

    rows_hidden = round_up(cap, 16)
    rows_slot = rows_hidden + round_up(8 * (-(-cap // 128)), 16)
    packed, shard = call(
        functools.partial(pack_kernel, dests, cap, pixels, own, half_wide),
        (
            jax.ShapeDtypeStruct((dests, rows_slot + rows_per * WIN, hidden_size), BF16),
            jax.ShapeDtypeStruct((1, rows_per, columns, channels), BF16),
        ),
        [smem_spec()] + vmem_specs(5),
        [pltpu.VMEM((rows_per, padded, 128), F32)],
        (2 * slots * slots * 128, 1 << 20, 0),
        60,
        slot_count,
        slot_target.reshape(slots // 128, 128),
        carry_flow.T,
        carry_hidden,
        context,
        frame_two.reshape(1, rows_per, columns, channels),
    )
    if dests == 8:

        def swap(value, flip):
            return lax.ppermute(value, "rows", [(i, i ^ flip) for i in range(dests)])

        beside, *others = (swap(shard, flip) for flip in (1, 2, 4, 6))
    else:
        beside, others = lax.all_gather(shard, "rows", axis=0, tiled=True), ()

    early = lax.all_to_all(packed, "rows", 0, 0, tiled=True)
    if others:
        near, across, wrap = others
        keys = (frame_two[None], beside, near, swap(beside, 2), across, swap(across, 1), wrap, swap(beside, 6))
    else:
        keys = (beside,)
    ow = jnp.pad(offset_weight, ((0, 2), (0, 0)))
    hidden_wide, flow_first, term = call(
        functools.partial(place_kernel, cap, half_wide, rows_per),
        (
            jax.ShapeDtypeStruct((rows_per, half_wide, 128), BF16),
            jax.ShapeDtypeStruct((8, pixels), F32),
            jax.ShapeDtypeStruct((rows_per, half_wide, 128), F32),
        ),
        vmem_specs(2),
        [pltpu.VMEM((rows_per, padded, 128), F32)] * 2,
        (2 * slots * pixels * 128, 1 << 20, 0),
        room,
        early,
        ow,
    )
    queries = frame_one.reshape(pixels, channels)
    chunks = dests // 2
    tile = 128
    keep, send = call(
        functools.partial(match_kernel, len(keys), len(keys) > 1, half_wide, rows_per),
        (jax.ShapeDtypeStruct((rows_per, half_wide, 384), F32),) * 2,
        vmem_specs(3 + len(keys)),
        [
            pltpu.VMEM((chunks, 4 * columns, channels), BF16),
            pltpu.VMEM((chunks, columns, channels), BF16),
            pltpu.VMEM((chunks, tile, 4 * columns), F32),
            pltpu.VMEM((pixels, 384), F32),
            pltpu.VMEM((rows_per, padded, 384), F32),
        ],
        (4 * pixels * chunks * 4 * columns * channels, 1 << 21, pixels * chunks * 5 * columns),
        room,
        queries,
        match_weight,
        ow,
        *keys,
    )
    other = lax.ppermute(send, "loop", [(i, (i + 1) % halves) for i in range(halves)])
    sending = call(
        functools.partial(merge_kernel, own),
        jax.ShapeDtypeStruct((dests, rows_per * WIN, 256), BF16),
        vmem_specs(4),
        [],
        (0, 1 << 20, 0),
        room,
        keep,
        other,
        term,
        hidden_wide,
    )
    arrived = lax.all_to_all(sending, "rows", 0, 0, tiled=True)
    count = dests * rows_per * WIN
    back_rows = rows_per * own + 8
    hbm = pl.BlockSpec(memory_space=pltpu.HBM)
    gate_weight = pltpu.with_memory_space_constraint(gate_weight, pltpu.HBM)
    state_weight = pltpu.with_memory_space_constraint(state_weight, pltpu.HBM)
    fixed = call(
        context_kernel,
        jax.ShapeDtypeStruct((2, count, 384), F32),
        [vmem_specs(1)[0], hbm, hbm, vmem_specs(1)[0]],
        [
            pltpu.VMEM((2, 5, 128, 256), BF16),
            pltpu.VMEM((2, 5, 128, 128), BF16),
            pltpu.VMEM((count + 4 * WIN, 128), BF16),
            pltpu.VMEM((TILE, 640), BF16),
            pltpu.SemaphoreType.DMA((2,)),
        ],
        (4 * count * 5 * 128 * 384, 1 << 22, 0),
        room,
        early,
        gate_weight,
        state_weight,
        gru_bias,
    )
    outgoing = call(
        functools.partial(update_kernel, own, width),
        jax.ShapeDtypeStruct((dests, back_rows, 128), F32),
        vmem_specs(3) + [hbm, hbm] + vmem_specs(2),
        [
            pltpu.VMEM((count, 128), BF16),
            pltpu.VMEM((count, 128), F32),
            pltpu.VMEM((count + 4 * WIN, 128), BF16),
            pltpu.VMEM((count + 4 * WIN, 128), BF16),
            pltpu.VMEM((count + 4 * WIN, 128), BF16),
            pltpu.VMEM((count, 128), F32),
            pltpu.VMEM((TILE, 1280), BF16),
            pltpu.VMEM((8, count), F32),
            pltpu.VMEM((count, 8), F32),
            pltpu.VMEM((2, 5, 256, 256), BF16),
            pltpu.VMEM((2, 5, 256, 128), BF16),
            pltpu.SemaphoreType.DMA((8,)),
        ],
        (8 * count * 5 * 256 * 384, 1 << 22, 8 * count * 384),
        room,
        arrived,
        fixed,
        ow,
        gate_weight,
        state_weight,
        head_weight,
        jnp.pad(delta_weight, ((0, 6), (0, 0))),
    )
    back = lax.all_to_all(outgoing, "rows", 0, 0, tiled=True)
    both = lax.all_gather(back, "loop", axis=0)
    cells = both[:, :, : rows_per * own, :].reshape(halves, dests, rows_per, own, hidden_size)
    hidden_out = cells.transpose(2, 0, 1, 3, 4).reshape(rows_per, width, hidden_size)
    moved = both[:, :, rows_per * own : rows_per * own + 2, : rows_per * WIN]
    moved = moved.reshape(halves, dests, 2, rows_per, WIN)[..., HALO : HALO + own]
    moved = moved.transpose(2, 3, 0, 1, 4).reshape(2, rows_per, width)
    flow_out = flow_first[:2].reshape(2, rows_per, width) + moved
    return (hidden_out, flow_out)


def solution(mesh):
    return jax.shard_map(
        local,
        mesh=mesh,
        in_specs=(
            P(("groups", "rows"), None, None),
            P(("groups", "rows"), "loop", None),
            P(("groups", "rows"), None, None),
            P(("groups", "rows"), None),
            P(("groups", "rows"), None),
            P(("groups", "rows")),
            P(("groups", "rows")),
            P(),
            P(),
            P(),
            P(),
            P(),
            P(),
            P(),
        ),
        out_specs=(P(("groups", "rows"), None, None), P(None, ("groups", "rows"), None)),
        check_vma=False,
    )
```

```python
import functools
import math

import jax
import jax.numpy as jnp
from jax import lax
from jax.experimental import pallas as pl
from jax.experimental.pallas import tpu as pltpu
from jax.sharding import PartitionSpec as P

ITERS = 2
WIN = 32
HALO = 8
TILE = 512
OFFSET_SCALE = 0.03125
F32 = jnp.float32
BF16 = jnp.bfloat16
VMEM = pltpu.VMEM
NT = (((1,), (1,)), ((), ()))


def iota(shape, dim):
    return lax.broadcasted_iota(jnp.int32, shape, dim)


def round_up(value, step):
    return -(-value // step) * step


def dot(a, b):
    return jnp.dot(a, b, preferred_element_type=F32)


def dot_nt(a, b):
    return lax.dot_general(a, b, NT, preferred_element_type=F32)


def vmem_specs(count):
    return [pl.BlockSpec(memory_space=VMEM)] * count


def smem_spec():
    return pl.BlockSpec(memory_space=pltpu.SMEM)


def loop(count, body, carry):
    return lax.fori_loop(0, count, body, carry, unroll=count <= 4)


def call(kernel, out_shape, in_specs, scratch, cost, room, *args):
    single = not isinstance(out_shape, (tuple, list))
    return pl.pallas_call(
        kernel,
        out_shape=out_shape,
        in_specs=in_specs,
        out_specs=vmem_specs(1)[0] if single else vmem_specs(len(out_shape)),
        scratch_shapes=scratch,
        compiler_params=pltpu.CompilerParams(vmem_limit_bytes=room * 1024 * 1024),
        cost_estimate=pl.CostEstimate(flops=cost[0], bytes_accessed=cost[1], transcendentals=cost[2]),
    )(*args)


def pack_kernel(dests, cap, pixels, own, half_wide, count_ref, target_ref, flow_ref, hidden_ref, context_ref, out_ref, wide):
    slots = hidden_ref.shape[0]
    target = jnp.concatenate([target_ref[k : k + 1, :] for k in range(slots // 128)], axis=1)
    counted = iota((1, slots), 1) < count_ref[0]
    owner = target // pixels
    within = target % pixels
    belongs = (iota((dests, slots), 0) == owner) & counted
    member = jnp.where(belongs, 1.0, 0.0)
    upper = jnp.where(iota((128, 128), 0) <= iota((128, 128), 1), 1.0, 0.0).astype(BF16)
    before = jnp.zeros((dests, 1), F32)
    ranks = []
    for start in range(0, slots, 128):
        running = dot(member[:, start : start + 128].astype(BF16), upper) + before
        before = running[:, 127:128]
        ranks.append(running)
    rank = jnp.concatenate(ranks, axis=1) - 1.0
    place_at = jnp.sum(
        jnp.where(belongs, rank + iota((dests, slots), 0).astype(F32) * cap, 0.0), axis=0, keepdims=True
    )
    landing = jnp.where(counted, place_at, -1.0).astype(jnp.int32)
    row = iota((8, slots), 0)
    flow = flow_ref[...].astype(F32)
    side = jnp.where(row == 0, flow[0:1], 0.0)
    side = jnp.where(row == 1, flow[1:2], side)
    side = jnp.where(row == 2, (within // 256).astype(F32), side)
    side = jnp.where(row == 3, (within % 256).astype(F32), side)
    side = jnp.where(row == 4, 1.0, side).astype(BF16)
    hidden = hidden_ref[...]
    rows_hidden = round_up(cap, 16)
    together = max(1, min(dests, 192 // cap))
    for first in range(0, dests, together):
        spots = together * cap
        chosen = jnp.where(iota((spots, slots), 0) + first * cap == landing, 1.0, 0.0).astype(BF16)
        moved = dot(chosen, hidden)
        moved_side = dot_nt(side, chosen)
        for k in range(together):
            out_ref[first + k, 0:cap, :] = moved[k * cap : (k + 1) * cap].astype(BF16)
            for t in range(-(-cap // 128)):
                width = min(128, cap - t * 128)
                piece = moved_side[:, k * cap + t * 128 : k * cap + t * 128 + width]
                if width < 128:
                    piece = jnp.concatenate([piece, jnp.zeros((8, 128 - width), F32)], axis=1)
                base = rows_hidden + 8 * t
                out_ref[first + k, base : base + 8, :] = piece.astype(BF16)
    rows_per, width, _ = context_ref.shape
    top = out_ref.shape[1] - rows_per * WIN
    start = pl.multiple_of(lax.axis_index("loop") * (width // 2), 128)
    wide[...] = jnp.zeros_like(wide)
    for r in range(rows_per):
        wide[r, HALO : HALO + width, :] = context_ref[r].astype(F32)
        part = wide[r, pl.ds(start, half_wide), :]
        for j in range(dests):
            out_ref[j, top + r * WIN : top + (r + 1) * WIN, :] = part[j * own : j * own + WIN].astype(BF16)


def place_kernel(cap, half_wide, rows_per, got_ref, ow_ref, hidden_ref, flow_ref, term_ref, wide_hidden, wide_term):
    half = lax.axis_index("loop")
    dests = got_ref.shape[0]
    pixels = flow_ref.shape[1]
    width = pixels // rows_per
    rows_hidden = round_up(cap, 16)
    hidden = jnp.zeros((pixels, 128), F32)
    flow = jnp.zeros((8, pixels), F32)
    for j in range(dests):
        pieces = []
        for t in range(-(-cap // 128)):
            base = rows_hidden + 8 * t
            pieces.append(got_ref[j, base : base + 8, 0 : min(128, cap - t * 128)].astype(F32))
        side = pieces[0] if len(pieces) == 1 else jnp.concatenate(pieces, axis=1)
        place = jnp.where(side[4:5] > 0.5, side[2:3] * 256.0 + side[3:4], -1.0).astype(jnp.int32)
        chosen = jnp.where(iota((pixels, cap), 0) == place, 1.0, 0.0).astype(BF16)
        hidden = hidden + dot(chosen, got_ref[j, 0:cap, :])
        flow = flow + dot_nt(side.astype(BF16), chosen)
    flow_ref[...] = flow
    columns = flow.T
    ow = ow_ref[...]
    term = columns[:, 0:1] * (OFFSET_SCALE * (ow[4:5] - ow[0:1] - ow[2:3])) + columns[:, 1:2] * (
        OFFSET_SCALE * (ow[5:6] - ow[1:2] - ow[3:4])
    )
    start = pl.multiple_of(half * (width // 2), 128)
    for wide, value, out in ((wide_hidden, hidden, hidden_ref), (wide_term, term, term_ref)):
        wide[...] = jnp.zeros_like(wide)
        for r in range(rows_per):
            wide[r, HALO : HALO + width, :] = value[r * width : (r + 1) * width]
            out[r] = wide[r, pl.ds(start, half_wide), :].astype(out.dtype)


def match_kernel(
    count, flip, half_wide, rows_per, queries_ref, weight_ref, ow_ref, *refs
):
    key_refs, (keep_ref, send_ref, fine, coarse, scores, mixed, wide) = refs[:count], refs[count:]
    me, half = lax.axis_index("rows"), lax.axis_index("loop")
    pixels, channels = queries_ref.shape
    width = pixels // rows_per
    columns = width // 2
    quarter = columns // 2
    chunks = fine.shape[0]
    shards = chunks * 2
    per_ref = shards // count
    spread = jnp.where(
        iota((columns, columns), 1)
        == jnp.where(iota((columns, columns), 0) < quarter, 2 * iota((columns, columns), 0), 2 * (iota((columns, columns), 0) - quarter) + 1),
        1.0,
        0.0,
    ).astype(BF16)

    def sort_shard(ref, m, shard, lane):
        even, odd = [], []
        for r in range(rows_per):
            parted = dot(spread, ref[m, r])
            even.append(parted[:quarter])
            odd.append(parted[quarter:])
            for p, part in ((0, even[-1]), (1, odd[-1])):
                g = 2 * r + p
                fine[shard, g * 2 * quarter + lane * quarter : g * 2 * quarter + (lane + 1) * quarter, :] = part.astype(BF16)
        pooled = (even[0] + odd[0] + even[1] + odd[1]) * 0.25
        coarse[shard, lane * quarter : (lane + 1) * quarter, :] = pooled.astype(BF16)

    if per_ref == 1:
        for m in range(shards):
            sort_shard(key_refs[m], 0, m // 2, m % 2)
    else:
        def sort_chunk(c, carry):
            for lane in range(2):
                sort_shard(key_refs[0], c * 2 + lane, c, lane)
            return carry

        lax.fori_loop(0, chunks, sort_chunk, 0)

    group = 2 * quarter
    tile = scores.shape[1]
    lane = iota((1, group), 1)
    lane_col = ((lane % quarter) * 2 + half * columns).astype(F32)
    ow = ow_ref[...] * OFFSET_SCALE
    weight = weight_ref[...]

    def lane_row(c):
        arrival = c * 2 + lane // quarter
        shard = lax.bitwise_xor(arrival, me) if flip else arrival
        return (shard * rows_per).astype(F32)

    wide[...] = jnp.zeros_like(wide)

    def one_tile(t, carry):
        first = pl.multiple_of(t * tile, tile)
        queries = queries_ref[pl.ds(first, tile), :] * jnp.asarray(1.0 / math.sqrt(channels), BF16)

        def score(c, peaks):
            values = dot_nt(queries, fine[c])
            scores[c] = values
            parts = [values[:, g * group : (g + 1) * group] for g in range(4)]
            blended = (parts[0] + parts[1] + parts[2] + parts[3]) * 0.25
            high = jnp.maximum(jnp.maximum(parts[0], parts[1]), jnp.maximum(parts[2], parts[3]))
            return jnp.maximum(peaks[0], high), jnp.maximum(peaks[1], blended)

        low = jnp.full((tile, group), -jnp.inf, F32)
        peaks = loop(chunks, score, (low, low))
        peak_fine = jnp.max(peaks[0], axis=1, keepdims=True)
        peak_coarse = jnp.max(peaks[1], axis=1, keepdims=True)

        def absorb(c, so_far):
            total, below, right, rows, c_total, c_rows, acc_fine, acc_coarse = so_far
            parts = [scores[c, :, g * group : (g + 1) * group] for g in range(4)]
            blended = (parts[0] + parts[1] + parts[2] + parts[3]) * 0.25
            expo = [jnp.exp(part - peak_fine) for part in parts]
            c_expo = jnp.exp(blended - peak_coarse)
            lower = expo[2] + expo[3]
            everything = expo[0] + expo[1] + lower
            at = lane_row(c)
            weights = jnp.concatenate([e.astype(BF16) for e in expo], axis=1)
            return (
                total + everything,
                below + lower,
                right + (expo[1] + expo[3]),
                rows + everything * at,
                c_total + c_expo,
                c_rows + c_expo * at,
                acc_fine + dot(weights, fine[c]),
                acc_coarse + dot(c_expo.astype(BF16), coarse[c]),
            )

        zero = jnp.zeros((tile, group), F32)
        blank = jnp.zeros((tile, channels), F32)
        total, below, right, rows, c_total, c_rows, acc_fine, acc_coarse = loop(
            chunks, absorb, (zero, zero, zero, zero, zero, zero, blank, blank)
        )

        def over(value):
            return jnp.sum(value, axis=1, keepdims=True)

        pixel = first + iota((tile, 1), 0)
        own_row = (me * rows_per + pixel // width).astype(F32)
        own_col = (pixel % width).astype(F32)
        fine_sum, coarse_sum = over(total), over(c_total)
        fine_row = over(rows + below) / fine_sum - own_row
        fine_col = over(total * lane_col + right) / fine_sum - own_col
        coarse_row = over(c_rows) / coarse_sum + 0.5 - own_row
        coarse_col = over(c_total * lane_col) / coarse_sum + 0.5 - own_col
        fine_out = dot((acc_fine / fine_sum).astype(BF16), weight[:channels])
        coarse_out = dot((acc_coarse / coarse_sum).astype(BF16), weight[channels:])
        mixed[pl.ds(first, tile), 0:128] = fine_out + fine_row * ow[0:1] + fine_col * ow[1:2]
        mixed[pl.ds(first, tile), 128:256] = coarse_out + coarse_row * ow[2:3] + coarse_col * ow[3:4]
        mixed[pl.ds(first, tile), 256:384] = jnp.where(
            iota((tile, 128), 1) < 64,
            peak_fine + jnp.log(fine_sum),
            peak_coarse + jnp.log(coarse_sum),
        )
        return carry

    lax.fori_loop(0, pixels // tile, one_tile, 0)
    start = pl.multiple_of(half * columns, 128)
    other = pl.multiple_of((1 - half) * columns, 128)
    for r in range(rows_per):
        wide[r, HALO : HALO + width, :] = mixed[r * width : (r + 1) * width, :]
        keep_ref[r] = wide[r, pl.ds(start, half_wide), :]
        send_ref[r] = wide[r, pl.ds(other, half_wide), :]


def merge_kernel(own, keep_ref, got_ref, term_ref, hidden_ref, out_ref):
    dests = out_ref.shape[0]
    for r in range(keep_ref.shape[0]):
        keep, got = keep_ref[r], got_ref[r]
        gap = got[:, 256:384] - keep[:, 256:384]
        share = 1.0 / (1.0 + jnp.exp(gap))
        share_fine, share_coarse = share[:, 0:1], share[:, 64:65]
        base = (
            got[:, 0:128]
            + (keep[:, 0:128] - got[:, 0:128]) * share_fine
            + got[:, 128:256]
            + (keep[:, 128:256] - got[:, 128:256]) * share_coarse
            + term_ref[r]
        )
        hidden = hidden_ref[r].astype(F32)
        for j in range(dests):
            out_ref[j, r * WIN : (r + 1) * WIN, 0:128] = base[j * own : j * own + WIN].astype(BF16)
            out_ref[j, r * WIN : (r + 1) * WIN, 128:256] = hidden[j * own : j * own + WIN].astype(BF16)


def sigmoid(x):
    return 0.5 * jnp.tanh(0.5 * x) + 0.5


def shifted(value, tap):
    return value if tap == 2 else pltpu.roll(value, (2 - tap) % TILE, 0)


def each_tile(count, body):
    def step(t, carry):
        body(pl.multiple_of(t * TILE, TILE))
        return carry

    lax.fori_loop(0, count // TILE, step, 0, unroll=count == TILE)


def fetch(copies, sems, first=0):
    handles = []
    for k, (source, target) in enumerate(copies):
        handles.append(pltpu.make_async_copy(source, target, sems.at[first + k]))
        handles[-1].start()
    return handles


def context_kernel(early_ref, gate_hbm, state_hbm, bias_ref, fixed_ref, gate_ref, state_ref, padded, taps, sems):
    handles = fetch(
        [
            (gate_hbm.at[:, :, pl.ds(128, 128), :], gate_ref),
            (state_hbm.at[:, :, pl.ds(128, 128), :], state_ref),
        ],
        sems,
    )
    dests = early_ref.shape[0]
    count = fixed_ref.shape[1]
    per_dest = count // dests
    first = early_ref.shape[1] - per_dest
    pad = 2 * WIN
    padded[0:pad, :] = jnp.zeros((pad, 128), BF16)
    padded[pad + count : pad + count + pad, :] = jnp.zeros((pad, 128), BF16)
    for j in range(dests):
        padded[pad + j * per_dest : pad + (j + 1) * per_dest, :] = early_ref[j, first : first + per_dest, :]
    for handle in handles:
        handle.wait()
    for p in range(2):

        def one(at):
            for tap in range(5):
                if p == 0:
                    value = shifted(padded[pl.ds(pad + at, TILE), :].astype(F32), tap).astype(BF16)
                else:
                    value = padded[pl.ds(at + tap * WIN, TILE), :]
                taps[:, tap * 128 : (tap + 1) * 128] = value
            gate = gate_ref[p].reshape(640, 256)
            state = state_ref[p].reshape(640, 128)
            fixed_ref[p, pl.ds(at, TILE), 0:256] = dot(taps[...], gate) + bias_ref[p : p + 1, 0:256]
            fixed_ref[p, pl.ds(at, TILE), 256:384] = dot(taps[...], state) + bias_ref[p : p + 1, 256:384]

        each_tile(count, one)


def update_kernel(
    own, width, got_ref, fixed_ref, ow_ref, gate_hbm, state_hbm, head_ref, delta_ref,
    out_ref, base, hidden, motions, states, resets, updates, taps, flow, flow_cols, gate_ref, state_ref, sems,
):
    handles = []
    for p in range(2):
        for source, target in ((gate_hbm, gate_ref), (state_hbm, state_ref)):
            parts = [
                (source.at[p, :, pl.ds(256 * k, 128), :], target.at[p, :, pl.ds(128 * k, 128), :]) for k in range(2)
            ]
            handles.append(fetch(parts, sems, 2 * len(handles)))

    def ready(k):
        for handle in handles[k]:
            handle.wait()

    me, half = lax.axis_index("rows"), lax.axis_index("loop")
    dests, per_dest, _ = got_ref.shape
    rows_per = per_dest // WIN
    count = dests * per_dest
    pad = 2 * WIN
    first_col = (half * dests + me) * own - HALO
    column = first_col + iota((TILE, 128), 0) % WIN
    inside = (column >= 0) & (column < width)
    mask = jnp.where(inside, 1.0, 0.0)
    ow = ow_ref[...]
    add_row = OFFSET_SCALE * (ow[4:5] - ow[0:1] - ow[2:3])
    add_col = OFFSET_SCALE * (ow[5:6] - ow[1:2] - ow[3:4])

    for ref in (motions, states, resets):
        ref[0:pad, :] = jnp.zeros((pad, 128), BF16)
        ref[pad + count : pad + count + pad, :] = jnp.zeros((pad, 128), BF16)
    for j in range(dests):
        at = j * per_dest
        base[at : at + per_dest, :] = got_ref[j, :, 0:128]
        hidden[at : at + per_dest, :] = got_ref[j, :, 128:256].astype(F32)

    def finish(at, update, candidate):
        old = hidden[pl.ds(at, TILE), :]
        new = (old + update * (candidate - old)) * mask
        hidden[pl.ds(at, TILE), :] = new
        return new

    for iteration in range(ITERS):

        def columns_pass(at):
            motion = base[pl.ds(at, TILE), :].astype(F32)
            if iteration > 0:
                moved = flow_cols[pl.ds(at, TILE), :]
                motion = (motion + moved[:, 0:1] * add_row + moved[:, 1:2] * add_col) * mask
            motion = jnp.maximum(motion, 0.0)
            rounded = motion.astype(BF16)
            motions[pl.ds(pad + at, TILE), :] = rounded
            motion = rounded.astype(F32)
            state = hidden[pl.ds(at, TILE), :].astype(BF16).astype(F32)
            for tap in range(5):
                taps[:, tap * 256 : tap * 256 + 128] = shifted(state, tap).astype(BF16)
                taps[:, tap * 256 + 128 : tap * 256 + 256] = shifted(motion, tap).astype(BF16)
            if iteration == 0 and count == TILE:
                ready(0)
            gates = sigmoid(dot(taps[...], gate_ref[0].reshape(1280, 256)) + fixed_ref[0, pl.ds(at, TILE), 0:256])
            reset = (gates[:, 128:256] * state).astype(BF16).astype(F32)
            for tap in range(5):
                taps[:, tap * 256 : tap * 256 + 128] = shifted(reset, tap).astype(BF16)
            if iteration == 0 and count == TILE:
                ready(1)
            candidate = jnp.tanh(dot(taps[...], state_ref[0].reshape(1280, 128)) + fixed_ref[0, pl.ds(at, TILE), 256:384])
            states[pl.ds(pad + at, TILE), :] = finish(at, gates[:, 0:128], candidate).astype(BF16)

        def fill(first, at):
            for tap in range(5):
                taps[:, tap * 256 : tap * 256 + 128] = first[pl.ds(at + tap * WIN, TILE), :]
                taps[:, tap * 256 + 128 : tap * 256 + 256] = motions[pl.ds(at + tap * WIN, TILE), :]

        def gate_rows(at):
            fill(states, at)
            gates = sigmoid(dot(taps[...], gate_ref[1].reshape(1280, 256)) + fixed_ref[1, pl.ds(at, TILE), 0:256])
            updates[pl.ds(at, TILE), :] = gates[:, 0:128]
            resets[pl.ds(pad + at, TILE), :] = (
                gates[:, 128:256] * states[pl.ds(pad + at, TILE), :].astype(F32)
            ).astype(BF16)

        def state_rows(at):
            fill(resets, at)
            candidate = jnp.tanh(dot(taps[...], state_ref[1].reshape(1280, 128)) + fixed_ref[1, pl.ds(at, TILE), 256:384])
            new = finish(at, updates[pl.ds(at, TILE), :], candidate)
            lifted = jnp.maximum(dot(new.astype(BF16), head_ref[...]), 0.0).astype(BF16)
            step = dot_nt(delta_ref[...], lifted)
            if iteration == 0:
                flow[:, pl.ds(at, TILE)] = step
                flow_cols[pl.ds(at, TILE), :] = step.T
            else:
                flow[:, pl.ds(at, TILE)] = flow[:, pl.ds(at, TILE)] + step

        if iteration == 0 and count != TILE:
            ready(0)
            ready(1)
        each_tile(count, columns_pass)
        if iteration == 0:
            ready(2)
            ready(3)
        each_tile(count, gate_rows)
        each_tile(count, state_rows)

    for j in range(dests):
        for r in range(rows_per):
            at = j * per_dest + r * WIN + HALO
            out_ref[j, r * own : (r + 1) * own, :] = hidden[at : at + own, :]
        moved = flow[:, j * per_dest : (j + 1) * per_dest]
        out_ref[j, rows_per * own : rows_per * own + 8, :] = jnp.concatenate(
            [moved, jnp.zeros((8, 128 - per_dest), F32)], axis=1
        )


def local(
    frame_one,
    frame_two,
    context,
    carry_hidden,
    carry_flow,
    slot_target,
    slot_count,
    match_weight,
    offset_weight,
    gate_weight,
    state_weight,
    gru_bias,
    head_weight,
    delta_weight,
):
    dests = lax.axis_size("rows")
    halves = lax.axis_size("loop")
    rows_per, width, channels = frame_one.shape
    columns = frame_two.shape[1]
    pixels = rows_per * width
    slots, hidden_size = carry_hidden.shape
    cap = slots // dests
    own = columns // dests
    half_wide = round_up(columns - own + WIN, 8)
    padded = columns + half_wide
    room = 16 if dests <= 8 else 56

    rows_hidden = round_up(cap, 16)
    rows_slot = rows_hidden + round_up(8 * (-(-cap // 128)), 16)
    shard = frame_two.reshape(1, rows_per, columns, channels)
    if dests == 8:

        def swap(value, flip):
            return lax.ppermute(value, "rows", [(i, i ^ flip) for i in range(dests)])

        beside, near, wrap, across = (swap(shard, flip) for flip in (1, 2, 6, 4))
        near_beside, wrap_beside = (swap(beside, flip) for flip in (2, 6))
    else:
        beside = lax.all_gather(shard, "rows", axis=0, tiled=True)
    slot_target, beside = lax.optimization_barrier((slot_target, beside))
    packed = call(
        functools.partial(pack_kernel, dests, cap, pixels, own, half_wide),
        jax.ShapeDtypeStruct((dests, rows_slot + rows_per * WIN, hidden_size), BF16),
        [smem_spec()] + vmem_specs(4),
        [pltpu.VMEM((rows_per, padded, 128), F32)],
        (2 * slots * slots * 128, 1 << 20, 0),
        60,
        slot_count,
        slot_target.reshape(slots // 128, 128),
        carry_flow.T,
        carry_hidden,
        context,
    )
    if dests == 8:
        packed, near, wrap, across, near_beside, wrap_beside = lax.optimization_barrier(
            (packed, near, wrap, across, near_beside, wrap_beside)
        )
        keys = (shard, beside, near, near_beside, across, swap(across, 1), wrap, wrap_beside)
    else:
        keys = (beside,)
    early = lax.all_to_all(packed, "rows", 0, 0, tiled=True)
    ow = jnp.pad(offset_weight, ((0, 2), (0, 0)))
    hidden_wide, flow_first, term = call(
        functools.partial(place_kernel, cap, half_wide, rows_per),
        (
            jax.ShapeDtypeStruct((rows_per, half_wide, 128), BF16),
            jax.ShapeDtypeStruct((8, pixels), F32),
            jax.ShapeDtypeStruct((rows_per, half_wide, 128), F32),
        ),
        vmem_specs(2),
        [pltpu.VMEM((rows_per, padded, 128), F32)] * 2,
        (2 * slots * pixels * 128, 1 << 20, 0),
        room,
        early,
        ow,
    )
    queries = frame_one.reshape(pixels, channels)
    chunks = dests // 2
    tile = 128
    keep, send = call(
        functools.partial(match_kernel, len(keys), len(keys) > 1, half_wide, rows_per),
        (jax.ShapeDtypeStruct((rows_per, half_wide, 384), F32),) * 2,
        vmem_specs(3 + len(keys)),
        [
            pltpu.VMEM((chunks, 4 * columns, channels), BF16),
            pltpu.VMEM((chunks, columns, channels), BF16),
            pltpu.VMEM((chunks, tile, 4 * columns), F32),
            pltpu.VMEM((pixels, 384), F32),
            pltpu.VMEM((rows_per, padded, 384), F32),
        ],
        (4 * pixels * chunks * 4 * columns * channels, 1 << 21, pixels * chunks * 5 * columns),
        room,
        queries,
        match_weight,
        ow,
        *keys,
    )
    other = lax.ppermute(send, "loop", [(i, (i + 1) % halves) for i in range(halves)])
    sending = call(
        functools.partial(merge_kernel, own),
        jax.ShapeDtypeStruct((dests, rows_per * WIN, 256), BF16),
        vmem_specs(4),
        [],
        (0, 1 << 20, 0),
        room,
        keep,
        other,
        term,
        hidden_wide,
    )
    arrived = lax.all_to_all(sending, "rows", 0, 0, tiled=True)
    count = dests * rows_per * WIN
    back_rows = rows_per * own + 8
    hbm = pl.BlockSpec(memory_space=pltpu.HBM)
    gate_weight = pltpu.with_memory_space_constraint(gate_weight, pltpu.HBM)
    state_weight = pltpu.with_memory_space_constraint(state_weight, pltpu.HBM)
    fixed = call(
        context_kernel,
        jax.ShapeDtypeStruct((2, count, 384), F32),
        [vmem_specs(1)[0], hbm, hbm, vmem_specs(1)[0]],
        [
            pltpu.VMEM((2, 5, 128, 256), BF16),
            pltpu.VMEM((2, 5, 128, 128), BF16),
            pltpu.VMEM((count + 4 * WIN, 128), BF16),
            pltpu.VMEM((TILE, 640), BF16),
            pltpu.SemaphoreType.DMA((2,)),
        ],
        (4 * count * 5 * 128 * 384, 1 << 22, 0),
        room,
        early,
        gate_weight,
        state_weight,
        gru_bias,
    )
    outgoing = call(
        functools.partial(update_kernel, own, width),
        jax.ShapeDtypeStruct((dests, back_rows, 128), F32),
        vmem_specs(3) + [hbm, hbm] + vmem_specs(2),
        [
            pltpu.VMEM((count, 128), BF16),
            pltpu.VMEM((count, 128), F32),
            pltpu.VMEM((count + 4 * WIN, 128), BF16),
            pltpu.VMEM((count + 4 * WIN, 128), BF16),
            pltpu.VMEM((count + 4 * WIN, 128), BF16),
            pltpu.VMEM((count, 128), F32),
            pltpu.VMEM((TILE, 1280), BF16),
            pltpu.VMEM((8, count), F32),
            pltpu.VMEM((count, 8), F32),
            pltpu.VMEM((2, 5, 256, 256), BF16),
            pltpu.VMEM((2, 5, 256, 128), BF16),
            pltpu.SemaphoreType.DMA((8,)),
        ],
        (8 * count * 5 * 256 * 384, 1 << 22, 8 * count * 384),
        room,
        arrived,
        fixed,
        ow,
        gate_weight,
        state_weight,
        head_weight,
        jnp.pad(delta_weight, ((0, 6), (0, 0))),
    )
    back = lax.all_to_all(outgoing, "rows", 0, 0, tiled=True)
    both = lax.all_gather(back, "loop", axis=0)
    cells = both[:, :, : rows_per * own, :].reshape(halves, dests, rows_per, own, hidden_size)
    hidden_out = cells.transpose(2, 0, 1, 3, 4).reshape(rows_per, width, hidden_size)
    moved = both[:, :, rows_per * own : rows_per * own + 2, : rows_per * WIN]
    moved = moved.reshape(halves, dests, 2, rows_per, WIN)[..., HALO : HALO + own]
    moved = moved.transpose(2, 3, 0, 1, 4).reshape(2, rows_per, width)
    flow_out = flow_first[:2].reshape(2, rows_per, width) + moved
    return (hidden_out, flow_out)


def solution(mesh):
    return jax.shard_map(
        local,
        mesh=mesh,
        in_specs=(
            P(("groups", "rows"), None, None),
            P(("groups", "rows"), "loop", None),
            P(("groups", "rows"), None, None),
            P(("groups", "rows"), None),
            P(("groups", "rows"), None),
            P(("groups", "rows")),
            P(("groups", "rows")),
            P(),
            P(),
            P(),
            P(),
            P(),
            P(),
            P(),
        ),
        out_specs=(P(("groups", "rows"), None, None), P(None, ("groups", "rows"), None)),
        check_vma=False,
    )
```

```python
import functools
import math

import jax
import jax.numpy as jnp
from jax import lax
from jax.experimental import pallas as pl
from jax.experimental.pallas import tpu as pltpu
from jax.sharding import PartitionSpec as P

ITERS = 2
WIN = 32
HALO = 8
TILE = 512
OFFSET_SCALE = 0.03125
F32 = jnp.float32
BF16 = jnp.bfloat16
VMEM = pltpu.VMEM
NT = (((1,), (1,)), ((), ()))


def iota(shape, dim):
    return lax.broadcasted_iota(jnp.int32, shape, dim)


def round_up(value, step):
    return -(-value // step) * step


def dot(a, b):
    return jnp.dot(a, b, preferred_element_type=F32)


def dot_nt(a, b):
    return lax.dot_general(a, b, NT, preferred_element_type=F32)


def vmem_specs(count):
    return [pl.BlockSpec(memory_space=VMEM)] * count


def smem_spec():
    return pl.BlockSpec(memory_space=pltpu.SMEM)


def loop(count, body, carry):
    return lax.fori_loop(0, count, body, carry, unroll=count <= 4)


def call(kernel, out_shape, in_specs, scratch, cost, room, *args):
    single = not isinstance(out_shape, (tuple, list))
    return pl.pallas_call(
        kernel,
        out_shape=out_shape,
        in_specs=in_specs,
        out_specs=vmem_specs(1)[0] if single else vmem_specs(len(out_shape)),
        scratch_shapes=scratch,
        compiler_params=pltpu.CompilerParams(vmem_limit_bytes=room * 1024 * 1024),
        cost_estimate=pl.CostEstimate(flops=cost[0], bytes_accessed=cost[1], transcendentals=cost[2]),
    )(*args)


def pack_kernel(dests, cap, pixels, own, half_wide, count_ref, target_ref, flow_ref, hidden_ref, context_ref, out_ref, wide):
    slots = hidden_ref.shape[0]
    target = jnp.concatenate([target_ref[k : k + 1, :] for k in range(slots // 128)], axis=1)
    counted = iota((1, slots), 1) < count_ref[0]
    owner = target // pixels
    within = target % pixels
    belongs = (iota((dests, slots), 0) == owner) & counted
    member = jnp.where(belongs, 1.0, 0.0)
    upper = jnp.where(iota((128, 128), 0) <= iota((128, 128), 1), 1.0, 0.0).astype(BF16)
    before = jnp.zeros((dests, 1), F32)
    ranks = []
    for start in range(0, slots, 128):
        running = dot(member[:, start : start + 128].astype(BF16), upper) + before
        before = running[:, 127:128]
        ranks.append(running)
    rank = jnp.concatenate(ranks, axis=1) - 1.0 - (lax.axis_index("loop") * cap).astype(F32)
    belongs = belongs & (rank >= 0.0) & (rank < cap)
    place_at = jnp.sum(
        jnp.where(belongs, rank + iota((dests, slots), 0).astype(F32) * cap, 0.0), axis=0, keepdims=True
    )
    taken = jnp.max(jnp.where(belongs, 1.0, 0.0), axis=0, keepdims=True)
    landing = jnp.where(taken > 0.5, place_at, -1.0).astype(jnp.int32)
    row = iota((8, slots), 0)
    flow = flow_ref[...].astype(F32)
    side = jnp.where(row == 0, flow[0:1], 0.0)
    side = jnp.where(row == 1, flow[1:2], side)
    side = jnp.where(row == 2, (within // 256).astype(F32), side)
    side = jnp.where(row == 3, (within % 256).astype(F32), side)
    side = jnp.where(row == 4, 1.0, side).astype(BF16)
    hidden = hidden_ref[...]
    rows_hidden = round_up(cap, 16)
    together = max(1, min(dests, 192 // cap))
    for first in range(0, dests, together):
        spots = together * cap
        chosen = jnp.where(iota((spots, slots), 0) + first * cap == landing, 1.0, 0.0).astype(BF16)
        moved = dot(chosen, hidden)
        moved_side = dot_nt(side, chosen)
        for k in range(together):
            out_ref[first + k, 0:cap, :] = moved[k * cap : (k + 1) * cap].astype(BF16)
            for t in range(-(-cap // 128)):
                width = min(128, cap - t * 128)
                piece = moved_side[:, k * cap + t * 128 : k * cap + t * 128 + width]
                if width < 128:
                    piece = jnp.concatenate([piece, jnp.zeros((8, 128 - width), F32)], axis=1)
                base = rows_hidden + 8 * t
                out_ref[first + k, base : base + 8, :] = piece.astype(BF16)
    rows_per, width, _ = context_ref.shape
    top = out_ref.shape[1] - rows_per * WIN
    start = pl.multiple_of(lax.axis_index("loop") * (width // 2), 128)
    wide[...] = jnp.zeros_like(wide)
    for r in range(rows_per):
        wide[r, HALO : HALO + width, :] = context_ref[r].astype(F32)
        part = wide[r, pl.ds(start, half_wide), :]
        for j in range(dests):
            out_ref[j, top + r * WIN : top + (r + 1) * WIN, :] = part[j * own : j * own + WIN].astype(BF16)


def place_kernel(cap, half_wide, rows_per, first_ref, second_ref, ow_ref, hidden_ref, flow_ref, term_ref, wide_hidden, wide_term):
    half = lax.axis_index("loop")
    dests = first_ref.shape[0]
    pixels = flow_ref.shape[1]
    width = pixels // rows_per
    rows_hidden = round_up(cap, 16)
    hidden = jnp.zeros((pixels, 128), F32)
    flow = jnp.zeros((8, pixels), F32)
    for j, got_ref in [(j, ref) for j in range(dests) for ref in (first_ref, second_ref)]:
        pieces = []
        for t in range(-(-cap // 128)):
            base = rows_hidden + 8 * t
            pieces.append(got_ref[j, base : base + 8, 0 : min(128, cap - t * 128)].astype(F32))
        side = pieces[0] if len(pieces) == 1 else jnp.concatenate(pieces, axis=1)
        place = jnp.where(side[4:5] > 0.5, side[2:3] * 256.0 + side[3:4], -1.0).astype(jnp.int32)
        chosen = jnp.where(iota((pixels, cap), 0) == place, 1.0, 0.0).astype(BF16)
        hidden = hidden + dot(chosen, got_ref[j, 0:cap, :])
        flow = flow + dot_nt(side.astype(BF16), chosen)
    flow_ref[...] = flow
    columns = flow.T
    ow = ow_ref[...]
    term = columns[:, 0:1] * (OFFSET_SCALE * (ow[4:5] - ow[0:1] - ow[2:3])) + columns[:, 1:2] * (
        OFFSET_SCALE * (ow[5:6] - ow[1:2] - ow[3:4])
    )
    start = pl.multiple_of(half * (width // 2), 128)
    for wide, value, out in ((wide_hidden, hidden, hidden_ref), (wide_term, term, term_ref)):
        wide[...] = jnp.zeros_like(wide)
        for r in range(rows_per):
            wide[r, HALO : HALO + width, :] = value[r * width : (r + 1) * width]
            out[r] = wide[r, pl.ds(start, half_wide), :].astype(out.dtype)


def match_kernel(
    count, flip, half_wide, rows_per, queries_ref, weight_ref, ow_ref, *refs
):
    key_refs, (keep_ref, send_ref, fine, coarse, scores, mixed, wide) = refs[:count], refs[count:]
    me, half = lax.axis_index("rows"), lax.axis_index("loop")
    pixels, channels = queries_ref.shape
    width = pixels // rows_per
    columns = width // 2
    quarter = columns // 2
    chunks = fine.shape[0]
    shards = chunks * 2
    per_ref = shards // count
    spread = jnp.where(
        iota((columns, columns), 1)
        == jnp.where(iota((columns, columns), 0) < quarter, 2 * iota((columns, columns), 0), 2 * (iota((columns, columns), 0) - quarter) + 1),
        1.0,
        0.0,
    ).astype(BF16)

    def sort_shard(ref, m, shard, lane):
        even, odd = [], []
        for r in range(rows_per):
            parted = dot(spread, ref[m, r])
            even.append(parted[:quarter])
            odd.append(parted[quarter:])
            for p, part in ((0, even[-1]), (1, odd[-1])):
                g = 2 * r + p
                fine[shard, g * 2 * quarter + lane * quarter : g * 2 * quarter + (lane + 1) * quarter, :] = part.astype(BF16)
        pooled = (even[0] + odd[0] + even[1] + odd[1]) * 0.25
        coarse[shard, lane * quarter : (lane + 1) * quarter, :] = pooled.astype(BF16)

    if per_ref == 1:
        for m in range(shards):
            sort_shard(key_refs[m], 0, m // 2, m % 2)
    else:
        def sort_chunk(c, carry):
            for lane in range(2):
                sort_shard(key_refs[0], c * 2 + lane, c, lane)
            return carry

        lax.fori_loop(0, chunks, sort_chunk, 0)

    group = 2 * quarter
    tile = scores.shape[1]
    lane = iota((1, group), 1)
    lane_col = ((lane % quarter) * 2 + half * columns).astype(F32)
    ow = ow_ref[...] * OFFSET_SCALE
    weight = weight_ref[...]

    def lane_row(c):
        arrival = c * 2 + lane // quarter
        shard = lax.bitwise_xor(arrival, me) if flip else arrival
        return (shard * rows_per).astype(F32)

    wide[...] = jnp.zeros_like(wide)

    def one_tile(t, carry):
        first = pl.multiple_of(t * tile, tile)
        queries = queries_ref[pl.ds(first, tile), :] * jnp.asarray(1.0 / math.sqrt(channels), BF16)

        def score(c, peaks):
            values = dot_nt(queries, fine[c])
            scores[c] = values
            parts = [values[:, g * group : (g + 1) * group] for g in range(4)]
            blended = (parts[0] + parts[1] + parts[2] + parts[3]) * 0.25
            high = jnp.maximum(jnp.maximum(parts[0], parts[1]), jnp.maximum(parts[2], parts[3]))
            return jnp.maximum(peaks[0], high), jnp.maximum(peaks[1], blended)

        low = jnp.full((tile, group), -jnp.inf, F32)
        peaks = loop(chunks, score, (low, low))
        peak_fine = jnp.max(peaks[0], axis=1, keepdims=True)
        peak_coarse = jnp.max(peaks[1], axis=1, keepdims=True)

        def absorb(c, so_far):
            total, below, right, rows, c_total, c_rows, acc_fine, acc_coarse = so_far
            parts = [scores[c, :, g * group : (g + 1) * group] for g in range(4)]
            blended = (parts[0] + parts[1] + parts[2] + parts[3]) * 0.25
            expo = [jnp.exp(part - peak_fine) for part in parts]
            c_expo = jnp.exp(blended - peak_coarse)
            lower = expo[2] + expo[3]
            everything = expo[0] + expo[1] + lower
            at = lane_row(c)
            weights = jnp.concatenate([e.astype(BF16) for e in expo], axis=1)
            return (
                total + everything,
                below + lower,
                right + (expo[1] + expo[3]),
                rows + everything * at,
                c_total + c_expo,
                c_rows + c_expo * at,
                acc_fine + dot(weights, fine[c]),
                acc_coarse + dot(c_expo.astype(BF16), coarse[c]),
            )

        zero = jnp.zeros((tile, group), F32)
        blank = jnp.zeros((tile, channels), F32)
        total, below, right, rows, c_total, c_rows, acc_fine, acc_coarse = loop(
            chunks, absorb, (zero, zero, zero, zero, zero, zero, blank, blank)
        )

        def over(value):
            return jnp.sum(value, axis=1, keepdims=True)

        pixel = first + iota((tile, 1), 0)
        own_row = (me * rows_per + pixel // width).astype(F32)
        own_col = (pixel % width).astype(F32)
        fine_sum, coarse_sum = over(total), over(c_total)
        fine_row = over(rows + below) / fine_sum - own_row
        fine_col = over(total * lane_col + right) / fine_sum - own_col
        coarse_row = over(c_rows) / coarse_sum + 0.5 - own_row
        coarse_col = over(c_total * lane_col) / coarse_sum + 0.5 - own_col
        fine_out = dot((acc_fine / fine_sum).astype(BF16), weight[:channels])
        coarse_out = dot((acc_coarse / coarse_sum).astype(BF16), weight[channels:])
        mixed[pl.ds(first, tile), 0:128] = fine_out + fine_row * ow[0:1] + fine_col * ow[1:2]
        mixed[pl.ds(first, tile), 128:256] = coarse_out + coarse_row * ow[2:3] + coarse_col * ow[3:4]
        mixed[pl.ds(first, tile), 256:384] = jnp.where(
            iota((tile, 128), 1) < 64,
            peak_fine + jnp.log(fine_sum),
            peak_coarse + jnp.log(coarse_sum),
        )
        return carry

    lax.fori_loop(0, pixels // tile, one_tile, 0)
    start = pl.multiple_of(half * columns, 128)
    other = pl.multiple_of((1 - half) * columns, 128)
    for r in range(rows_per):
        wide[r, HALO : HALO + width, :] = mixed[r * width : (r + 1) * width, :]
        keep_ref[r] = wide[r, pl.ds(start, half_wide), :]
        send_ref[r] = wide[r, pl.ds(other, half_wide), :]


def merge_kernel(own, keep_ref, got_ref, term_ref, hidden_ref, out_ref):
    dests = out_ref.shape[0]
    for r in range(keep_ref.shape[0]):
        keep, got = keep_ref[r], got_ref[r]
        gap = got[:, 256:384] - keep[:, 256:384]
        share = 1.0 / (1.0 + jnp.exp(gap))
        share_fine, share_coarse = share[:, 0:1], share[:, 64:65]
        base = (
            got[:, 0:128]
            + (keep[:, 0:128] - got[:, 0:128]) * share_fine
            + got[:, 128:256]
            + (keep[:, 128:256] - got[:, 128:256]) * share_coarse
            + term_ref[r]
        )
        hidden = hidden_ref[r].astype(F32)
        for j in range(dests):
            out_ref[j, r * WIN : (r + 1) * WIN, 0:128] = base[j * own : j * own + WIN].astype(BF16)
            out_ref[j, r * WIN : (r + 1) * WIN, 128:256] = hidden[j * own : j * own + WIN].astype(BF16)


def sigmoid(x):
    return 0.5 * jnp.tanh(0.5 * x) + 0.5


def shifted(value, tap):
    return value if tap == 2 else pltpu.roll(value, (2 - tap) % TILE, 0)


def each_tile(count, body):
    def step(t, carry):
        body(pl.multiple_of(t * TILE, TILE))
        return carry

    lax.fori_loop(0, count // TILE, step, 0, unroll=count == TILE)


def fetch(copies, sems, first=0):
    handles = []
    for k, (source, target) in enumerate(copies):
        handles.append(pltpu.make_async_copy(source, target, sems.at[first + k]))
        handles[-1].start()
    return handles


def context_kernel(early_ref, gate_hbm, state_hbm, bias_ref, fixed_ref, gate_ref, state_ref, padded, taps, sems):
    handles = fetch(
        [
            (gate_hbm.at[:, :, pl.ds(128, 128), :], gate_ref),
            (state_hbm.at[:, :, pl.ds(128, 128), :], state_ref),
        ],
        sems,
    )
    dests = early_ref.shape[0]
    count = fixed_ref.shape[1]
    per_dest = count // dests
    first = early_ref.shape[1] - per_dest
    pad = 2 * WIN
    padded[0:pad, :] = jnp.zeros((pad, 128), BF16)
    padded[pad + count : pad + count + pad, :] = jnp.zeros((pad, 128), BF16)
    for j in range(dests):
        padded[pad + j * per_dest : pad + (j + 1) * per_dest, :] = early_ref[j, first : first + per_dest, :]
    for handle in handles:
        handle.wait()
    for p in range(2):

        def one(at):
            for tap in range(5):
                if p == 0:
                    value = shifted(padded[pl.ds(pad + at, TILE), :].astype(F32), tap).astype(BF16)
                else:
                    value = padded[pl.ds(at + tap * WIN, TILE), :]
                taps[:, tap * 128 : (tap + 1) * 128] = value
            gate = gate_ref[p].reshape(640, 256)
            state = state_ref[p].reshape(640, 128)
            fixed_ref[p, pl.ds(at, TILE), 0:256] = dot(taps[...], gate) + bias_ref[p : p + 1, 0:256]
            fixed_ref[p, pl.ds(at, TILE), 256:384] = dot(taps[...], state) + bias_ref[p : p + 1, 256:384]

        each_tile(count, one)


def update_kernel(
    own, width, got_ref, fixed_ref, ow_ref, gate_hbm, state_hbm, head_ref, delta_ref,
    out_ref, base, hidden, motions, states, resets, updates, taps, flow, flow_cols, gate_ref, state_ref, sems,
):
    handles = []
    for p in range(2):
        for source, target in ((gate_hbm, gate_ref), (state_hbm, state_ref)):
            parts = [
                (source.at[p, :, pl.ds(256 * k, 128), :], target.at[p, :, pl.ds(128 * k, 128), :]) for k in range(2)
            ]
            handles.append(fetch(parts, sems, 2 * len(handles)))

    def ready(k):
        for handle in handles[k]:
            handle.wait()

    me, half = lax.axis_index("rows"), lax.axis_index("loop")
    dests, per_dest, _ = got_ref.shape
    rows_per = per_dest // WIN
    count = dests * per_dest
    pad = 2 * WIN
    first_col = (half * dests + me) * own - HALO
    column = first_col + iota((TILE, 128), 0) % WIN
    inside = (column >= 0) & (column < width)
    mask = jnp.where(inside, 1.0, 0.0)
    ow = ow_ref[...]
    add_row = OFFSET_SCALE * (ow[4:5] - ow[0:1] - ow[2:3])
    add_col = OFFSET_SCALE * (ow[5:6] - ow[1:2] - ow[3:4])

    for ref in (motions, states, resets):
        ref[0:pad, :] = jnp.zeros((pad, 128), BF16)
        ref[pad + count : pad + count + pad, :] = jnp.zeros((pad, 128), BF16)
    for j in range(dests):
        at = j * per_dest
        base[at : at + per_dest, :] = got_ref[j, :, 0:128]
        hidden[at : at + per_dest, :] = got_ref[j, :, 128:256].astype(F32)

    def finish(at, update, candidate):
        old = hidden[pl.ds(at, TILE), :]
        new = (old + update * (candidate - old)) * mask
        hidden[pl.ds(at, TILE), :] = new
        return new

    for iteration in range(ITERS):

        def columns_pass(at):
            motion = base[pl.ds(at, TILE), :].astype(F32)
            if iteration > 0:
                moved = flow_cols[pl.ds(at, TILE), :]
                motion = (motion + moved[:, 0:1] * add_row + moved[:, 1:2] * add_col) * mask
            motion = jnp.maximum(motion, 0.0)
            rounded = motion.astype(BF16)
            motions[pl.ds(pad + at, TILE), :] = rounded
            motion = rounded.astype(F32)
            state = hidden[pl.ds(at, TILE), :].astype(BF16).astype(F32)
            for tap in range(5):
                taps[:, tap * 256 : tap * 256 + 128] = shifted(state, tap).astype(BF16)
                taps[:, tap * 256 + 128 : tap * 256 + 256] = shifted(motion, tap).astype(BF16)
            if iteration == 0 and count == TILE:
                ready(0)
            gates = sigmoid(dot(taps[...], gate_ref[0].reshape(1280, 256)) + fixed_ref[0, pl.ds(at, TILE), 0:256])
            reset = (gates[:, 128:256] * state).astype(BF16).astype(F32)
            for tap in range(5):
                taps[:, tap * 256 : tap * 256 + 128] = shifted(reset, tap).astype(BF16)
            if iteration == 0 and count == TILE:
                ready(1)
            candidate = jnp.tanh(dot(taps[...], state_ref[0].reshape(1280, 128)) + fixed_ref[0, pl.ds(at, TILE), 256:384])
            states[pl.ds(pad + at, TILE), :] = finish(at, gates[:, 0:128], candidate).astype(BF16)

        def fill(first, at):
            for tap in range(5):
                taps[:, tap * 256 : tap * 256 + 128] = first[pl.ds(at + tap * WIN, TILE), :]
                taps[:, tap * 256 + 128 : tap * 256 + 256] = motions[pl.ds(at + tap * WIN, TILE), :]

        def gate_rows(at):
            fill(states, at)
            gates = sigmoid(dot(taps[...], gate_ref[1].reshape(1280, 256)) + fixed_ref[1, pl.ds(at, TILE), 0:256])
            updates[pl.ds(at, TILE), :] = gates[:, 0:128]
            resets[pl.ds(pad + at, TILE), :] = (
                gates[:, 128:256] * states[pl.ds(pad + at, TILE), :].astype(F32)
            ).astype(BF16)

        def state_rows(at):
            fill(resets, at)
            candidate = jnp.tanh(dot(taps[...], state_ref[1].reshape(1280, 128)) + fixed_ref[1, pl.ds(at, TILE), 256:384])
            new = finish(at, updates[pl.ds(at, TILE), :], candidate)
            lifted = jnp.maximum(dot(new.astype(BF16), head_ref[...]), 0.0).astype(BF16)
            step = dot_nt(delta_ref[...], lifted)
            if iteration == 0:
                flow[:, pl.ds(at, TILE)] = step
                flow_cols[pl.ds(at, TILE), :] = step.T
            else:
                flow[:, pl.ds(at, TILE)] = flow[:, pl.ds(at, TILE)] + step

        if iteration == 0 and count != TILE:
            ready(0)
            ready(1)
        each_tile(count, columns_pass)
        if iteration == 0:
            ready(2)
            ready(3)
        each_tile(count, gate_rows)
        each_tile(count, state_rows)

    for j in range(dests):
        for r in range(rows_per):
            at = j * per_dest + r * WIN + HALO
            out_ref[j, r * own : (r + 1) * own, :] = hidden[at : at + own, :]
        moved = flow[:, j * per_dest : (j + 1) * per_dest]
        out_ref[j, rows_per * own : rows_per * own + 8, :] = jnp.concatenate(
            [moved, jnp.zeros((8, 128 - per_dest), F32)], axis=1
        )


def local(
    frame_one,
    frame_two,
    context,
    carry_hidden,
    carry_flow,
    slot_target,
    slot_count,
    match_weight,
    offset_weight,
    gate_weight,
    state_weight,
    gru_bias,
    head_weight,
    delta_weight,
):
    dests = lax.axis_size("rows")
    halves = lax.axis_size("loop")
    rows_per, width, channels = frame_one.shape
    columns = frame_two.shape[1]
    pixels = rows_per * width
    slots, hidden_size = carry_hidden.shape
    cap = -(-slots // (dests * halves))
    own = columns // dests
    half_wide = round_up(columns - own + WIN, 8)
    padded = columns + half_wide
    room = 16 if dests <= 8 else 56

    rows_hidden = round_up(cap, 16)
    rows_slot = rows_hidden + round_up(8 * (-(-cap // 128)), 16)
    shard = frame_two.reshape(1, rows_per, columns, channels)
    if dests == 8:

        def swap(value, flip):
            return lax.ppermute(value, "rows", [(i, i ^ flip) for i in range(dests)])

        beside, near, wrap, across = (swap(shard, flip) for flip in (1, 2, 6, 4))
        near_beside, wrap_beside = (swap(beside, flip) for flip in (2, 6))
    else:
        beside = lax.all_gather(shard, "rows", axis=0, tiled=True)
    slot_target, beside = lax.optimization_barrier((slot_target, beside))
    packed = call(
        functools.partial(pack_kernel, dests, cap, pixels, own, half_wide),
        jax.ShapeDtypeStruct((dests, rows_slot + rows_per * WIN, hidden_size), BF16),
        [smem_spec()] + vmem_specs(4),
        [pltpu.VMEM((rows_per, padded, 128), F32)],
        (2 * slots * slots * 128, 1 << 20, 0),
        60,
        slot_count,
        slot_target.reshape(slots // 128, 128),
        carry_flow.T,
        carry_hidden,
        context,
    )
    if dests == 8:
        packed, across = lax.optimization_barrier((packed, across))
        across_beside = swap(across, 1)
        packed, near, wrap, near_beside, wrap_beside, across_beside = lax.optimization_barrier(
            (packed, near, wrap, near_beside, wrap_beside, across_beside)
        )
        keys = (shard, beside, near, near_beside, across, across_beside, wrap, wrap_beside)
    else:
        keys = (beside,)
    early = lax.all_to_all(packed, "rows", 0, 0, tiled=True)
    around = [(i, (i + 1) % halves) for i in range(halves)]
    early_other = lax.ppermute(early, "loop", around)
    ow = jnp.pad(offset_weight, ((0, 2), (0, 0)))
    hidden_wide, flow_first, term = call(
        functools.partial(place_kernel, cap, half_wide, rows_per),
        (
            jax.ShapeDtypeStruct((rows_per, half_wide, 128), BF16),
            jax.ShapeDtypeStruct((8, pixels), F32),
            jax.ShapeDtypeStruct((rows_per, half_wide, 128), F32),
        ),
        vmem_specs(3),
        [pltpu.VMEM((rows_per, padded, 128), F32)] * 2,
        (2 * slots * pixels * 128, 1 << 20, 0),
        room,
        early,
        early_other,
        ow,
    )
    queries = frame_one.reshape(pixels, channels)
    chunks = dests // 2
    tile = 128
    keep, send = call(
        functools.partial(match_kernel, len(keys), len(keys) > 1, half_wide, rows_per),
        (jax.ShapeDtypeStruct((rows_per, half_wide, 384), F32),) * 2,
        vmem_specs(3 + len(keys)),
        [
            pltpu.VMEM((chunks, 4 * columns, channels), BF16),
            pltpu.VMEM((chunks, columns, channels), BF16),
            pltpu.VMEM((chunks, tile, 4 * columns), F32),
            pltpu.VMEM((pixels, 384), F32),
            pltpu.VMEM((rows_per, padded, 384), F32),
        ],
        (4 * pixels * chunks * 4 * columns * channels, 1 << 21, pixels * chunks * 5 * columns),
        room,
        queries,
        match_weight,
        ow,
        *keys,
    )
    other = lax.ppermute(send, "loop", around)
    sending = call(
        functools.partial(merge_kernel, own),
        jax.ShapeDtypeStruct((dests, rows_per * WIN, 256), BF16),
        vmem_specs(4),
        [],
        (0, 1 << 20, 0),
        room,
        keep,
        other,
        term,
        hidden_wide,
    )
    arrived = lax.all_to_all(sending, "rows", 0, 0, tiled=True)
    count = dests * rows_per * WIN
    back_rows = rows_per * own + 8
    hbm = pl.BlockSpec(memory_space=pltpu.HBM)
    gate_weight = pltpu.with_memory_space_constraint(gate_weight, pltpu.HBM)
    state_weight = pltpu.with_memory_space_constraint(state_weight, pltpu.HBM)
    fixed = call(
        context_kernel,
        jax.ShapeDtypeStruct((2, count, 384), F32),
        [vmem_specs(1)[0], hbm, hbm, vmem_specs(1)[0]],
        [
            pltpu.VMEM((2, 5, 128, 256), BF16),
            pltpu.VMEM((2, 5, 128, 128), BF16),
            pltpu.VMEM((count + 4 * WIN, 128), BF16),
            pltpu.VMEM((TILE, 640), BF16),
            pltpu.SemaphoreType.DMA((2,)),
        ],
        (4 * count * 5 * 128 * 384, 1 << 22, 0),
        room,
        early,
        gate_weight,
        state_weight,
        gru_bias,
    )
    outgoing = call(
        functools.partial(update_kernel, own, width),
        jax.ShapeDtypeStruct((dests, back_rows, 128), F32),
        vmem_specs(3) + [hbm, hbm] + vmem_specs(2),
        [
            pltpu.VMEM((count, 128), BF16),
            pltpu.VMEM((count, 128), F32),
            pltpu.VMEM((count + 4 * WIN, 128), BF16),
            pltpu.VMEM((count + 4 * WIN, 128), BF16),
            pltpu.VMEM((count + 4 * WIN, 128), BF16),
            pltpu.VMEM((count, 128), F32),
            pltpu.VMEM((TILE, 1280), BF16),
            pltpu.VMEM((8, count), F32),
            pltpu.VMEM((count, 8), F32),
            pltpu.VMEM((2, 5, 256, 256), BF16),
            pltpu.VMEM((2, 5, 256, 128), BF16),
            pltpu.SemaphoreType.DMA((8,)),
        ],
        (8 * count * 5 * 256 * 384, 1 << 22, 8 * count * 384),
        room,
        arrived,
        fixed,
        ow,
        gate_weight,
        state_weight,
        head_weight,
        jnp.pad(delta_weight, ((0, 6), (0, 0))),
    )
    back = lax.all_to_all(outgoing, "rows", 0, 0, tiled=True)
    both = lax.all_gather(back, "loop", axis=0)
    cells = both[:, :, : rows_per * own, :].reshape(halves, dests, rows_per, own, hidden_size)
    hidden_out = cells.transpose(2, 0, 1, 3, 4).reshape(rows_per, width, hidden_size)
    moved = both[:, :, rows_per * own : rows_per * own + 2, : rows_per * WIN]
    moved = moved.reshape(halves, dests, 2, rows_per, WIN)[..., HALO : HALO + own]
    moved = moved.transpose(2, 3, 0, 1, 4).reshape(2, rows_per, width)
    flow_out = flow_first[:2].reshape(2, rows_per, width) + moved
    return (hidden_out, flow_out)


def solution(mesh):
    return jax.shard_map(
        local,
        mesh=mesh,
        in_specs=(
            P(("groups", "rows"), None, None),
            P(("groups", "rows"), "loop", None),
            P(("groups", "rows"), None, None),
            P(("groups", "rows"), None),
            P(("groups", "rows"), None),
            P(("groups", "rows")),
            P(("groups", "rows")),
            P(),
            P(),
            P(),
            P(),
            P(),
            P(),
            P(),
        ),
        out_specs=(P(("groups", "rows"), None, None), P(None, ("groups", "rows"), None)),
        check_vma=False,
    )
```

```python
import functools
import math

import jax
import jax.numpy as jnp
from jax import lax
from jax.experimental import pallas as pl
from jax.experimental.pallas import tpu as pltpu
from jax.sharding import PartitionSpec as P

ITERS = 2
WIN = 32
SLIM = 16
HALO = 8
TILE = 512
SLIM_TILE = TILE * SLIM // WIN
OFFSET_SCALE = 0.03125
F32 = jnp.float32
BF16 = jnp.bfloat16
VMEM = pltpu.VMEM
NT = (((1,), (1,)), ((), ()))


def iota(shape, dim):
    return lax.broadcasted_iota(jnp.int32, shape, dim)


def round_up(value, step):
    return -(-value // step) * step


def dot(a, b):
    return jnp.dot(a, b, preferred_element_type=F32)


def dot_nt(a, b):
    return lax.dot_general(a, b, NT, preferred_element_type=F32)


def vmem_specs(count):
    return [pl.BlockSpec(memory_space=VMEM)] * count


def smem_spec():
    return pl.BlockSpec(memory_space=pltpu.SMEM)


def loop(count, body, carry):
    return lax.fori_loop(0, count, body, carry, unroll=count <= 4)


def call(kernel, out_shape, in_specs, scratch, cost, room, *args):
    single = not isinstance(out_shape, (tuple, list))
    return pl.pallas_call(
        kernel,
        out_shape=out_shape,
        in_specs=in_specs,
        out_specs=vmem_specs(1)[0] if single else vmem_specs(len(out_shape)),
        scratch_shapes=scratch,
        compiler_params=pltpu.CompilerParams(vmem_limit_bytes=room * 1024 * 1024),
        cost_estimate=pl.CostEstimate(flops=cost[0], bytes_accessed=cost[1], transcendentals=cost[2]),
    )(*args)


def pack_kernel(dests, cap, pixels, own, half_wide, count_ref, target_ref, flow_ref, hidden_ref, context_ref, out_ref, wide):
    slots = hidden_ref.shape[0]
    target = jnp.concatenate([target_ref[k : k + 1, :] for k in range(slots // 128)], axis=1)
    counted = iota((1, slots), 1) < count_ref[0]
    owner = target // pixels
    within = target % pixels
    belongs = (iota((dests, slots), 0) == owner) & counted
    member = jnp.where(belongs, 1.0, 0.0)
    upper = jnp.where(iota((128, 128), 0) <= iota((128, 128), 1), 1.0, 0.0).astype(BF16)
    before = jnp.zeros((dests, 1), F32)
    ranks = []
    for start in range(0, slots, 128):
        running = dot(member[:, start : start + 128].astype(BF16), upper) + before
        before = running[:, 127:128]
        ranks.append(running)
    rank = jnp.concatenate(ranks, axis=1) - 1.0 - (lax.axis_index("loop") * cap).astype(F32)
    belongs = belongs & (rank >= 0.0) & (rank < cap)
    place_at = jnp.sum(
        jnp.where(belongs, rank + iota((dests, slots), 0).astype(F32) * cap, 0.0), axis=0, keepdims=True
    )
    taken = jnp.max(jnp.where(belongs, 1.0, 0.0), axis=0, keepdims=True)
    landing = jnp.where(taken > 0.5, place_at, -1.0).astype(jnp.int32)
    row = iota((8, slots), 0)
    flow = flow_ref[...].astype(F32)
    side = jnp.where(row == 0, flow[0:1], 0.0)
    side = jnp.where(row == 1, flow[1:2], side)
    side = jnp.where(row == 2, (within // 256).astype(F32), side)
    side = jnp.where(row == 3, (within % 256).astype(F32), side)
    side = jnp.where(row == 4, 1.0, side).astype(BF16)
    hidden = hidden_ref[...]
    rows_hidden = round_up(cap, 16)
    together = max(1, min(dests, 192 // cap))
    for first in range(0, dests, together):
        spots = together * cap
        chosen = jnp.where(iota((spots, slots), 0) + first * cap == landing, 1.0, 0.0).astype(BF16)
        moved = dot(chosen, hidden)
        moved_side = dot_nt(side, chosen)
        for k in range(together):
            out_ref[first + k, 0:cap, :] = moved[k * cap : (k + 1) * cap].astype(BF16)
            for t in range(-(-cap // 128)):
                width = min(128, cap - t * 128)
                piece = moved_side[:, k * cap + t * 128 : k * cap + t * 128 + width]
                if width < 128:
                    piece = jnp.concatenate([piece, jnp.zeros((8, 128 - width), F32)], axis=1)
                base = rows_hidden + 8 * t
                out_ref[first + k, base : base + 8, :] = piece.astype(BF16)
    rows_per, width, _ = context_ref.shape
    top = out_ref.shape[1] - rows_per * WIN
    start = pl.multiple_of(lax.axis_index("loop") * (width // 2), 128)
    wide[...] = jnp.zeros_like(wide)
    for r in range(rows_per):
        wide[r, HALO : HALO + width, :] = context_ref[r].astype(F32)
        part = wide[r, pl.ds(start, half_wide), :]
        for j in range(dests):
            out_ref[j, top + r * WIN : top + (r + 1) * WIN, :] = part[j * own : j * own + WIN].astype(BF16)


def place_kernel(cap, half_wide, rows_per, first_ref, second_ref, ow_ref, hidden_ref, flow_ref, term_ref, wide_hidden, wide_term):
    half = lax.axis_index("loop")
    dests = first_ref.shape[0]
    pixels = flow_ref.shape[1]
    width = pixels // rows_per
    rows_hidden = round_up(cap, 16)
    hidden = jnp.zeros((pixels, 128), F32)
    flow = jnp.zeros((8, pixels), F32)
    for j, got_ref in [(j, ref) for j in range(dests) for ref in (first_ref, second_ref)]:
        pieces = []
        for t in range(-(-cap // 128)):
            base = rows_hidden + 8 * t
            pieces.append(got_ref[j, base : base + 8, 0 : min(128, cap - t * 128)].astype(F32))
        side = pieces[0] if len(pieces) == 1 else jnp.concatenate(pieces, axis=1)
        place = jnp.where(side[4:5] > 0.5, side[2:3] * 256.0 + side[3:4], -1.0).astype(jnp.int32)
        chosen = jnp.where(iota((pixels, cap), 0) == place, 1.0, 0.0).astype(BF16)
        hidden = hidden + dot(chosen, got_ref[j, 0:cap, :])
        flow = flow + dot_nt(side.astype(BF16), chosen)
    flow_ref[...] = flow
    columns = flow.T
    ow = ow_ref[...]
    term = columns[:, 0:1] * (OFFSET_SCALE * (ow[4:5] - ow[0:1] - ow[2:3])) + columns[:, 1:2] * (
        OFFSET_SCALE * (ow[5:6] - ow[1:2] - ow[3:4])
    )
    start = pl.multiple_of(half * (width // 2), 128)
    for wide, value, out in ((wide_hidden, hidden, hidden_ref), (wide_term, term, term_ref)):
        wide[...] = jnp.zeros_like(wide)
        for r in range(rows_per):
            wide[r, HALO : HALO + width, :] = value[r * width : (r + 1) * width]
            out[r] = wide[r, pl.ds(start, half_wide), :].astype(out.dtype)


def match_kernel(
    count, flip, half_wide, rows_per, queries_ref, weight_ref, ow_ref, *refs
):
    key_refs, (keep_ref, send_ref, fine, coarse, scores, mixed, wide) = refs[:count], refs[count:]
    me, half = lax.axis_index("rows"), lax.axis_index("loop")
    pixels, channels = queries_ref.shape
    width = pixels // rows_per
    columns = width // 2
    quarter = columns // 2
    chunks = fine.shape[0]
    shards = chunks * 2
    per_ref = shards // count
    spread = jnp.where(
        iota((columns, columns), 1)
        == jnp.where(iota((columns, columns), 0) < quarter, 2 * iota((columns, columns), 0), 2 * (iota((columns, columns), 0) - quarter) + 1),
        1.0,
        0.0,
    ).astype(BF16)

    def sort_shard(ref, m, shard, lane):
        even, odd = [], []
        for r in range(rows_per):
            parted = dot(spread, ref[m, r])
            even.append(parted[:quarter])
            odd.append(parted[quarter:])
            for p, part in ((0, even[-1]), (1, odd[-1])):
                g = 2 * r + p
                fine[shard, g * 2 * quarter + lane * quarter : g * 2 * quarter + (lane + 1) * quarter, :] = part.astype(BF16)
        pooled = (even[0] + odd[0] + even[1] + odd[1]) * 0.25
        coarse[shard, lane * quarter : (lane + 1) * quarter, :] = pooled.astype(BF16)

    if per_ref == 1:
        for m in range(shards):
            sort_shard(key_refs[m], 0, m // 2, m % 2)
    else:
        def sort_chunk(c, carry):
            for lane in range(2):
                sort_shard(key_refs[0], c * 2 + lane, c, lane)
            return carry

        lax.fori_loop(0, chunks, sort_chunk, 0)

    group = 2 * quarter
    tile = scores.shape[1]
    lane = iota((1, group), 1)
    lane_col = ((lane % quarter) * 2 + half * columns).astype(F32)
    ow = ow_ref[...] * OFFSET_SCALE
    weight = weight_ref[...]

    def lane_row(c):
        arrival = c * 2 + lane // quarter
        shard = lax.bitwise_xor(arrival, me) if flip else arrival
        return (shard * rows_per).astype(F32)

    wide[...] = jnp.zeros_like(wide)

    def one_tile(t, carry):
        first = pl.multiple_of(t * tile, tile)
        queries = queries_ref[pl.ds(first, tile), :] * jnp.asarray(1.0 / math.sqrt(channels), BF16)

        def score(c, peaks):
            values = dot_nt(queries, fine[c])
            scores[c] = values
            parts = [values[:, g * group : (g + 1) * group] for g in range(4)]
            blended = (parts[0] + parts[1] + parts[2] + parts[3]) * 0.25
            high = jnp.maximum(jnp.maximum(parts[0], parts[1]), jnp.maximum(parts[2], parts[3]))
            return jnp.maximum(peaks[0], high), jnp.maximum(peaks[1], blended)

        low = jnp.full((tile, group), -jnp.inf, F32)
        peaks = loop(chunks, score, (low, low))
        peak_fine = jnp.max(peaks[0], axis=1, keepdims=True)
        peak_coarse = jnp.max(peaks[1], axis=1, keepdims=True)

        def absorb(c, so_far):
            total, below, right, rows, c_total, c_rows, acc_fine, acc_coarse = so_far
            parts = [scores[c, :, g * group : (g + 1) * group] for g in range(4)]
            blended = (parts[0] + parts[1] + parts[2] + parts[3]) * 0.25
            expo = [jnp.exp(part - peak_fine) for part in parts]
            c_expo = jnp.exp(blended - peak_coarse)
            lower = expo[2] + expo[3]
            everything = expo[0] + expo[1] + lower
            at = lane_row(c)
            weights = jnp.concatenate([e.astype(BF16) for e in expo], axis=1)
            return (
                total + everything,
                below + lower,
                right + (expo[1] + expo[3]),
                rows + everything * at,
                c_total + c_expo,
                c_rows + c_expo * at,
                acc_fine + dot(weights, fine[c]),
                acc_coarse + dot(c_expo.astype(BF16), coarse[c]),
            )

        zero = jnp.zeros((tile, group), F32)
        blank = jnp.zeros((tile, channels), F32)
        total, below, right, rows, c_total, c_rows, acc_fine, acc_coarse = loop(
            chunks, absorb, (zero, zero, zero, zero, zero, zero, blank, blank)
        )

        def over(value):
            return jnp.sum(value, axis=1, keepdims=True)

        pixel = first + iota((tile, 1), 0)
        own_row = (me * rows_per + pixel // width).astype(F32)
        own_col = (pixel % width).astype(F32)
        fine_sum, coarse_sum = over(total), over(c_total)
        fine_row = over(rows + below) / fine_sum - own_row
        fine_col = over(total * lane_col + right) / fine_sum - own_col
        coarse_row = over(c_rows) / coarse_sum + 0.5 - own_row
        coarse_col = over(c_total * lane_col) / coarse_sum + 0.5 - own_col
        fine_out = dot((acc_fine / fine_sum).astype(BF16), weight[:channels])
        coarse_out = dot((acc_coarse / coarse_sum).astype(BF16), weight[channels:])
        mixed[pl.ds(first, tile), 0:128] = fine_out + fine_row * ow[0:1] + fine_col * ow[1:2]
        mixed[pl.ds(first, tile), 128:256] = coarse_out + coarse_row * ow[2:3] + coarse_col * ow[3:4]
        mixed[pl.ds(first, tile), 256:384] = jnp.where(
            iota((tile, 128), 1) < 64,
            peak_fine + jnp.log(fine_sum),
            peak_coarse + jnp.log(coarse_sum),
        )
        return carry

    lax.fori_loop(0, pixels // tile, one_tile, 0)
    start = pl.multiple_of(half * columns, 128)
    other = pl.multiple_of((1 - half) * columns, 128)
    for r in range(rows_per):
        wide[r, HALO : HALO + width, :] = mixed[r * width : (r + 1) * width, :]
        keep_ref[r] = wide[r, pl.ds(start, half_wide), :]
        send_ref[r] = wide[r, pl.ds(other, half_wide), :]


def merge_kernel(own, keep_ref, got_ref, term_ref, hidden_ref, out_ref):
    dests = out_ref.shape[0]
    for r in range(keep_ref.shape[0]):
        keep, got = keep_ref[r], got_ref[r]
        gap = got[:, 256:384] - keep[:, 256:384]
        share = 1.0 / (1.0 + jnp.exp(gap))
        share_fine, share_coarse = share[:, 0:1], share[:, 64:65]
        base = (
            got[:, 0:128]
            + (keep[:, 0:128] - got[:, 0:128]) * share_fine
            + got[:, 128:256]
            + (keep[:, 128:256] - got[:, 128:256]) * share_coarse
            + term_ref[r]
        )
        hidden = hidden_ref[r].astype(F32)
        for j in range(dests):
            out_ref[j, r * WIN : (r + 1) * WIN, 0:128] = base[j * own : j * own + WIN].astype(BF16)
            out_ref[j, r * WIN : (r + 1) * WIN, 128:256] = hidden[j * own : j * own + WIN].astype(BF16)


def sigmoid(x):
    return 0.5 * jnp.tanh(0.5 * x) + 0.5


def shifted(value, tap):
    return value if tap == 2 else pltpu.roll(value, (2 - tap) % TILE, 0)


def each_tile(count, body):
    def step(t, carry):
        body(pl.multiple_of(t * TILE, TILE))
        return carry

    lax.fori_loop(0, count // TILE, step, 0, unroll=count == TILE)


def fetch(copies, sems, first=0):
    handles = []
    for k, (source, target) in enumerate(copies):
        handles.append(pltpu.make_async_copy(source, target, sems.at[first + k]))
        handles[-1].start()
    return handles


def context_kernel(early_ref, gate_hbm, state_hbm, bias_ref, fixed_ref, gate_ref, state_ref, padded, taps, sems):
    handles = fetch(
        [
            (gate_hbm.at[:, :, pl.ds(128, 128), :], gate_ref),
            (state_hbm.at[:, :, pl.ds(128, 128), :], state_ref),
        ],
        sems,
    )
    dests = early_ref.shape[0]
    count = fixed_ref.shape[1]
    per_dest = count // dests
    first = early_ref.shape[1] - per_dest
    pad = 2 * WIN
    padded[0:pad, :] = jnp.zeros((pad, 128), BF16)
    padded[pad + count : pad + count + pad, :] = jnp.zeros((pad, 128), BF16)
    for j in range(dests):
        padded[pad + j * per_dest : pad + (j + 1) * per_dest, :] = early_ref[j, first : first + per_dest, :]
    for handle in handles:
        handle.wait()
    for p in range(2):

        def one(at):
            for tap in range(5):
                if p == 0:
                    value = shifted(padded[pl.ds(pad + at, TILE), :].astype(F32), tap).astype(BF16)
                else:
                    value = padded[pl.ds(at + tap * WIN, TILE), :]
                taps[:, tap * 128 : (tap + 1) * 128] = value
            gate = gate_ref[p].reshape(640, 256)
            state = state_ref[p].reshape(640, 128)
            fixed_ref[p, pl.ds(at, TILE), 0:256] = dot(taps[...], gate) + bias_ref[p : p + 1, 0:256]
            fixed_ref[p, pl.ds(at, TILE), 256:384] = dot(taps[...], state) + bias_ref[p : p + 1, 256:384]

        each_tile(count, one)


def update_kernel(
    own, width, got_ref, fixed_ref, ow_ref, gate_hbm, state_hbm, head_ref, delta_ref,
    out_ref, base, hidden, motions, states, resets, updates, taps, flow, flow_cols, gate_ref, state_ref,
    slim_taps, slim_states, slim_motions, slim_resets, slim_hidden, sems,
):
    handles = []
    for p in range(2):
        for source, target in ((gate_hbm, gate_ref), (state_hbm, state_ref)):
            parts = [
                (source.at[p, :, pl.ds(256 * k, 128), :], target.at[p, :, pl.ds(128 * k, 128), :]) for k in range(2)
            ]
            handles.append(fetch(parts, sems, 2 * len(handles)))

    def ready(k):
        for handle in handles[k]:
            handle.wait()

    me, half = lax.axis_index("rows"), lax.axis_index("loop")
    dests, per_dest, _ = got_ref.shape
    rows_per = per_dest // WIN
    count = dests * per_dest
    pad = 2 * WIN
    first_col = (half * dests + me) * own - HALO
    column = first_col + iota((TILE, 128), 0) % WIN
    inside = (column >= 0) & (column < width)
    mask = jnp.where(inside, 1.0, 0.0)
    ow = ow_ref[...]
    add_row = OFFSET_SCALE * (ow[4:5] - ow[0:1] - ow[2:3])
    add_col = OFFSET_SCALE * (ow[5:6] - ow[1:2] - ow[3:4])

    for ref in (motions, states, resets):
        ref[0:pad, :] = jnp.zeros((pad, 128), BF16)
        ref[pad + count : pad + count + pad, :] = jnp.zeros((pad, 128), BF16)
    slim_pad = 2 * SLIM
    for ref in (slim_motions, slim_states, slim_resets):
        ref[0:slim_pad, :] = jnp.zeros((slim_pad, 128), BF16)
        ref[slim_pad + count // 2 :, :] = jnp.zeros((slim_pad, 128), BF16)
    for j in range(dests):
        at = j * per_dest
        base[at : at + per_dest, :] = got_ref[j, :, 0:128]
        hidden[at : at + per_dest, :] = got_ref[j, :, 128:256].astype(F32)

    def finish(at, update, candidate):
        old = hidden[pl.ds(at, TILE), :]
        new = (old + update * (candidate - old)) * mask
        hidden[pl.ds(at, TILE), :] = new
        return new

    def slim(value):
        cube = value.reshape(TILE // WIN, WIN, value.shape[1])
        return cube[:, HALO : HALO + SLIM, :].reshape(SLIM_TILE, value.shape[1])

    for iteration in range(ITERS):
        last = iteration == ITERS - 1

        def columns_pass(at):
            motion = base[pl.ds(at, TILE), :].astype(F32)
            if iteration > 0:
                moved = flow_cols[pl.ds(at, TILE), :]
                motion = (motion + moved[:, 0:1] * add_row + moved[:, 1:2] * add_col) * mask
            motion = jnp.maximum(motion, 0.0)
            rounded = motion.astype(BF16)
            if not last:
                motions[pl.ds(pad + at, TILE), :] = rounded
            motion = rounded.astype(F32)
            state = hidden[pl.ds(at, TILE), :].astype(BF16).astype(F32)
            for tap in range(5):
                taps[:, tap * 256 : tap * 256 + 128] = shifted(state, tap).astype(BF16)
                taps[:, tap * 256 + 128 : tap * 256 + 256] = shifted(motion, tap).astype(BF16)
            if iteration == 0 and count == TILE:
                ready(0)
            gates = sigmoid(dot(taps[...], gate_ref[0].reshape(1280, 256)) + fixed_ref[0, pl.ds(at, TILE), 0:256])
            reset = (gates[:, 128:256] * state).astype(BF16).astype(F32)
            if last:
                to = pl.multiple_of(at // 2, SLIM_TILE)
                for tap in range(5):
                    slim_taps[:, tap * 256 : tap * 256 + 128] = slim(shifted(reset, tap)).astype(BF16)
                    slim_taps[:, tap * 256 + 128 : tap * 256 + 256] = slim(shifted(motion, tap)).astype(BF16)
                candidate = jnp.tanh(
                    dot(slim_taps[...], state_ref[0].reshape(1280, 128)) + slim(fixed_ref[0, pl.ds(at, TILE), 256:384])
                )
                old = slim(hidden[pl.ds(at, TILE), :])
                new = old + slim(gates[:, 0:128]) * (candidate - old)
                slim_hidden[pl.ds(to, SLIM_TILE), :] = new
                slim_states[pl.ds(slim_pad + to, SLIM_TILE), :] = new.astype(BF16)
                slim_motions[pl.ds(slim_pad + to, SLIM_TILE), :] = slim(motion).astype(BF16)
                return
            for tap in range(5):
                taps[:, tap * 256 : tap * 256 + 128] = shifted(reset, tap).astype(BF16)
            if iteration == 0 and count == TILE:
                ready(1)
            candidate = jnp.tanh(dot(taps[...], state_ref[0].reshape(1280, 128)) + fixed_ref[0, pl.ds(at, TILE), 256:384])
            states[pl.ds(pad + at, TILE), :] = finish(at, gates[:, 0:128], candidate).astype(BF16)

        def fill(out, first, second, at, stride, size):
            for tap in range(5):
                out[:, tap * 256 : tap * 256 + 128] = first[pl.ds(at + tap * stride, size), :]
                out[:, tap * 256 + 128 : tap * 256 + 256] = second[pl.ds(at + tap * stride, size), :]

        def gate_rows(at):
            fill(taps, states, motions, at, WIN, TILE)
            gates = sigmoid(dot(taps[...], gate_ref[1].reshape(1280, 256)) + fixed_ref[1, pl.ds(at, TILE), 0:256])
            updates[pl.ds(at, TILE), :] = gates[:, 0:128]
            resets[pl.ds(pad + at, TILE), :] = (
                gates[:, 128:256] * states[pl.ds(pad + at, TILE), :].astype(F32)
            ).astype(BF16)

        def head(new):
            lifted = jnp.maximum(dot(new.astype(BF16), head_ref[...]), 0.0).astype(BF16)
            return dot_nt(delta_ref[...], lifted)

        def state_rows(at):
            fill(taps, resets, motions, at, WIN, TILE)
            candidate = jnp.tanh(
                dot(taps[...], state_ref[1].reshape(1280, 128)) + fixed_ref[1, pl.ds(at, TILE), 256:384]
            )
            new = finish(at, updates[pl.ds(at, TILE), :], candidate)
            flow_cols[pl.ds(at, TILE), :] = head(new).T

        def slim_gate_rows(at):
            to = pl.multiple_of(at // 2, SLIM_TILE)
            fill(slim_taps, slim_states, slim_motions, to, SLIM, SLIM_TILE)
            gates = sigmoid(
                dot(slim_taps[...], gate_ref[1].reshape(1280, 256)) + slim(fixed_ref[1, pl.ds(at, TILE), 0:256])
            )
            updates[pl.ds(to, SLIM_TILE), :] = gates[:, 0:128]
            slim_resets[pl.ds(slim_pad + to, SLIM_TILE), :] = (
                gates[:, 128:256] * slim_states[pl.ds(slim_pad + to, SLIM_TILE), :].astype(F32)
            ).astype(BF16)

        def slim_state_rows(at):
            to = pl.multiple_of(at // 2, SLIM_TILE)
            fill(slim_taps, slim_resets, slim_motions, to, SLIM, SLIM_TILE)
            candidate = jnp.tanh(
                dot(slim_taps[...], state_ref[1].reshape(1280, 128)) + slim(fixed_ref[1, pl.ds(at, TILE), 256:384])
            )
            old = slim_hidden[pl.ds(to, SLIM_TILE), :]
            new = old + updates[pl.ds(to, SLIM_TILE), :] * (candidate - old)
            slim_hidden[pl.ds(to, SLIM_TILE), :] = new
            flow[:, pl.ds(to, SLIM_TILE)] = head(new) + slim(flow_cols[pl.ds(at, TILE), :]).T

        if iteration == 0 and count != TILE:
            ready(0)
            ready(1)
        each_tile(count, columns_pass)
        if iteration == 0:
            ready(2)
            ready(3)
            each_tile(count, gate_rows)
            each_tile(count, state_rows)
        else:
            each_tile(count, slim_gate_rows)
            each_tile(count, slim_state_rows)

    for j in range(dests):
        for r in range(rows_per):
            at = j * rows_per * SLIM + r * SLIM
            out_ref[j, r * own : (r + 1) * own, :] = slim_hidden[at : at + own, :]
        moved = flow[:, j * rows_per * SLIM : (j + 1) * rows_per * SLIM]
        out_ref[j, rows_per * own : rows_per * own + 8, :] = jnp.concatenate(
            [moved, jnp.zeros((8, 128 - rows_per * SLIM), F32)], axis=1
        )


def finish_kernel(own, mine_ref, other_ref, first_ref, hidden_ref, flow_ref):
    half = lax.axis_index("loop")
    rows_per, width, _ = hidden_ref.shape
    columns = width // 2
    dests = mine_ref.shape[0]
    for ref, side in ((mine_ref, half), (other_ref, 1 - half)):
        start = pl.multiple_of(side * columns, 128)
        for r in range(rows_per):
            cells = [ref[j, r * own : (r + 1) * own, :] for j in range(dests)]
            hidden_ref[r, pl.ds(start, columns), :] = jnp.concatenate(cells, axis=0)
            moved = jnp.concatenate(
                [ref[j, rows_per * own : rows_per * own + 8, r * SLIM : r * SLIM + own] for j in range(dests)], axis=1
            )
            at = pl.multiple_of(r * width + side * columns, 128)
            total = first_ref[:, pl.ds(at, columns)] + moved
            for k in range(2):
                flow_ref[k, r : r + 1, pl.ds(start, columns)] = total[k : k + 1]


def local(
    frame_one,
    frame_two,
    context,
    carry_hidden,
    carry_flow,
    slot_target,
    slot_count,
    match_weight,
    offset_weight,
    gate_weight,
    state_weight,
    gru_bias,
    head_weight,
    delta_weight,
):
    dests = lax.axis_size("rows")
    halves = lax.axis_size("loop")
    rows_per, width, channels = frame_one.shape
    columns = frame_two.shape[1]
    pixels = rows_per * width
    slots, hidden_size = carry_hidden.shape
    cap = -(-slots // (dests * halves))
    own = columns // dests
    half_wide = round_up(columns - own + WIN, 8)
    padded = columns + half_wide
    room = 16 if dests <= 8 else 56

    rows_hidden = round_up(cap, 16)
    rows_slot = rows_hidden + round_up(8 * (-(-cap // 128)), 16)
    shard = frame_two.reshape(1, rows_per, columns, channels)
    if dests == 8:

        def swap(value, flip):
            return lax.ppermute(value, "rows", [(i, i ^ flip) for i in range(dests)])

        beside, near, wrap, across = (swap(shard, flip) for flip in (1, 2, 6, 4))
        near_beside, wrap_beside = (swap(beside, flip) for flip in (2, 6))
    else:
        beside = lax.all_gather(shard, "rows", axis=0, tiled=True)
    slot_target, beside = lax.optimization_barrier((slot_target, beside))
    packed = call(
        functools.partial(pack_kernel, dests, cap, pixels, own, half_wide),
        jax.ShapeDtypeStruct((dests, rows_slot + rows_per * WIN, hidden_size), BF16),
        [smem_spec()] + vmem_specs(4),
        [pltpu.VMEM((rows_per, padded, 128), F32)],
        (2 * slots * slots * 128, 1 << 20, 0),
        60,
        slot_count,
        slot_target.reshape(slots // 128, 128),
        carry_flow.T,
        carry_hidden,
        context,
    )
    if dests == 8:
        packed, across = lax.optimization_barrier((packed, across))
        across_beside = swap(across, 1)
        packed, near, wrap, near_beside, wrap_beside, across_beside = lax.optimization_barrier(
            (packed, near, wrap, near_beside, wrap_beside, across_beside)
        )
        keys = (shard, beside, near, near_beside, across, across_beside, wrap, wrap_beside)
    else:
        keys = (beside,)
    early = lax.all_to_all(packed, "rows", 0, 0, tiled=True)
    around = [(i, (i + 1) % halves) for i in range(halves)]
    early_other = lax.ppermute(early, "loop", around)
    ow = jnp.pad(offset_weight, ((0, 2), (0, 0)))
    hidden_wide, flow_first, term = call(
        functools.partial(place_kernel, cap, half_wide, rows_per),
        (
            jax.ShapeDtypeStruct((rows_per, half_wide, 128), BF16),
            jax.ShapeDtypeStruct((8, pixels), F32),
            jax.ShapeDtypeStruct((rows_per, half_wide, 128), F32),
        ),
        vmem_specs(3),
        [pltpu.VMEM((rows_per, padded, 128), F32)] * 2,
        (2 * slots * pixels * 128, 1 << 20, 0),
        room,
        early,
        early_other,
        ow,
    )
    queries = frame_one.reshape(pixels, channels)
    chunks = dests // 2
    tile = 128
    keep, send = call(
        functools.partial(match_kernel, len(keys), len(keys) > 1, half_wide, rows_per),
        (jax.ShapeDtypeStruct((rows_per, half_wide, 384), F32),) * 2,
        vmem_specs(3 + len(keys)),
        [
            pltpu.VMEM((chunks, 4 * columns, channels), BF16),
            pltpu.VMEM((chunks, columns, channels), BF16),
            pltpu.VMEM((chunks, tile, 4 * columns), F32),
            pltpu.VMEM((pixels, 384), F32),
            pltpu.VMEM((rows_per, padded, 384), F32),
        ],
        (4 * pixels * chunks * 4 * columns * channels, 1 << 21, pixels * chunks * 5 * columns),
        room,
        queries,
        match_weight,
        ow,
        *keys,
    )
    other = lax.ppermute(send, "loop", around)
    sending = call(
        functools.partial(merge_kernel, own),
        jax.ShapeDtypeStruct((dests, rows_per * WIN, 256), BF16),
        vmem_specs(4),
        [],
        (0, 1 << 20, 0),
        room,
        keep,
        other,
        term,
        hidden_wide,
    )
    arrived = lax.all_to_all(sending, "rows", 0, 0, tiled=True)
    count = dests * rows_per * WIN
    back_rows = rows_per * own + 8
    hbm = pl.BlockSpec(memory_space=pltpu.HBM)
    gate_weight = pltpu.with_memory_space_constraint(gate_weight, pltpu.HBM)
    state_weight = pltpu.with_memory_space_constraint(state_weight, pltpu.HBM)
    fixed = call(
        context_kernel,
        jax.ShapeDtypeStruct((2, count, 384), F32),
        [vmem_specs(1)[0], hbm, hbm, vmem_specs(1)[0]],
        [
            pltpu.VMEM((2, 5, 128, 256), BF16),
            pltpu.VMEM((2, 5, 128, 128), BF16),
            pltpu.VMEM((count + 4 * WIN, 128), BF16),
            pltpu.VMEM((TILE, 640), BF16),
            pltpu.SemaphoreType.DMA((2,)),
        ],
        (4 * count * 5 * 128 * 384, 1 << 22, 0),
        room,
        early,
        gate_weight,
        state_weight,
        gru_bias,
    )
    outgoing = call(
        functools.partial(update_kernel, own, width),
        jax.ShapeDtypeStruct((dests, back_rows, 128), F32),
        vmem_specs(3) + [hbm, hbm] + vmem_specs(2),
        [
            pltpu.VMEM((count, 128), BF16),
            pltpu.VMEM((count, 128), F32),
            pltpu.VMEM((count + 4 * WIN, 128), BF16),
            pltpu.VMEM((count + 4 * WIN, 128), BF16),
            pltpu.VMEM((count + 4 * WIN, 128), BF16),
            pltpu.VMEM((count, 128), F32),
            pltpu.VMEM((TILE, 1280), BF16),
            pltpu.VMEM((8, count // 2), F32),
            pltpu.VMEM((count, 8), F32),
            pltpu.VMEM((2, 5, 256, 256), BF16),
            pltpu.VMEM((2, 5, 256, 128), BF16),
            pltpu.VMEM((SLIM_TILE, 1280), BF16),
            pltpu.VMEM((count // 2 + 4 * SLIM, 128), BF16),
            pltpu.VMEM((count // 2 + 4 * SLIM, 128), BF16),
            pltpu.VMEM((count // 2 + 4 * SLIM, 128), BF16),
            pltpu.VMEM((count // 2, 128), F32),
            pltpu.SemaphoreType.DMA((8,)),
        ],
        (8 * count * 5 * 256 * 384, 1 << 22, 8 * count * 384),
        room,
        arrived,
        fixed,
        ow,
        gate_weight,
        state_weight,
        head_weight,
        jnp.pad(delta_weight, ((0, 6), (0, 0))),
    )
    back = lax.all_to_all(outgoing, "rows", 0, 0, tiled=True)
    hidden_out, flow_out = call(
        functools.partial(finish_kernel, own),
        (
            jax.ShapeDtypeStruct((rows_per, width, hidden_size), F32),
            jax.ShapeDtypeStruct((2, rows_per, width), F32),
        ),
        vmem_specs(3),
        [],
        (0, 1 << 20, 0),
        room,
        back,
        lax.ppermute(back, "loop", around),
        flow_first,
    )
    return (hidden_out, flow_out)


def solution(mesh):
    return jax.shard_map(
        local,
        mesh=mesh,
        in_specs=(
            P(("groups", "rows"), None, None),
            P(("groups", "rows"), "loop", None),
            P(("groups", "rows"), None, None),
            P(("groups", "rows"), None),
            P(("groups", "rows"), None),
            P(("groups", "rows")),
            P(("groups", "rows")),
            P(),
            P(),
            P(),
            P(),
            P(),
            P(),
            P(),
        ),
        out_specs=(P(("groups", "rows"), None, None), P(None, ("groups", "rows"), None)),
        check_vma=False,
    )
```

```python
import functools
import math

import jax
import jax.numpy as jnp
from jax import lax
from jax.experimental import pallas as pl
from jax.experimental.pallas import tpu as pltpu
from jax.sharding import PartitionSpec as P

ITERS = 2
WIN = 32
SLIM = 16
HALO = 8
TILE = 512
SLIM_TILE = TILE * SLIM // WIN
OFFSET_SCALE = 0.03125
F32 = jnp.float32
BF16 = jnp.bfloat16
VMEM = pltpu.VMEM
NT = (((1,), (1,)), ((), ()))


def iota(shape, dim):
    return lax.broadcasted_iota(jnp.int32, shape, dim)


def round_up(value, step):
    return -(-value // step) * step


def dot(a, b):
    return jnp.dot(a, b, preferred_element_type=F32)


def dot_nt(a, b):
    return lax.dot_general(a, b, NT, preferred_element_type=F32)


def vmem_specs(count):
    return [pl.BlockSpec(memory_space=VMEM)] * count


def smem_spec():
    return pl.BlockSpec(memory_space=pltpu.SMEM)


def loop(count, body, carry):
    return lax.fori_loop(0, count, body, carry, unroll=count <= 4)


def call(kernel, out_shape, in_specs, scratch, cost, room, *args):
    single = not isinstance(out_shape, (tuple, list))
    return pl.pallas_call(
        kernel,
        out_shape=out_shape,
        in_specs=in_specs,
        out_specs=vmem_specs(1)[0] if single else vmem_specs(len(out_shape)),
        scratch_shapes=scratch,
        compiler_params=pltpu.CompilerParams(vmem_limit_bytes=room * 1024 * 1024),
        cost_estimate=pl.CostEstimate(flops=cost[0], bytes_accessed=cost[1], transcendentals=cost[2]),
    )(*args)


def pack_kernel(dests, cap, pixels, own, half_wide, count_ref, target_ref, flow_ref, hidden_ref, context_ref, out_ref, wide):
    slots = hidden_ref.shape[0]
    target = jnp.concatenate([target_ref[k : k + 1, :] for k in range(slots // 128)], axis=1)
    counted = iota((1, slots), 1) < count_ref[0]
    owner = target // pixels
    within = target % pixels
    belongs = (iota((dests, slots), 0) == owner) & counted
    member = jnp.where(belongs, 1.0, 0.0)
    upper = jnp.where(iota((128, 128), 0) <= iota((128, 128), 1), 1.0, 0.0).astype(BF16)
    before = jnp.zeros((dests, 1), F32)
    ranks = []
    for start in range(0, slots, 128):
        running = dot(member[:, start : start + 128].astype(BF16), upper) + before
        before = running[:, 127:128]
        ranks.append(running)
    rank = jnp.concatenate(ranks, axis=1) - 1.0 - (lax.axis_index("loop") * cap).astype(F32)
    belongs = belongs & (rank >= 0.0) & (rank < cap)
    place_at = jnp.sum(
        jnp.where(belongs, rank + iota((dests, slots), 0).astype(F32) * cap, 0.0), axis=0, keepdims=True
    )
    taken = jnp.max(jnp.where(belongs, 1.0, 0.0), axis=0, keepdims=True)
    landing = jnp.where(taken > 0.5, place_at, -1.0).astype(jnp.int32)
    row = iota((8, slots), 0)
    flow = flow_ref[...].astype(F32)
    side = jnp.where(row == 0, flow[0:1], 0.0)
    side = jnp.where(row == 1, flow[1:2], side)
    side = jnp.where(row == 2, (within // 256).astype(F32), side)
    side = jnp.where(row == 3, (within % 256).astype(F32), side)
    side = jnp.where(row == 4, 1.0, side).astype(BF16)
    hidden = hidden_ref[...]
    rows_hidden = round_up(cap, 16)
    together = max(1, min(dests, 192 // cap))
    for first in range(0, dests, together):
        spots = together * cap
        chosen = jnp.where(iota((spots, slots), 0) + first * cap == landing, 1.0, 0.0).astype(BF16)
        moved = dot(chosen, hidden)
        moved_side = dot_nt(side, chosen)
        for k in range(together):
            out_ref[first + k, 0:cap, :] = moved[k * cap : (k + 1) * cap].astype(BF16)
            for t in range(-(-cap // 128)):
                width = min(128, cap - t * 128)
                piece = moved_side[:, k * cap + t * 128 : k * cap + t * 128 + width]
                if width < 128:
                    piece = jnp.concatenate([piece, jnp.zeros((8, 128 - width), F32)], axis=1)
                base = rows_hidden + 8 * t
                out_ref[first + k, base : base + 8, :] = piece.astype(BF16)
    rows_per, width, _ = context_ref.shape
    top = out_ref.shape[1] - rows_per * WIN
    start = pl.multiple_of(lax.axis_index("loop") * (width // 2), 128)
    wide[...] = jnp.zeros_like(wide)
    for r in range(rows_per):
        wide[r, HALO : HALO + width, :] = context_ref[r].astype(F32)
        part = wide[r, pl.ds(start, half_wide), :]
        for j in range(dests):
            out_ref[j, top + r * WIN : top + (r + 1) * WIN, :] = part[j * own : j * own + WIN].astype(BF16)


def gather_slots(cap, got_ref, hidden, flow):
    rows_hidden = round_up(cap, 16)
    pixels = flow.shape[1]
    for j in range(got_ref.shape[0]):
        pieces = []
        for t in range(-(-cap // 128)):
            base = rows_hidden + 8 * t
            pieces.append(got_ref[j, base : base + 8, 0 : min(128, cap - t * 128)].astype(F32))
        side = pieces[0] if len(pieces) == 1 else jnp.concatenate(pieces, axis=1)
        place = jnp.where(side[4:5] > 0.5, side[2:3] * 256.0 + side[3:4], -1.0).astype(jnp.int32)
        chosen = jnp.where(iota((pixels, cap), 0) == place, 1.0, 0.0).astype(BF16)
        hidden = hidden + dot(chosen, got_ref[j, 0:cap, :])
        flow = flow + dot_nt(side.astype(BF16), chosen)
    return hidden, flow


def own_slots_kernel(cap, got_ref, hidden_ref, flow_ref):
    zeros = jnp.zeros(hidden_ref.shape, F32), jnp.zeros(flow_ref.shape, F32)
    hidden_ref[...], flow_ref[...] = gather_slots(cap, got_ref, *zeros)


def place_kernel(cap, half_wide, rows_per, got_ref, part_ref, flow_part_ref, ow_ref, hidden_ref, flow_ref, term_ref, wide_hidden, wide_term):
    half = lax.axis_index("loop")
    pixels = flow_ref.shape[1]
    width = pixels // rows_per
    hidden, flow = gather_slots(cap, got_ref, part_ref[...], flow_part_ref[...])
    flow_ref[...] = flow
    columns = flow.T
    ow = ow_ref[...]
    term = columns[:, 0:1] * (OFFSET_SCALE * (ow[4:5] - ow[0:1] - ow[2:3])) + columns[:, 1:2] * (
        OFFSET_SCALE * (ow[5:6] - ow[1:2] - ow[3:4])
    )
    start = pl.multiple_of(half * (width // 2), 128)
    for wide, value, out in ((wide_hidden, hidden, hidden_ref), (wide_term, term, term_ref)):
        wide[...] = jnp.zeros_like(wide)
        for r in range(rows_per):
            wide[r, HALO : HALO + width, :] = value[r * width : (r + 1) * width]
            out[r] = wide[r, pl.ds(start, half_wide), :].astype(out.dtype)


def match_kernel(
    count, flip, half_wide, rows_per, queries_ref, weight_ref, ow_ref, *refs
):
    key_refs, (keep_ref, send_ref, fine, coarse, scores, mixed, wide) = refs[:count], refs[count:]
    me, half = lax.axis_index("rows"), lax.axis_index("loop")
    pixels, channels = queries_ref.shape
    width = pixels // rows_per
    columns = width // 2
    quarter = columns // 2
    chunks = fine.shape[0]
    shards = chunks * 2
    per_ref = shards // count
    spread = jnp.where(
        iota((columns, columns), 1)
        == jnp.where(iota((columns, columns), 0) < quarter, 2 * iota((columns, columns), 0), 2 * (iota((columns, columns), 0) - quarter) + 1),
        1.0,
        0.0,
    ).astype(BF16)

    def sort_shard(ref, m, shard, lane):
        even, odd = [], []
        for r in range(rows_per):
            parted = dot(spread, ref[m, r])
            even.append(parted[:quarter])
            odd.append(parted[quarter:])
            for p, part in ((0, even[-1]), (1, odd[-1])):
                g = 2 * r + p
                fine[shard, g * 2 * quarter + lane * quarter : g * 2 * quarter + (lane + 1) * quarter, :] = part.astype(BF16)
        pooled = (even[0] + odd[0] + even[1] + odd[1]) * 0.25
        coarse[shard, lane * quarter : (lane + 1) * quarter, :] = pooled.astype(BF16)

    if per_ref == 1:
        for m in range(shards):
            sort_shard(key_refs[m], 0, m // 2, m % 2)
    else:
        def sort_chunk(c, carry):
            for lane in range(2):
                sort_shard(key_refs[0], c * 2 + lane, c, lane)
            return carry

        lax.fori_loop(0, chunks, sort_chunk, 0)

    group = 2 * quarter
    tile = scores.shape[1]
    lane = iota((1, group), 1)
    lane_col = ((lane % quarter) * 2 + half * columns).astype(F32)
    ow = ow_ref[...] * OFFSET_SCALE
    weight = weight_ref[...]

    def lane_row(c):
        arrival = c * 2 + lane // quarter
        shard = lax.bitwise_xor(arrival, me) if flip else arrival
        return (shard * rows_per).astype(F32)

    wide[...] = jnp.zeros_like(wide)

    def one_tile(t, carry):
        first = pl.multiple_of(t * tile, tile)
        queries = queries_ref[pl.ds(first, tile), :] * jnp.asarray(1.0 / math.sqrt(channels), BF16)

        def score(c, peaks):
            values = dot_nt(queries, fine[c])
            scores[c] = values
            parts = [values[:, g * group : (g + 1) * group] for g in range(4)]
            blended = (parts[0] + parts[1] + parts[2] + parts[3]) * 0.25
            high = jnp.maximum(jnp.maximum(parts[0], parts[1]), jnp.maximum(parts[2], parts[3]))
            return jnp.maximum(peaks[0], high), jnp.maximum(peaks[1], blended)

        low = jnp.full((tile, group), -jnp.inf, F32)
        peaks = loop(chunks, score, (low, low))
        peak_fine = jnp.max(peaks[0], axis=1, keepdims=True)
        peak_coarse = jnp.max(peaks[1], axis=1, keepdims=True)

        def absorb(c, so_far):
            total, below, right, rows, c_total, c_rows, acc_fine, acc_coarse = so_far
            parts = [scores[c, :, g * group : (g + 1) * group] for g in range(4)]
            blended = (parts[0] + parts[1] + parts[2] + parts[3]) * 0.25
            expo = [jnp.exp(part - peak_fine) for part in parts]
            c_expo = jnp.exp(blended - peak_coarse)
            lower = expo[2] + expo[3]
            everything = expo[0] + expo[1] + lower
            at = lane_row(c)
            weights = jnp.concatenate([e.astype(BF16) for e in expo], axis=1)
            return (
                total + everything,
                below + lower,
                right + (expo[1] + expo[3]),
                rows + everything * at,
                c_total + c_expo,
                c_rows + c_expo * at,
                acc_fine + dot(weights, fine[c]),
                acc_coarse + dot(c_expo.astype(BF16), coarse[c]),
            )

        zero = jnp.zeros((tile, group), F32)
        blank = jnp.zeros((tile, channels), F32)
        total, below, right, rows, c_total, c_rows, acc_fine, acc_coarse = loop(
            chunks, absorb, (zero, zero, zero, zero, zero, zero, blank, blank)
        )

        def over(value):
            return jnp.sum(value, axis=1, keepdims=True)

        pixel = first + iota((tile, 1), 0)
        own_row = (me * rows_per + pixel // width).astype(F32)
        own_col = (pixel % width).astype(F32)
        fine_sum, coarse_sum = over(total), over(c_total)
        fine_row = over(rows + below) / fine_sum - own_row
        fine_col = over(total * lane_col + right) / fine_sum - own_col
        coarse_row = over(c_rows) / coarse_sum + 0.5 - own_row
        coarse_col = over(c_total * lane_col) / coarse_sum + 0.5 - own_col
        fine_out = dot((acc_fine / fine_sum).astype(BF16), weight[:channels])
        coarse_out = dot((acc_coarse / coarse_sum).astype(BF16), weight[channels:])
        mixed[pl.ds(first, tile), 0:128] = fine_out + fine_row * ow[0:1] + fine_col * ow[1:2]
        mixed[pl.ds(first, tile), 128:256] = coarse_out + coarse_row * ow[2:3] + coarse_col * ow[3:4]
        mixed[pl.ds(first, tile), 256:384] = jnp.where(
            iota((tile, 128), 1) < 64,
            peak_fine + jnp.log(fine_sum),
            peak_coarse + jnp.log(coarse_sum),
        )
        return carry

    lax.fori_loop(0, pixels // tile, one_tile, 0)
    start = pl.multiple_of(half * columns, 128)
    other = pl.multiple_of((1 - half) * columns, 128)
    for r in range(rows_per):
        wide[r, HALO : HALO + width, :] = mixed[r * width : (r + 1) * width, :]
        keep_ref[r] = wide[r, pl.ds(start, half_wide), :]
        send_ref[r] = wide[r, pl.ds(other, half_wide), :]


def merge_kernel(own, keep_ref, got_ref, term_ref, hidden_ref, out_ref):
    dests = out_ref.shape[0]
    for r in range(keep_ref.shape[0]):
        keep, got = keep_ref[r], got_ref[r]
        gap = got[:, 256:384] - keep[:, 256:384]
        share = 1.0 / (1.0 + jnp.exp(gap))
        share_fine, share_coarse = share[:, 0:1], share[:, 64:65]
        base = (
            got[:, 0:128]
            + (keep[:, 0:128] - got[:, 0:128]) * share_fine
            + got[:, 128:256]
            + (keep[:, 128:256] - got[:, 128:256]) * share_coarse
            + term_ref[r]
        )
        hidden = hidden_ref[r].astype(F32)
        for j in range(dests):
            out_ref[j, r * WIN : (r + 1) * WIN, 0:128] = base[j * own : j * own + WIN].astype(BF16)
            out_ref[j, r * WIN : (r + 1) * WIN, 128:256] = hidden[j * own : j * own + WIN].astype(BF16)


def sigmoid(x):
    return 0.5 * jnp.tanh(0.5 * x) + 0.5


def shifted(value, tap):
    return value if tap == 2 else pltpu.roll(value, (2 - tap) % TILE, 0)


def each_tile(count, body):
    def step(t, carry):
        body(pl.multiple_of(t * TILE, TILE))
        return carry

    lax.fori_loop(0, count // TILE, step, 0, unroll=count == TILE)


def fetch(copies, sems, first=0):
    handles = []
    for k, (source, target) in enumerate(copies):
        handles.append(pltpu.make_async_copy(source, target, sems.at[first + k]))
        handles[-1].start()
    return handles


def context_kernel(early_ref, gate_hbm, state_hbm, bias_ref, fixed_ref, gate_ref, state_ref, padded, taps, sems):
    handles = fetch(
        [
            (gate_hbm.at[:, :, pl.ds(128, 128), :], gate_ref),
            (state_hbm.at[:, :, pl.ds(128, 128), :], state_ref),
        ],
        sems,
    )
    dests = early_ref.shape[0]
    count = fixed_ref.shape[1]
    per_dest = count // dests
    first = early_ref.shape[1] - per_dest
    pad = 2 * WIN
    padded[0:pad, :] = jnp.zeros((pad, 128), BF16)
    padded[pad + count : pad + count + pad, :] = jnp.zeros((pad, 128), BF16)
    for j in range(dests):
        padded[pad + j * per_dest : pad + (j + 1) * per_dest, :] = early_ref[j, first : first + per_dest, :]
    for handle in handles:
        handle.wait()
    for p in range(2):

        def one(at):
            for tap in range(5):
                if p == 0:
                    value = shifted(padded[pl.ds(pad + at, TILE), :].astype(F32), tap).astype(BF16)
                else:
                    value = padded[pl.ds(at + tap * WIN, TILE), :]
                taps[:, tap * 128 : (tap + 1) * 128] = value
            gate = gate_ref[p].reshape(640, 256)
            state = state_ref[p].reshape(640, 128)
            fixed_ref[p, pl.ds(at, TILE), 0:256] = dot(taps[...], gate) + bias_ref[p : p + 1, 0:256]
            fixed_ref[p, pl.ds(at, TILE), 256:384] = dot(taps[...], state) + bias_ref[p : p + 1, 256:384]

        each_tile(count, one)


def update_kernel(
    own, width, got_ref, fixed_ref, ow_ref, gate_hbm, state_hbm, head_ref, delta_ref,
    out_ref, base, hidden, motions, states, resets, updates, taps, flow, flow_cols, gate_ref, state_ref,
    slim_taps, slim_states, slim_motions, slim_resets, slim_hidden, sems,
):
    handles = []
    for p in range(2):
        for source, target in ((gate_hbm, gate_ref), (state_hbm, state_ref)):
            parts = [
                (source.at[p, :, pl.ds(256 * k, 128), :], target.at[p, :, pl.ds(128 * k, 128), :]) for k in range(2)
            ]
            handles.append(fetch(parts, sems, 2 * len(handles)))

    def ready(k):
        for handle in handles[k]:
            handle.wait()

    me, half = lax.axis_index("rows"), lax.axis_index("loop")
    dests, per_dest, _ = got_ref.shape
    rows_per = per_dest // WIN
    count = dests * per_dest
    pad = 2 * WIN
    first_col = (half * dests + me) * own - HALO
    column = first_col + iota((TILE, 128), 0) % WIN
    inside = (column >= 0) & (column < width)
    mask = jnp.where(inside, 1.0, 0.0)
    ow = ow_ref[...]
    add_row = OFFSET_SCALE * (ow[4:5] - ow[0:1] - ow[2:3])
    add_col = OFFSET_SCALE * (ow[5:6] - ow[1:2] - ow[3:4])

    for ref in (motions, states, resets):
        ref[0:pad, :] = jnp.zeros((pad, 128), BF16)
        ref[pad + count : pad + count + pad, :] = jnp.zeros((pad, 128), BF16)
    slim_pad = 2 * SLIM
    for ref in (slim_motions, slim_states, slim_resets):
        ref[0:slim_pad, :] = jnp.zeros((slim_pad, 128), BF16)
        ref[slim_pad + count // 2 :, :] = jnp.zeros((slim_pad, 128), BF16)
    for j in range(dests):
        at = j * per_dest
        base[at : at + per_dest, :] = got_ref[j, :, 0:128]
        hidden[at : at + per_dest, :] = got_ref[j, :, 128:256].astype(F32)

    def finish(at, update, candidate):
        old = hidden[pl.ds(at, TILE), :]
        new = (old + update * (candidate - old)) * mask
        hidden[pl.ds(at, TILE), :] = new
        return new

    def slim(value):
        cube = value.reshape(TILE // WIN, WIN, value.shape[1])
        return cube[:, HALO : HALO + SLIM, :].reshape(SLIM_TILE, value.shape[1])

    for iteration in range(ITERS):
        last = iteration == ITERS - 1

        def columns_pass(at):
            motion = base[pl.ds(at, TILE), :].astype(F32)
            if iteration > 0:
                moved = flow_cols[pl.ds(at, TILE), :]
                motion = (motion + moved[:, 0:1] * add_row + moved[:, 1:2] * add_col) * mask
            motion = jnp.maximum(motion, 0.0)
            rounded = motion.astype(BF16)
            if not last:
                motions[pl.ds(pad + at, TILE), :] = rounded
            motion = rounded.astype(F32)
            state = hidden[pl.ds(at, TILE), :].astype(BF16).astype(F32)
            for tap in range(5):
                taps[:, tap * 256 : tap * 256 + 128] = shifted(state, tap).astype(BF16)
                taps[:, tap * 256 + 128 : tap * 256 + 256] = shifted(motion, tap).astype(BF16)
            if iteration == 0 and count == TILE:
                ready(0)
            gates = sigmoid(dot(taps[...], gate_ref[0].reshape(1280, 256)) + fixed_ref[0, pl.ds(at, TILE), 0:256])
            reset = (gates[:, 128:256] * state).astype(BF16).astype(F32)
            if last:
                to = pl.multiple_of(at // 2, SLIM_TILE)
                for tap in range(5):
                    slim_taps[:, tap * 256 : tap * 256 + 128] = slim(shifted(reset, tap)).astype(BF16)
                    slim_taps[:, tap * 256 + 128 : tap * 256 + 256] = slim(shifted(motion, tap)).astype(BF16)
                candidate = jnp.tanh(
                    dot(slim_taps[...], state_ref[0].reshape(1280, 128)) + slim(fixed_ref[0, pl.ds(at, TILE), 256:384])
                )
                old = slim(hidden[pl.ds(at, TILE), :])
                new = old + slim(gates[:, 0:128]) * (candidate - old)
                slim_hidden[pl.ds(to, SLIM_TILE), :] = new
                slim_states[pl.ds(slim_pad + to, SLIM_TILE), :] = new.astype(BF16)
                slim_motions[pl.ds(slim_pad + to, SLIM_TILE), :] = slim(motion).astype(BF16)
                return
            for tap in range(5):
                taps[:, tap * 256 : tap * 256 + 128] = shifted(reset, tap).astype(BF16)
            if iteration == 0 and count == TILE:
                ready(1)
            candidate = jnp.tanh(dot(taps[...], state_ref[0].reshape(1280, 128)) + fixed_ref[0, pl.ds(at, TILE), 256:384])
            states[pl.ds(pad + at, TILE), :] = finish(at, gates[:, 0:128], candidate).astype(BF16)

        def fill(out, first, second, at, stride, size):
            for tap in range(5):
                out[:, tap * 256 : tap * 256 + 128] = first[pl.ds(at + tap * stride, size), :]
                out[:, tap * 256 + 128 : tap * 256 + 256] = second[pl.ds(at + tap * stride, size), :]

        def gate_rows(at):
            fill(taps, states, motions, at, WIN, TILE)
            gates = sigmoid(dot(taps[...], gate_ref[1].reshape(1280, 256)) + fixed_ref[1, pl.ds(at, TILE), 0:256])
            updates[pl.ds(at, TILE), :] = gates[:, 0:128]
            resets[pl.ds(pad + at, TILE), :] = (
                gates[:, 128:256] * states[pl.ds(pad + at, TILE), :].astype(F32)
            ).astype(BF16)

        def head(new):
            lifted = jnp.maximum(dot(new.astype(BF16), head_ref[...]), 0.0).astype(BF16)
            return dot_nt(delta_ref[...], lifted)

        def state_rows(at):
            fill(taps, resets, motions, at, WIN, TILE)
            candidate = jnp.tanh(
                dot(taps[...], state_ref[1].reshape(1280, 128)) + fixed_ref[1, pl.ds(at, TILE), 256:384]
            )
            new = finish(at, updates[pl.ds(at, TILE), :], candidate)
            flow_cols[pl.ds(at, TILE), :] = head(new).T

        def slim_gate_rows(at):
            to = pl.multiple_of(at // 2, SLIM_TILE)
            fill(slim_taps, slim_states, slim_motions, to, SLIM, SLIM_TILE)
            gates = sigmoid(
                dot(slim_taps[...], gate_ref[1].reshape(1280, 256)) + slim(fixed_ref[1, pl.ds(at, TILE), 0:256])
            )
            updates[pl.ds(to, SLIM_TILE), :] = gates[:, 0:128]
            slim_resets[pl.ds(slim_pad + to, SLIM_TILE), :] = (
                gates[:, 128:256] * slim_states[pl.ds(slim_pad + to, SLIM_TILE), :].astype(F32)
            ).astype(BF16)

        def slim_state_rows(at):
            to = pl.multiple_of(at // 2, SLIM_TILE)
            fill(slim_taps, slim_resets, slim_motions, to, SLIM, SLIM_TILE)
            candidate = jnp.tanh(
                dot(slim_taps[...], state_ref[1].reshape(1280, 128)) + slim(fixed_ref[1, pl.ds(at, TILE), 256:384])
            )
            old = slim_hidden[pl.ds(to, SLIM_TILE), :]
            new = old + updates[pl.ds(to, SLIM_TILE), :] * (candidate - old)
            slim_hidden[pl.ds(to, SLIM_TILE), :] = new
            flow[:, pl.ds(to, SLIM_TILE)] = head(new) + slim(flow_cols[pl.ds(at, TILE), :]).T

        if iteration == 0 and count != TILE:
            ready(0)
            ready(1)
        each_tile(count, columns_pass)
        if iteration == 0:
            ready(2)
            ready(3)
            each_tile(count, gate_rows)
            each_tile(count, state_rows)
        else:
            each_tile(count, slim_gate_rows)
            each_tile(count, slim_state_rows)

    for j in range(dests):
        for r in range(rows_per):
            at = j * rows_per * SLIM + r * SLIM
            out_ref[j, r * own : (r + 1) * own, :] = slim_hidden[at : at + own, :]
        moved = flow[:, j * rows_per * SLIM : (j + 1) * rows_per * SLIM]
        out_ref[j, rows_per * own : rows_per * own + 8, :] = jnp.concatenate(
            [moved, jnp.zeros((8, 128 - rows_per * SLIM), F32)], axis=1
        )


def finish_kernel(own, mine_ref, other_ref, first_ref, hidden_ref, flow_ref):
    half = lax.axis_index("loop")
    rows_per, width, _ = hidden_ref.shape
    columns = width // 2
    dests = mine_ref.shape[0]
    for ref, side in ((mine_ref, half), (other_ref, 1 - half)):
        start = pl.multiple_of(side * columns, 128)
        for r in range(rows_per):
            cells = [ref[j, r * own : (r + 1) * own, :] for j in range(dests)]
            hidden_ref[r, pl.ds(start, columns), :] = jnp.concatenate(cells, axis=0)
            moved = jnp.concatenate(
                [ref[j, rows_per * own : rows_per * own + 8, r * SLIM : r * SLIM + own] for j in range(dests)], axis=1
            )
            at = pl.multiple_of(r * width + side * columns, 128)
            total = first_ref[:, pl.ds(at, columns)] + moved
            for k in range(2):
                flow_ref[k, r : r + 1, pl.ds(start, columns)] = total[k : k + 1]


def local(
    frame_one,
    frame_two,
    context,
    carry_hidden,
    carry_flow,
    slot_target,
    slot_count,
    match_weight,
    offset_weight,
    gate_weight,
    state_weight,
    gru_bias,
    head_weight,
    delta_weight,
):
    dests = lax.axis_size("rows")
    halves = lax.axis_size("loop")
    rows_per, width, channels = frame_one.shape
    columns = frame_two.shape[1]
    pixels = rows_per * width
    slots, hidden_size = carry_hidden.shape
    cap = -(-slots // (dests * halves))
    own = columns // dests
    half_wide = round_up(columns - own + WIN, 8)
    padded = columns + half_wide
    room = 16 if dests <= 8 else 56

    rows_hidden = round_up(cap, 16)
    rows_slot = rows_hidden + round_up(8 * (-(-cap // 128)), 16)
    shard = frame_two.reshape(1, rows_per, columns, channels)
    if dests == 8:

        def swap(value, flip):
            return lax.ppermute(value, "rows", [(i, i ^ flip) for i in range(dests)])

        beside, near, wrap, across = (swap(shard, flip) for flip in (1, 2, 6, 4))
        near_beside, wrap_beside = (swap(beside, flip) for flip in (2, 6))
    else:
        beside = lax.all_gather(shard, "rows", axis=0, tiled=True)
    slot_target, beside = lax.optimization_barrier((slot_target, beside))
    packed = call(
        functools.partial(pack_kernel, dests, cap, pixels, own, half_wide),
        jax.ShapeDtypeStruct((dests, rows_slot + rows_per * WIN, hidden_size), BF16),
        [smem_spec()] + vmem_specs(4),
        [pltpu.VMEM((rows_per, padded, 128), F32)],
        (2 * slots * slots * 128, 1 << 20, 0),
        60,
        slot_count,
        slot_target.reshape(slots // 128, 128),
        carry_flow.T,
        carry_hidden,
        context,
    )
    if dests == 8:
        packed, across = lax.optimization_barrier((packed, across))
        across_beside = swap(across, 1)
        packed, near, wrap, near_beside, wrap_beside, across_beside = lax.optimization_barrier(
            (packed, near, wrap, near_beside, wrap_beside, across_beside)
        )
        keys = (shard, beside, near, near_beside, across, across_beside, wrap, wrap_beside)
    else:
        keys = (beside,)
    early = lax.all_to_all(packed, "rows", 0, 0, tiled=True)
    around = [(i, (i + 1) % halves) for i in range(halves)]
    early_other = lax.ppermute(early, "loop", around)
    ow = jnp.pad(offset_weight, ((0, 2), (0, 0)))
    hidden_part, flow_part = call(
        functools.partial(own_slots_kernel, cap),
        (jax.ShapeDtypeStruct((pixels, 128), F32), jax.ShapeDtypeStruct((8, pixels), F32)),
        vmem_specs(1),
        [],
        (slots * pixels * 128, 1 << 20, 0),
        room,
        early,
    )
    hidden_wide, flow_first, term = call(
        functools.partial(place_kernel, cap, half_wide, rows_per),
        (
            jax.ShapeDtypeStruct((rows_per, half_wide, 128), BF16),
            jax.ShapeDtypeStruct((8, pixels), F32),
            jax.ShapeDtypeStruct((rows_per, half_wide, 128), F32),
        ),
        vmem_specs(4),
        [pltpu.VMEM((rows_per, padded, 128), F32)] * 2,
        (slots * pixels * 128, 1 << 20, 0),
        room,
        early_other,
        hidden_part,
        flow_part,
        ow,
    )
    queries = frame_one.reshape(pixels, channels)
    chunks = dests // 2
    tile = 128
    keep, send = call(
        functools.partial(match_kernel, len(keys), len(keys) > 1, half_wide, rows_per),
        (jax.ShapeDtypeStruct((rows_per, half_wide, 384), F32),) * 2,
        vmem_specs(3 + len(keys)),
        [
            pltpu.VMEM((chunks, 4 * columns, channels), BF16),
            pltpu.VMEM((chunks, columns, channels), BF16),
            pltpu.VMEM((chunks, tile, 4 * columns), F32),
            pltpu.VMEM((pixels, 384), F32),
            pltpu.VMEM((rows_per, padded, 384), F32),
        ],
        (4 * pixels * chunks * 4 * columns * channels, 1 << 21, pixels * chunks * 5 * columns),
        room,
        queries,
        match_weight,
        ow,
        *keys,
    )
    other = lax.ppermute(send, "loop", around)
    sending = call(
        functools.partial(merge_kernel, own),
        jax.ShapeDtypeStruct((dests, rows_per * WIN, 256), BF16),
        vmem_specs(4),
        [],
        (0, 1 << 20, 0),
        room,
        keep,
        other,
        term,
        hidden_wide,
    )
    arrived = lax.all_to_all(sending, "rows", 0, 0, tiled=True)
    count = dests * rows_per * WIN
    back_rows = rows_per * own + 8
    hbm = pl.BlockSpec(memory_space=pltpu.HBM)
    gate_weight = pltpu.with_memory_space_constraint(gate_weight, pltpu.HBM)
    state_weight = pltpu.with_memory_space_constraint(state_weight, pltpu.HBM)
    fixed = call(
        context_kernel,
        jax.ShapeDtypeStruct((2, count, 384), F32),
        [vmem_specs(1)[0], hbm, hbm, vmem_specs(1)[0]],
        [
            pltpu.VMEM((2, 5, 128, 256), BF16),
            pltpu.VMEM((2, 5, 128, 128), BF16),
            pltpu.VMEM((count + 4 * WIN, 128), BF16),
            pltpu.VMEM((TILE, 640), BF16),
            pltpu.SemaphoreType.DMA((2,)),
        ],
        (4 * count * 5 * 128 * 384, 1 << 22, 0),
        room,
        early,
        gate_weight,
        state_weight,
        gru_bias,
    )
    outgoing = call(
        functools.partial(update_kernel, own, width),
        jax.ShapeDtypeStruct((dests, back_rows, 128), F32),
        vmem_specs(3) + [hbm, hbm] + vmem_specs(2),
        [
            pltpu.VMEM((count, 128), BF16),
            pltpu.VMEM((count, 128), F32),
            pltpu.VMEM((count + 4 * WIN, 128), BF16),
            pltpu.VMEM((count + 4 * WIN, 128), BF16),
            pltpu.VMEM((count + 4 * WIN, 128), BF16),
            pltpu.VMEM((count, 128), F32),
            pltpu.VMEM((TILE, 1280), BF16),
            pltpu.VMEM((8, count // 2), F32),
            pltpu.VMEM((count, 8), F32),
            pltpu.VMEM((2, 5, 256, 256), BF16),
            pltpu.VMEM((2, 5, 256, 128), BF16),
            pltpu.VMEM((SLIM_TILE, 1280), BF16),
            pltpu.VMEM((count // 2 + 4 * SLIM, 128), BF16),
            pltpu.VMEM((count // 2 + 4 * SLIM, 128), BF16),
            pltpu.VMEM((count // 2 + 4 * SLIM, 128), BF16),
            pltpu.VMEM((count // 2, 128), F32),
            pltpu.SemaphoreType.DMA((8,)),
        ],
        (8 * count * 5 * 256 * 384, 1 << 22, 8 * count * 384),
        room,
        arrived,
        fixed,
        ow,
        gate_weight,
        state_weight,
        head_weight,
        jnp.pad(delta_weight, ((0, 6), (0, 0))),
    )
    back = lax.all_to_all(outgoing, "rows", 0, 0, tiled=True)
    hidden_out, flow_out = call(
        functools.partial(finish_kernel, own),
        (
            jax.ShapeDtypeStruct((rows_per, width, hidden_size), F32),
            jax.ShapeDtypeStruct((2, rows_per, width), F32),
        ),
        vmem_specs(3),
        [],
        (0, 1 << 20, 0),
        room,
        back,
        lax.ppermute(back, "loop", around),
        flow_first,
    )
    return (hidden_out, flow_out)


def solution(mesh):
    return jax.shard_map(
        local,
        mesh=mesh,
        in_specs=(
            P(("groups", "rows"), None, None),
            P(("groups", "rows"), "loop", None),
            P(("groups", "rows"), None, None),
            P(("groups", "rows"), None),
            P(("groups", "rows"), None),
            P(("groups", "rows")),
            P(("groups", "rows")),
            P(),
            P(),
            P(),
            P(),
            P(),
            P(),
            P(),
        ),
        out_specs=(P(("groups", "rows"), None, None), P(None, ("groups", "rows"), None)),
        check_vma=False,
    )
```

```python
import functools
import math

import jax
import jax.numpy as jnp
from jax import lax
from jax.experimental import pallas as pl
from jax.experimental.pallas import tpu as pltpu
from jax.sharding import PartitionSpec as P

ITERS = 2
WIN = 32
SLIM = 16
HALO = 8
TILE = 512
SLIM_TILE = TILE * SLIM // WIN
OFFSET_SCALE = 0.03125
F32 = jnp.float32
BF16 = jnp.bfloat16
VMEM = pltpu.VMEM
NT = (((1,), (1,)), ((), ()))


def iota(shape, dim):
    return lax.broadcasted_iota(jnp.int32, shape, dim)


def round_up(value, step):
    return -(-value // step) * step


def dot(a, b):
    return jnp.dot(a, b, preferred_element_type=F32)


def dot_nt(a, b):
    return lax.dot_general(a, b, NT, preferred_element_type=F32)


def vmem_specs(count):
    return [pl.BlockSpec(memory_space=VMEM)] * count


def smem_spec():
    return pl.BlockSpec(memory_space=pltpu.SMEM)


def loop(count, body, carry):
    return lax.fori_loop(0, count, body, carry, unroll=count <= 4)


def call(kernel, out_shape, in_specs, scratch, cost, room, *args):
    single = not isinstance(out_shape, (tuple, list))
    return pl.pallas_call(
        kernel,
        out_shape=out_shape,
        in_specs=in_specs,
        out_specs=vmem_specs(1)[0] if single else vmem_specs(len(out_shape)),
        scratch_shapes=scratch,
        compiler_params=pltpu.CompilerParams(vmem_limit_bytes=room * 1024 * 1024),
        cost_estimate=pl.CostEstimate(flops=cost[0], bytes_accessed=cost[1], transcendentals=cost[2]),
    )(*args)


def pack_kernel(dests, cap, pixels, own, half_wide, count_ref, target_ref, flow_ref, hidden_ref, context_ref, out_ref, wide):
    slots = hidden_ref.shape[0]
    target = jnp.concatenate([target_ref[k : k + 1, :] for k in range(slots // 128)], axis=1)
    counted = iota((1, slots), 1) < count_ref[0]
    owner = target // pixels
    within = target % pixels
    belongs = (iota((dests, slots), 0) == owner) & counted
    member = jnp.where(belongs, 1.0, 0.0)
    upper = jnp.where(iota((128, 128), 0) <= iota((128, 128), 1), 1.0, 0.0).astype(BF16)
    before = jnp.zeros((dests, 1), F32)
    ranks = []
    for start in range(0, slots, 128):
        running = dot(member[:, start : start + 128].astype(BF16), upper) + before
        before = running[:, 127:128]
        ranks.append(running)
    rank = jnp.concatenate(ranks, axis=1) - 1.0 - (lax.axis_index("loop") * cap).astype(F32)
    belongs = belongs & (rank >= 0.0) & (rank < cap)
    place_at = jnp.sum(
        jnp.where(belongs, rank + iota((dests, slots), 0).astype(F32) * cap, 0.0), axis=0, keepdims=True
    )
    taken = jnp.max(jnp.where(belongs, 1.0, 0.0), axis=0, keepdims=True)
    landing = jnp.where(taken > 0.5, place_at, -1.0).astype(jnp.int32)
    row = iota((8, slots), 0)
    flow = flow_ref[...].astype(F32)
    side = jnp.where(row == 0, flow[0:1], 0.0)
    side = jnp.where(row == 1, flow[1:2], side)
    side = jnp.where(row == 2, (within // 256).astype(F32), side)
    side = jnp.where(row == 3, (within % 256).astype(F32), side)
    side = jnp.where(row == 4, 1.0, side).astype(BF16)
    hidden = hidden_ref[...]
    rows_hidden = round_up(cap, 16)
    together = max(1, min(dests, 192 // cap))
    for first in range(0, dests, together):
        spots = together * cap
        chosen = jnp.where(iota((spots, slots), 0) + first * cap == landing, 1.0, 0.0).astype(BF16)
        moved = dot(chosen, hidden)
        moved_side = dot_nt(side, chosen)
        for k in range(together):
            out_ref[first + k, 0:cap, :] = moved[k * cap : (k + 1) * cap].astype(BF16)
            for t in range(-(-cap // 128)):
                width = min(128, cap - t * 128)
                piece = moved_side[:, k * cap + t * 128 : k * cap + t * 128 + width]
                if width < 128:
                    piece = jnp.concatenate([piece, jnp.zeros((8, 128 - width), F32)], axis=1)
                base = rows_hidden + 8 * t
                out_ref[first + k, base : base + 8, :] = piece.astype(BF16)
    rows_per, width, _ = context_ref.shape
    top = out_ref.shape[1] - rows_per * WIN
    start = pl.multiple_of(lax.axis_index("loop") * (width // 2), 128)
    wide[...] = jnp.zeros_like(wide)
    for r in range(rows_per):
        wide[r, HALO : HALO + width, :] = context_ref[r].astype(F32)
        part = wide[r, pl.ds(start, half_wide), :]
        for j in range(dests):
            out_ref[j, top + r * WIN : top + (r + 1) * WIN, :] = part[j * own : j * own + WIN].astype(BF16)


def gather_slots(cap, got_ref, hidden, flow):
    rows_hidden = round_up(cap, 16)
    pixels = flow.shape[1]
    for j in range(got_ref.shape[0]):
        pieces = []
        for t in range(-(-cap // 128)):
            base = rows_hidden + 8 * t
            pieces.append(got_ref[j, base : base + 8, 0 : min(128, cap - t * 128)].astype(F32))
        side = pieces[0] if len(pieces) == 1 else jnp.concatenate(pieces, axis=1)
        place = jnp.where(side[4:5] > 0.5, side[2:3] * 256.0 + side[3:4], -1.0).astype(jnp.int32)
        chosen = jnp.where(iota((pixels, cap), 0) == place, 1.0, 0.0).astype(BF16)
        hidden = hidden + dot(chosen, got_ref[j, 0:cap, :])
        flow = flow + dot_nt(side.astype(BF16), chosen)
    return hidden, flow


def own_slots_kernel(cap, got_ref, hidden_ref, flow_ref):
    zeros = jnp.zeros(hidden_ref.shape, F32), jnp.zeros(flow_ref.shape, F32)
    hidden_ref[...], flow_ref[...] = gather_slots(cap, got_ref, *zeros)


def place_kernel(cap, half_wide, rows_per, got_ref, part_ref, flow_part_ref, ow_ref, hidden_ref, flow_ref, term_ref, wide_hidden, wide_term):
    half = lax.axis_index("loop")
    pixels = flow_ref.shape[1]
    width = pixels // rows_per
    hidden, flow = gather_slots(cap, got_ref, part_ref[...], flow_part_ref[...])
    flow_ref[...] = flow
    columns = flow.T
    ow = ow_ref[...]
    term = columns[:, 0:1] * (OFFSET_SCALE * (ow[4:5] - ow[0:1] - ow[2:3])) + columns[:, 1:2] * (
        OFFSET_SCALE * (ow[5:6] - ow[1:2] - ow[3:4])
    )
    start = pl.multiple_of(half * (width // 2), 128)
    for wide, value, out in ((wide_hidden, hidden, hidden_ref), (wide_term, term, term_ref)):
        wide[...] = jnp.zeros_like(wide)
        for r in range(rows_per):
            wide[r, HALO : HALO + width, :] = value[r * width : (r + 1) * width]
            out[r] = wide[r, pl.ds(start, half_wide), :].astype(out.dtype)


def match_kernel(
    count, flip, half_wide, rows_per, queries_ref, weight_ref, ow_ref, *refs
):
    key_refs, (keep_ref, send_ref, fine, coarse, scores, mixed, wide) = refs[:count], refs[count:]
    me, half = lax.axis_index("rows"), lax.axis_index("loop")
    pixels, channels = queries_ref.shape
    width = pixels // rows_per
    columns = width // 2
    quarter = columns // 2
    chunks = fine.shape[0]
    shards = chunks * 2
    per_ref = shards // count
    spread = jnp.where(
        iota((columns, columns), 1)
        == jnp.where(iota((columns, columns), 0) < quarter, 2 * iota((columns, columns), 0), 2 * (iota((columns, columns), 0) - quarter) + 1),
        1.0,
        0.0,
    ).astype(BF16)

    def sort_shard(ref, m, shard, lane):
        even, odd = [], []
        for r in range(rows_per):
            parted = dot(spread, ref[m, r])
            even.append(parted[:quarter])
            odd.append(parted[quarter:])
            for p, part in ((0, even[-1]), (1, odd[-1])):
                g = 2 * r + p
                fine[shard, g * 2 * quarter + lane * quarter : g * 2 * quarter + (lane + 1) * quarter, :] = part.astype(BF16)
        pooled = (even[0] + odd[0] + even[1] + odd[1]) * 0.25
        coarse[shard, lane * quarter : (lane + 1) * quarter, :] = pooled.astype(BF16)

    if per_ref == 1:
        for m in range(shards):
            sort_shard(key_refs[m], 0, m // 2, m % 2)
    else:
        def sort_chunk(c, carry):
            for lane in range(2):
                sort_shard(key_refs[0], c * 2 + lane, c, lane)
            return carry

        lax.fori_loop(0, chunks, sort_chunk, 0)

    group = 2 * quarter
    tile = scores.shape[1]
    lane = iota((1, group), 1)
    lane_col = ((lane % quarter) * 2 + half * columns).astype(F32)
    ow = ow_ref[...] * OFFSET_SCALE
    weight = weight_ref[...]

    def lane_row(c):
        arrival = c * 2 + lane // quarter
        shard = lax.bitwise_xor(arrival, me) if flip else arrival
        return (shard * rows_per).astype(F32)

    wide[...] = jnp.zeros_like(wide)

    def one_tile(t, carry):
        first = pl.multiple_of(t * tile, tile)
        queries = queries_ref[pl.ds(first, tile), :] * jnp.asarray(1.0 / math.sqrt(channels), BF16)

        def score(c, peaks):
            values = dot_nt(queries, fine[c])
            scores[c] = values
            parts = [values[:, g * group : (g + 1) * group] for g in range(4)]
            blended = (parts[0] + parts[1] + parts[2] + parts[3]) * 0.25
            high = jnp.maximum(jnp.maximum(parts[0], parts[1]), jnp.maximum(parts[2], parts[3]))
            return jnp.maximum(peaks[0], high), jnp.maximum(peaks[1], blended)

        low = jnp.full((tile, group), -jnp.inf, F32)
        peaks = loop(chunks, score, (low, low))
        peak_fine = jnp.max(peaks[0], axis=1, keepdims=True)
        peak_coarse = jnp.max(peaks[1], axis=1, keepdims=True)

        def absorb(c, so_far):
            total, below, right, rows, c_total, c_rows, acc_fine, acc_coarse = so_far
            parts = [scores[c, :, g * group : (g + 1) * group] for g in range(4)]
            blended = (parts[0] + parts[1] + parts[2] + parts[3]) * 0.25
            expo = [jnp.exp(part - peak_fine) for part in parts]
            c_expo = jnp.exp(blended - peak_coarse)
            lower = expo[2] + expo[3]
            everything = expo[0] + expo[1] + lower
            at = lane_row(c)
            weights = jnp.concatenate([e.astype(BF16) for e in expo], axis=1)
            return (
                total + everything,
                below + lower,
                right + (expo[1] + expo[3]),
                rows + everything * at,
                c_total + c_expo,
                c_rows + c_expo * at,
                acc_fine + dot(weights, fine[c]),
                acc_coarse + dot(c_expo.astype(BF16), coarse[c]),
            )

        zero = jnp.zeros((tile, group), F32)
        blank = jnp.zeros((tile, channels), F32)
        total, below, right, rows, c_total, c_rows, acc_fine, acc_coarse = loop(
            chunks, absorb, (zero, zero, zero, zero, zero, zero, blank, blank)
        )

        def over(value):
            return jnp.sum(value, axis=1, keepdims=True)

        pixel = first + iota((tile, 1), 0)
        own_row = (me * rows_per + pixel // width).astype(F32)
        own_col = (pixel % width).astype(F32)
        fine_sum, coarse_sum = over(total), over(c_total)
        fine_row = over(rows + below) / fine_sum - own_row
        fine_col = over(total * lane_col + right) / fine_sum - own_col
        coarse_row = over(c_rows) / coarse_sum + 0.5 - own_row
        coarse_col = over(c_total * lane_col) / coarse_sum + 0.5 - own_col
        fine_out = dot((acc_fine / fine_sum).astype(BF16), weight[:channels])
        coarse_out = dot((acc_coarse / coarse_sum).astype(BF16), weight[channels:])
        mixed[pl.ds(first, tile), 0:128] = fine_out + fine_row * ow[0:1] + fine_col * ow[1:2]
        mixed[pl.ds(first, tile), 128:256] = coarse_out + coarse_row * ow[2:3] + coarse_col * ow[3:4]
        mixed[pl.ds(first, tile), 256:384] = jnp.where(
            iota((tile, 128), 1) < 64,
            peak_fine + jnp.log(fine_sum),
            peak_coarse + jnp.log(coarse_sum),
        )
        return carry

    lax.fori_loop(0, pixels // tile, one_tile, 0)
    start = pl.multiple_of(half * columns, 128)
    other = pl.multiple_of((1 - half) * columns, 128)
    for r in range(rows_per):
        wide[r, HALO : HALO + width, :] = mixed[r * width : (r + 1) * width, :]
        keep_ref[r] = wide[r, pl.ds(start, half_wide), :]
        send_ref[r] = wide[r, pl.ds(other, half_wide), :]


def combine_kernel(keep_ref, got_ref, out_ref):
    for r in range(keep_ref.shape[0]):
        keep, got = keep_ref[r], got_ref[r]
        gap = got[:, 256:384] - keep[:, 256:384]
        share = 1.0 / (1.0 + jnp.exp(gap))
        out_ref[r] = (
            got[:, 0:128]
            + (keep[:, 0:128] - got[:, 0:128]) * share[:, 0:1]
            + got[:, 128:256]
            + (keep[:, 128:256] - got[:, 128:256]) * share[:, 64:65]
        )


def merge_kernel(own, base_ref, term_ref, hidden_ref, out_ref):
    dests = out_ref.shape[0]
    for r in range(base_ref.shape[0]):
        base = base_ref[r] + term_ref[r]
        hidden = hidden_ref[r].astype(F32)
        for j in range(dests):
            out_ref[j, r * WIN : (r + 1) * WIN, 0:128] = base[j * own : j * own + WIN].astype(BF16)
            out_ref[j, r * WIN : (r + 1) * WIN, 128:256] = hidden[j * own : j * own + WIN].astype(BF16)


def sigmoid(x):
    return 0.5 * jnp.tanh(0.5 * x) + 0.5


def shifted(value, tap):
    return value if tap == 2 else pltpu.roll(value, (2 - tap) % TILE, 0)


def each_tile(count, body):
    def step(t, carry):
        body(pl.multiple_of(t * TILE, TILE))
        return carry

    lax.fori_loop(0, count // TILE, step, 0, unroll=count == TILE)


def fetch(copies, sems, first=0):
    handles = []
    for k, (source, target) in enumerate(copies):
        handles.append(pltpu.make_async_copy(source, target, sems.at[first + k]))
        handles[-1].start()
    return handles


def context_kernel(early_ref, gate_hbm, state_hbm, bias_ref, fixed_ref, gate_ref, state_ref, padded, taps, sems):
    handles = fetch(
        [
            (gate_hbm.at[:, :, pl.ds(128, 128), :], gate_ref),
            (state_hbm.at[:, :, pl.ds(128, 128), :], state_ref),
        ],
        sems,
    )
    dests = early_ref.shape[0]
    count = fixed_ref.shape[1]
    per_dest = count // dests
    first = early_ref.shape[1] - per_dest
    pad = 2 * WIN
    padded[0:pad, :] = jnp.zeros((pad, 128), BF16)
    padded[pad + count : pad + count + pad, :] = jnp.zeros((pad, 128), BF16)
    for j in range(dests):
        padded[pad + j * per_dest : pad + (j + 1) * per_dest, :] = early_ref[j, first : first + per_dest, :]
    for handle in handles:
        handle.wait()
    for p in range(2):

        def one(at):
            for tap in range(5):
                if p == 0:
                    value = shifted(padded[pl.ds(pad + at, TILE), :].astype(F32), tap).astype(BF16)
                else:
                    value = padded[pl.ds(at + tap * WIN, TILE), :]
                taps[:, tap * 128 : (tap + 1) * 128] = value
            gate = gate_ref[p].reshape(640, 256)
            state = state_ref[p].reshape(640, 128)
            fixed_ref[p, pl.ds(at, TILE), 0:256] = dot(taps[...], gate) + bias_ref[p : p + 1, 0:256]
            fixed_ref[p, pl.ds(at, TILE), 256:384] = dot(taps[...], state) + bias_ref[p : p + 1, 256:384]

        each_tile(count, one)


def update_kernel(
    own, width, got_ref, fixed_ref, ow_ref, gate_hbm, state_hbm, head_ref, delta_ref,
    out_ref, base, hidden, motions, states, resets, updates, taps, flow, flow_cols, gate_ref, state_ref,
    slim_taps, slim_states, slim_motions, slim_resets, slim_hidden, sems,
):
    handles = []
    for p in range(2):
        for source, target in ((gate_hbm, gate_ref), (state_hbm, state_ref)):
            parts = [
                (source.at[p, :, pl.ds(256 * k, 128), :], target.at[p, :, pl.ds(128 * k, 128), :]) for k in range(2)
            ]
            handles.append(fetch(parts, sems, 2 * len(handles)))

    def ready(k):
        for handle in handles[k]:
            handle.wait()

    me, half = lax.axis_index("rows"), lax.axis_index("loop")
    dests, per_dest, _ = got_ref.shape
    rows_per = per_dest // WIN
    count = dests * per_dest
    pad = 2 * WIN
    first_col = (half * dests + me) * own - HALO
    column = first_col + iota((TILE, 128), 0) % WIN
    inside = (column >= 0) & (column < width)
    mask = jnp.where(inside, 1.0, 0.0)
    ow = ow_ref[...]
    add_row = OFFSET_SCALE * (ow[4:5] - ow[0:1] - ow[2:3])
    add_col = OFFSET_SCALE * (ow[5:6] - ow[1:2] - ow[3:4])

    for ref in (motions, states, resets):
        ref[0:pad, :] = jnp.zeros((pad, 128), BF16)
        ref[pad + count : pad + count + pad, :] = jnp.zeros((pad, 128), BF16)
    slim_pad = 2 * SLIM
    for ref in (slim_motions, slim_states, slim_resets):
        ref[0:slim_pad, :] = jnp.zeros((slim_pad, 128), BF16)
        ref[slim_pad + count // 2 :, :] = jnp.zeros((slim_pad, 128), BF16)
    for j in range(dests):
        at = j * per_dest
        base[at : at + per_dest, :] = got_ref[j, :, 0:128]
        hidden[at : at + per_dest, :] = got_ref[j, :, 128:256].astype(F32)

    def finish(at, update, candidate):
        old = hidden[pl.ds(at, TILE), :]
        new = (old + update * (candidate - old)) * mask
        hidden[pl.ds(at, TILE), :] = new
        return new

    def slim(value):
        cube = value.reshape(TILE // WIN, WIN, value.shape[1])
        return cube[:, HALO : HALO + SLIM, :].reshape(SLIM_TILE, value.shape[1])

    for iteration in range(ITERS):
        last = iteration == ITERS - 1

        def columns_pass(at):
            motion = base[pl.ds(at, TILE), :].astype(F32)
            if iteration > 0:
                moved = flow_cols[pl.ds(at, TILE), :]
                motion = (motion + moved[:, 0:1] * add_row + moved[:, 1:2] * add_col) * mask
            motion = jnp.maximum(motion, 0.0)
            rounded = motion.astype(BF16)
            if not last:
                motions[pl.ds(pad + at, TILE), :] = rounded
            motion = rounded.astype(F32)
            state = hidden[pl.ds(at, TILE), :].astype(BF16).astype(F32)
            for tap in range(5):
                taps[:, tap * 256 : tap * 256 + 128] = shifted(state, tap).astype(BF16)
                taps[:, tap * 256 + 128 : tap * 256 + 256] = shifted(motion, tap).astype(BF16)
            if iteration == 0 and count == TILE:
                ready(0)
            gates = sigmoid(dot(taps[...], gate_ref[0].reshape(1280, 256)) + fixed_ref[0, pl.ds(at, TILE), 0:256])
            reset = (gates[:, 128:256] * state).astype(BF16).astype(F32)
            if last:
                to = pl.multiple_of(at // 2, SLIM_TILE)
                for tap in range(5):
                    slim_taps[:, tap * 256 : tap * 256 + 128] = slim(shifted(reset, tap)).astype(BF16)
                    slim_taps[:, tap * 256 + 128 : tap * 256 + 256] = slim(shifted(motion, tap)).astype(BF16)
                candidate = jnp.tanh(
                    dot(slim_taps[...], state_ref[0].reshape(1280, 128)) + slim(fixed_ref[0, pl.ds(at, TILE), 256:384])
                )
                old = slim(hidden[pl.ds(at, TILE), :])
                new = old + slim(gates[:, 0:128]) * (candidate - old)
                slim_hidden[pl.ds(to, SLIM_TILE), :] = new
                slim_states[pl.ds(slim_pad + to, SLIM_TILE), :] = new.astype(BF16)
                slim_motions[pl.ds(slim_pad + to, SLIM_TILE), :] = slim(motion).astype(BF16)
                return
            for tap in range(5):
                taps[:, tap * 256 : tap * 256 + 128] = shifted(reset, tap).astype(BF16)
            if iteration == 0 and count == TILE:
                ready(1)
            candidate = jnp.tanh(dot(taps[...], state_ref[0].reshape(1280, 128)) + fixed_ref[0, pl.ds(at, TILE), 256:384])
            states[pl.ds(pad + at, TILE), :] = finish(at, gates[:, 0:128], candidate).astype(BF16)

        def fill(out, first, second, at, stride, size):
            for tap in range(5):
                out[:, tap * 256 : tap * 256 + 128] = first[pl.ds(at + tap * stride, size), :]
                out[:, tap * 256 + 128 : tap * 256 + 256] = second[pl.ds(at + tap * stride, size), :]

        def gate_rows(at):
            fill(taps, states, motions, at, WIN, TILE)
            gates = sigmoid(dot(taps[...], gate_ref[1].reshape(1280, 256)) + fixed_ref[1, pl.ds(at, TILE), 0:256])
            updates[pl.ds(at, TILE), :] = gates[:, 0:128]
            resets[pl.ds(pad + at, TILE), :] = (
                gates[:, 128:256] * states[pl.ds(pad + at, TILE), :].astype(F32)
            ).astype(BF16)

        def head(new):
            lifted = jnp.maximum(dot(new.astype(BF16), head_ref[...]), 0.0).astype(BF16)
            return dot_nt(delta_ref[...], lifted)

        def state_rows(at):
            fill(taps, resets, motions, at, WIN, TILE)
            candidate = jnp.tanh(
                dot(taps[...], state_ref[1].reshape(1280, 128)) + fixed_ref[1, pl.ds(at, TILE), 256:384]
            )
            new = finish(at, updates[pl.ds(at, TILE), :], candidate)
            flow_cols[pl.ds(at, TILE), :] = head(new).T

        def slim_gate_rows(at):
            to = pl.multiple_of(at // 2, SLIM_TILE)
            fill(slim_taps, slim_states, slim_motions, to, SLIM, SLIM_TILE)
            gates = sigmoid(
                dot(slim_taps[...], gate_ref[1].reshape(1280, 256)) + slim(fixed_ref[1, pl.ds(at, TILE), 0:256])
            )
            updates[pl.ds(to, SLIM_TILE), :] = gates[:, 0:128]
            slim_resets[pl.ds(slim_pad + to, SLIM_TILE), :] = (
                gates[:, 128:256] * slim_states[pl.ds(slim_pad + to, SLIM_TILE), :].astype(F32)
            ).astype(BF16)

        def slim_state_rows(at):
            to = pl.multiple_of(at // 2, SLIM_TILE)
            fill(slim_taps, slim_resets, slim_motions, to, SLIM, SLIM_TILE)
            candidate = jnp.tanh(
                dot(slim_taps[...], state_ref[1].reshape(1280, 128)) + slim(fixed_ref[1, pl.ds(at, TILE), 256:384])
            )
            old = slim_hidden[pl.ds(to, SLIM_TILE), :]
            new = old + updates[pl.ds(to, SLIM_TILE), :] * (candidate - old)
            slim_hidden[pl.ds(to, SLIM_TILE), :] = new
            flow[:, pl.ds(to, SLIM_TILE)] = head(new) + slim(flow_cols[pl.ds(at, TILE), :]).T

        if iteration == 0 and count != TILE:
            ready(0)
            ready(1)
        each_tile(count, columns_pass)
        if iteration == 0:
            ready(2)
            ready(3)
            each_tile(count, gate_rows)
            each_tile(count, state_rows)
        else:
            each_tile(count, slim_gate_rows)
            each_tile(count, slim_state_rows)

    for j in range(dests):
        for r in range(rows_per):
            at = j * rows_per * SLIM + r * SLIM
            out_ref[j, r * own : (r + 1) * own, :] = slim_hidden[at : at + own, :]
        moved = flow[:, j * rows_per * SLIM : (j + 1) * rows_per * SLIM]
        out_ref[j, rows_per * own : rows_per * own + 8, :] = jnp.concatenate(
            [moved, jnp.zeros((8, 128 - rows_per * SLIM), F32)], axis=1
        )


def finish_kernel(own, mine_ref, other_ref, first_ref, hidden_ref, flow_ref):
    half = lax.axis_index("loop")
    rows_per, width, _ = hidden_ref.shape
    columns = width // 2
    dests = mine_ref.shape[0]
    for ref, side in ((mine_ref, half), (other_ref, 1 - half)):
        start = pl.multiple_of(side * columns, 128)
        for r in range(rows_per):
            cells = [ref[j, r * own : (r + 1) * own, :] for j in range(dests)]
            hidden_ref[r, pl.ds(start, columns), :] = jnp.concatenate(cells, axis=0)
            moved = jnp.concatenate(
                [ref[j, rows_per * own : rows_per * own + 8, r * SLIM : r * SLIM + own] for j in range(dests)], axis=1
            )
            at = pl.multiple_of(r * width + side * columns, 128)
            total = first_ref[:, pl.ds(at, columns)] + moved
            for k in range(2):
                flow_ref[k, r : r + 1, pl.ds(start, columns)] = total[k : k + 1]


def local(
    frame_one,
    frame_two,
    context,
    carry_hidden,
    carry_flow,
    slot_target,
    slot_count,
    match_weight,
    offset_weight,
    gate_weight,
    state_weight,
    gru_bias,
    head_weight,
    delta_weight,
):
    dests = lax.axis_size("rows")
    halves = lax.axis_size("loop")
    rows_per, width, channels = frame_one.shape
    columns = frame_two.shape[1]
    pixels = rows_per * width
    slots, hidden_size = carry_hidden.shape
    cap = -(-slots // (dests * halves))
    own = columns // dests
    half_wide = round_up(columns - own + WIN, 8)
    padded = columns + half_wide
    room = 16 if dests <= 8 else 56

    rows_hidden = round_up(cap, 16)
    rows_slot = rows_hidden + 8 * (-(-cap // 128))
    shard = frame_two.reshape(1, rows_per, columns, channels)
    if dests == 8:

        def swap(value, flip):
            return lax.ppermute(value, "rows", [(i, i ^ flip) for i in range(dests)])

        beside, near, wrap, across = (swap(shard, flip) for flip in (1, 2, 6, 4))
        near_beside, wrap_beside = (swap(beside, flip) for flip in (2, 6))
    else:
        beside = lax.all_gather(shard, "rows", axis=0, tiled=True)
    slot_target, beside = lax.optimization_barrier((slot_target, beside))
    packed = call(
        functools.partial(pack_kernel, dests, cap, pixels, own, half_wide),
        jax.ShapeDtypeStruct((dests, rows_slot + rows_per * WIN, hidden_size), BF16),
        [smem_spec()] + vmem_specs(4),
        [pltpu.VMEM((rows_per, padded, 128), F32)],
        (2 * slots * slots * 128, 1 << 20, 0),
        60,
        slot_count,
        slot_target.reshape(slots // 128, 128),
        carry_flow.T,
        carry_hidden,
        context,
    )
    if dests == 8:
        packed, across = lax.optimization_barrier((packed, across))
        across_beside = swap(across, 1)
        packed, near, wrap, near_beside, wrap_beside, across_beside = lax.optimization_barrier(
            (packed, near, wrap, near_beside, wrap_beside, across_beside)
        )
        keys = (shard, beside, near, near_beside, across, across_beside, wrap, wrap_beside)
    else:
        keys = (beside,)
    early = lax.all_to_all(packed, "rows", 0, 0, tiled=True)
    around = [(i, (i + 1) % halves) for i in range(halves)]
    early_other = lax.ppermute(early, "loop", around)
    ow = jnp.pad(offset_weight, ((0, 2), (0, 0)))
    hidden_part, flow_part = call(
        functools.partial(own_slots_kernel, cap),
        (jax.ShapeDtypeStruct((pixels, 128), F32), jax.ShapeDtypeStruct((8, pixels), F32)),
        vmem_specs(1),
        [],
        (slots * pixels * 128, 1 << 20, 0),
        room,
        early,
    )
    hidden_wide, flow_first, term = call(
        functools.partial(place_kernel, cap, half_wide, rows_per),
        (
            jax.ShapeDtypeStruct((rows_per, half_wide, 128), BF16),
            jax.ShapeDtypeStruct((8, pixels), F32),
            jax.ShapeDtypeStruct((rows_per, half_wide, 128), F32),
        ),
        vmem_specs(4),
        [pltpu.VMEM((rows_per, padded, 128), F32)] * 2,
        (slots * pixels * 128, 1 << 20, 0),
        room,
        early_other,
        hidden_part,
        flow_part,
        ow,
    )
    queries = frame_one.reshape(pixels, channels)
    chunks = dests // 2
    tile = 128
    keep, send = call(
        functools.partial(match_kernel, len(keys), len(keys) > 1, half_wide, rows_per),
        (jax.ShapeDtypeStruct((rows_per, half_wide, 384), F32),) * 2,
        vmem_specs(3 + len(keys)),
        [
            pltpu.VMEM((chunks, 4 * columns, channels), BF16),
            pltpu.VMEM((chunks, columns, channels), BF16),
            pltpu.VMEM((chunks, tile, 4 * columns), F32),
            pltpu.VMEM((pixels, 384), F32),
            pltpu.VMEM((rows_per, padded, 384), F32),
        ],
        (4 * pixels * chunks * 4 * columns * channels, 1 << 21, pixels * chunks * 5 * columns),
        room,
        queries,
        match_weight,
        ow,
        *keys,
    )
    other = lax.ppermute(send, "loop", around)
    combined = call(
        combine_kernel,
        jax.ShapeDtypeStruct((rows_per, half_wide, 128), F32),
        vmem_specs(2),
        [],
        (0, 1 << 20, 0),
        room,
        keep,
        other,
    )
    sending = call(
        functools.partial(merge_kernel, own),
        jax.ShapeDtypeStruct((dests, rows_per * WIN, 256), BF16),
        vmem_specs(3),
        [],
        (0, 1 << 20, 0),
        room,
        combined,
        term,
        hidden_wide,
    )
    arrived = lax.all_to_all(sending, "rows", 0, 0, tiled=True)
    count = dests * rows_per * WIN
    back_rows = rows_per * own + 8
    hbm = pl.BlockSpec(memory_space=pltpu.HBM)
    gate_weight = pltpu.with_memory_space_constraint(gate_weight, pltpu.HBM)
    state_weight = pltpu.with_memory_space_constraint(state_weight, pltpu.HBM)
    fixed = call(
        context_kernel,
        jax.ShapeDtypeStruct((2, count, 384), F32),
        [vmem_specs(1)[0], hbm, hbm, vmem_specs(1)[0]],
        [
            pltpu.VMEM((2, 5, 128, 256), BF16),
            pltpu.VMEM((2, 5, 128, 128), BF16),
            pltpu.VMEM((count + 4 * WIN, 128), BF16),
            pltpu.VMEM((TILE, 640), BF16),
            pltpu.SemaphoreType.DMA((2,)),
        ],
        (4 * count * 5 * 128 * 384, 1 << 22, 0),
        room,
        early,
        gate_weight,
        state_weight,
        gru_bias,
    )
    outgoing = call(
        functools.partial(update_kernel, own, width),
        jax.ShapeDtypeStruct((dests, back_rows, 128), F32),
        vmem_specs(3) + [hbm, hbm] + vmem_specs(2),
        [
            pltpu.VMEM((count, 128), BF16),
            pltpu.VMEM((count, 128), F32),
            pltpu.VMEM((count + 4 * WIN, 128), BF16),
            pltpu.VMEM((count + 4 * WIN, 128), BF16),
            pltpu.VMEM((count + 4 * WIN, 128), BF16),
            pltpu.VMEM((count, 128), F32),
            pltpu.VMEM((TILE, 1280), BF16),
            pltpu.VMEM((8, count // 2), F32),
            pltpu.VMEM((count, 8), F32),
            pltpu.VMEM((2, 5, 256, 256), BF16),
            pltpu.VMEM((2, 5, 256, 128), BF16),
            pltpu.VMEM((SLIM_TILE, 1280), BF16),
            pltpu.VMEM((count // 2 + 4 * SLIM, 128), BF16),
            pltpu.VMEM((count // 2 + 4 * SLIM, 128), BF16),
            pltpu.VMEM((count // 2 + 4 * SLIM, 128), BF16),
            pltpu.VMEM((count // 2, 128), F32),
            pltpu.SemaphoreType.DMA((8,)),
        ],
        (8 * count * 5 * 256 * 384, 1 << 22, 8 * count * 384),
        room,
        arrived,
        fixed,
        ow,
        gate_weight,
        state_weight,
        head_weight,
        jnp.pad(delta_weight, ((0, 6), (0, 0))),
    )
    back = lax.all_to_all(outgoing, "rows", 0, 0, tiled=True)
    hidden_out, flow_out = call(
        functools.partial(finish_kernel, own),
        (
            jax.ShapeDtypeStruct((rows_per, width, hidden_size), F32),
            jax.ShapeDtypeStruct((2, rows_per, width), F32),
        ),
        vmem_specs(3),
        [],
        (0, 1 << 20, 0),
        room,
        back,
        lax.ppermute(back, "loop", around),
        flow_first,
    )
    return (hidden_out, flow_out)


def solution(mesh):
    return jax.shard_map(
        local,
        mesh=mesh,
        in_specs=(
            P(("groups", "rows"), None, None),
            P(("groups", "rows"), "loop", None),
            P(("groups", "rows"), None, None),
            P(("groups", "rows"), None),
            P(("groups", "rows"), None),
            P(("groups", "rows")),
            P(("groups", "rows")),
            P(),
            P(),
            P(),
            P(),
            P(),
            P(),
            P(),
        ),
        out_specs=(P(("groups", "rows"), None, None), P(None, ("groups", "rows"), None)),
        check_vma=False,
    )
```

```python
import functools
import math

import jax
import jax.numpy as jnp
from jax import lax
from jax.experimental import pallas as pl
from jax.experimental.pallas import tpu as pltpu
from jax.sharding import PartitionSpec as P

ITERS = 2
WIN = 32
SLIM = 16
HALO = 8
TILE = 512
SLIM_TILE = TILE * SLIM // WIN
OFFSET_SCALE = 0.03125
F32 = jnp.float32
BF16 = jnp.bfloat16
VMEM = pltpu.VMEM
NT = (((1,), (1,)), ((), ()))


def iota(shape, dim):
    return lax.broadcasted_iota(jnp.int32, shape, dim)


def round_up(value, step):
    return -(-value // step) * step


def dot(a, b):
    return jnp.dot(a, b, preferred_element_type=F32)


def dot_nt(a, b):
    return lax.dot_general(a, b, NT, preferred_element_type=F32)


def vmem_specs(count):
    return [pl.BlockSpec(memory_space=VMEM)] * count


def smem_spec():
    return pl.BlockSpec(memory_space=pltpu.SMEM)


def loop(count, body, carry):
    return lax.fori_loop(0, count, body, carry, unroll=count <= 4)


def call(kernel, out_shape, in_specs, scratch, cost, room, *args):
    single = not isinstance(out_shape, (tuple, list))
    return pl.pallas_call(
        kernel,
        out_shape=out_shape,
        in_specs=in_specs,
        out_specs=vmem_specs(1)[0] if single else vmem_specs(len(out_shape)),
        scratch_shapes=scratch,
        compiler_params=pltpu.CompilerParams(vmem_limit_bytes=room * 1024 * 1024),
        cost_estimate=pl.CostEstimate(flops=cost[0], bytes_accessed=cost[1], transcendentals=cost[2]),
    )(*args)


def pack_kernel(dests, cap, pixels, own, half_wide, count_ref, target_ref, flow_ref, hidden_ref, context_ref, out_ref, wide):
    slots = hidden_ref.shape[0]
    target = jnp.concatenate([target_ref[k : k + 1, :] for k in range(slots // 128)], axis=1)
    counted = iota((1, slots), 1) < count_ref[0]
    owner = target // pixels
    within = target % pixels
    belongs = (iota((dests, slots), 0) == owner) & counted
    member = jnp.where(belongs, 1.0, 0.0)
    upper = jnp.where(iota((128, 128), 0) <= iota((128, 128), 1), 1.0, 0.0).astype(BF16)
    before = jnp.zeros((dests, 1), F32)
    ranks = []
    for start in range(0, slots, 128):
        running = dot(member[:, start : start + 128].astype(BF16), upper) + before
        before = running[:, 127:128]
        ranks.append(running)
    rank = jnp.concatenate(ranks, axis=1) - 1.0 - (lax.axis_index("loop") * cap).astype(F32)
    belongs = belongs & (rank >= 0.0) & (rank < cap)
    place_at = jnp.sum(
        jnp.where(belongs, rank + iota((dests, slots), 0).astype(F32) * cap, 0.0), axis=0, keepdims=True
    )
    taken = jnp.max(jnp.where(belongs, 1.0, 0.0), axis=0, keepdims=True)
    landing = jnp.where(taken > 0.5, place_at, -1.0).astype(jnp.int32)
    row = iota((8, slots), 0)
    flow = flow_ref[...].astype(F32)
    side = jnp.where(row == 0, flow[0:1], 0.0)
    side = jnp.where(row == 1, flow[1:2], side)
    side = jnp.where(row == 2, (within // 256).astype(F32), side)
    side = jnp.where(row == 3, (within % 256).astype(F32), side)
    side = jnp.where(row == 4, 1.0, side).astype(BF16)
    hidden = hidden_ref[...]
    rows_hidden = round_up(cap, 16)
    together = max(1, min(dests, 192 // cap))
    for first in range(0, dests, together):
        spots = together * cap
        chosen = jnp.where(iota((spots, slots), 0) + first * cap == landing, 1.0, 0.0).astype(BF16)
        moved = dot(chosen, hidden)
        moved_side = dot_nt(side, chosen)
        for k in range(together):
            out_ref[first + k, 0:cap, :] = moved[k * cap : (k + 1) * cap].astype(BF16)
            for t in range(-(-cap // 128)):
                width = min(128, cap - t * 128)
                piece = moved_side[:, k * cap + t * 128 : k * cap + t * 128 + width]
                if width < 128:
                    piece = jnp.concatenate([piece, jnp.zeros((8, 128 - width), F32)], axis=1)
                base = rows_hidden + 8 * t
                out_ref[first + k, base : base + 8, :] = piece.astype(BF16)
    rows_per, width, _ = context_ref.shape
    top = out_ref.shape[1] - rows_per * WIN
    start = pl.multiple_of(lax.axis_index("loop") * (width // 2), 128)
    wide[...] = jnp.zeros_like(wide)
    for r in range(rows_per):
        wide[r, HALO : HALO + width, :] = context_ref[r].astype(F32)
        part = wide[r, pl.ds(start, half_wide), :]
        for j in range(dests):
            out_ref[j, top + r * WIN : top + (r + 1) * WIN, :] = part[j * own : j * own + WIN].astype(BF16)


def gather_slots(cap, got_ref, hidden, flow):
    rows_hidden = round_up(cap, 16)
    pixels = flow.shape[1]
    for j in range(got_ref.shape[0]):
        pieces = []
        for t in range(-(-cap // 128)):
            base = rows_hidden + 8 * t
            pieces.append(got_ref[j, base : base + 8, 0 : min(128, cap - t * 128)].astype(F32))
        side = pieces[0] if len(pieces) == 1 else jnp.concatenate(pieces, axis=1)
        place = jnp.where(side[4:5] > 0.5, side[2:3] * 256.0 + side[3:4], -1.0).astype(jnp.int32)
        chosen = jnp.where(iota((pixels, cap), 0) == place, 1.0, 0.0).astype(BF16)
        hidden = hidden + dot(chosen, got_ref[j, 0:cap, :])
        flow = flow + dot_nt(side.astype(BF16), chosen)
    return hidden, flow


def own_slots_kernel(cap, got_ref, hidden_ref, flow_ref):
    zeros = jnp.zeros(hidden_ref.shape, F32), jnp.zeros(flow_ref.shape, F32)
    hidden_ref[...], flow_ref[...] = gather_slots(cap, got_ref, *zeros)


def place_kernel(cap, half_wide, rows_per, got_ref, part_ref, flow_part_ref, ow_ref, hidden_ref, flow_ref, term_ref, wide_hidden, wide_term):
    half = lax.axis_index("loop")
    pixels = flow_ref.shape[1]
    width = pixels // rows_per
    hidden, flow = gather_slots(cap, got_ref, part_ref[...], flow_part_ref[...])
    flow_ref[...] = flow
    columns = flow.T
    ow = ow_ref[...]
    term = columns[:, 0:1] * (OFFSET_SCALE * (ow[4:5] - ow[0:1] - ow[2:3])) + columns[:, 1:2] * (
        OFFSET_SCALE * (ow[5:6] - ow[1:2] - ow[3:4])
    )
    start = pl.multiple_of(half * (width // 2), 128)
    for wide, value, out in ((wide_hidden, hidden, hidden_ref), (wide_term, term, term_ref)):
        wide[...] = jnp.zeros_like(wide)
        for r in range(rows_per):
            wide[r, HALO : HALO + width, :] = value[r * width : (r + 1) * width]
            out[r] = wide[r, pl.ds(start, half_wide), :].astype(out.dtype)


def match_kernel(
    count, flip, half_wide, rows_per, queries_ref, weight_ref, ow_ref, *refs
):
    key_refs, (keep_ref, send_ref, fine, coarse, scores, mixed, wide) = refs[:count], refs[count:]
    me, half = lax.axis_index("rows"), lax.axis_index("loop")
    pixels, channels = queries_ref.shape
    width = pixels // rows_per
    columns = width // 2
    quarter = columns // 2
    chunks = fine.shape[0]
    shards = chunks * 2
    per_ref = shards // count
    spread = jnp.where(
        iota((columns, columns), 1)
        == jnp.where(iota((columns, columns), 0) < quarter, 2 * iota((columns, columns), 0), 2 * (iota((columns, columns), 0) - quarter) + 1),
        1.0,
        0.0,
    ).astype(BF16)

    def sort_shard(ref, m, shard, lane):
        even, odd = [], []
        for r in range(rows_per):
            parted = dot(spread, ref[m, r])
            even.append(parted[:quarter])
            odd.append(parted[quarter:])
            for p, part in ((0, even[-1]), (1, odd[-1])):
                g = 2 * r + p
                fine[shard, g * 2 * quarter + lane * quarter : g * 2 * quarter + (lane + 1) * quarter, :] = part.astype(BF16)
        pooled = (even[0] + odd[0] + even[1] + odd[1]) * 0.25
        coarse[shard, lane * quarter : (lane + 1) * quarter, :] = pooled.astype(BF16)

    if per_ref == 1:
        for m in range(shards):
            sort_shard(key_refs[m], 0, m // 2, m % 2)
    else:
        def sort_chunk(c, carry):
            for lane in range(2):
                sort_shard(key_refs[0], c * 2 + lane, c, lane)
            return carry

        lax.fori_loop(0, chunks, sort_chunk, 0)

    group = 2 * quarter
    tile = scores.shape[1]
    lane = iota((1, group), 1)
    lane_col = ((lane % quarter) * 2 + half * columns).astype(F32)
    ow = ow_ref[...] * OFFSET_SCALE
    weight = weight_ref[...]

    def lane_row(c):
        arrival = c * 2 + lane // quarter
        shard = lax.bitwise_xor(arrival, me) if flip else arrival
        return (shard * rows_per).astype(F32)

    wide[...] = jnp.zeros_like(wide)

    def one_tile(t, carry):
        first = pl.multiple_of(t * tile, tile)
        queries = queries_ref[pl.ds(first, tile), :] * jnp.asarray(1.0 / math.sqrt(channels), BF16)

        def score(c, peaks):
            values = dot_nt(queries, fine[c])
            scores[c] = values
            parts = [values[:, g * group : (g + 1) * group] for g in range(4)]
            blended = (parts[0] + parts[1] + parts[2] + parts[3]) * 0.25
            high = jnp.maximum(jnp.maximum(parts[0], parts[1]), jnp.maximum(parts[2], parts[3]))
            return jnp.maximum(peaks[0], high), jnp.maximum(peaks[1], blended)

        low = jnp.full((tile, group), -jnp.inf, F32)
        peaks = loop(chunks, score, (low, low))
        peak_fine = jnp.max(peaks[0], axis=1, keepdims=True)
        peak_coarse = jnp.max(peaks[1], axis=1, keepdims=True)

        def absorb(c, so_far):
            total, below, right, rows, c_total, c_rows, acc_fine, acc_coarse = so_far
            parts = [scores[c, :, g * group : (g + 1) * group] for g in range(4)]
            blended = (parts[0] + parts[1] + parts[2] + parts[3]) * 0.25
            expo = [jnp.exp(part - peak_fine) for part in parts]
            c_expo = jnp.exp(blended - peak_coarse)
            lower = expo[2] + expo[3]
            everything = expo[0] + expo[1] + lower
            at = lane_row(c)
            weights = jnp.concatenate([e.astype(BF16) for e in expo], axis=1)
            return (
                total + everything,
                below + lower,
                right + (expo[1] + expo[3]),
                rows + everything * at,
                c_total + c_expo,
                c_rows + c_expo * at,
                acc_fine + dot(weights, fine[c]),
                acc_coarse + dot(c_expo.astype(BF16), coarse[c]),
            )

        zero = jnp.zeros((tile, group), F32)
        blank = jnp.zeros((tile, channels), F32)
        total, below, right, rows, c_total, c_rows, acc_fine, acc_coarse = loop(
            chunks, absorb, (zero, zero, zero, zero, zero, zero, blank, blank)
        )

        def over(value):
            return jnp.sum(value, axis=1, keepdims=True)

        pixel = first + iota((tile, 1), 0)
        own_row = (me * rows_per + pixel // width).astype(F32)
        own_col = (pixel % width).astype(F32)
        fine_sum, coarse_sum = over(total), over(c_total)
        fine_row = over(rows + below) / fine_sum - own_row
        fine_col = over(total * lane_col + right) / fine_sum - own_col
        coarse_row = over(c_rows) / coarse_sum + 0.5 - own_row
        coarse_col = over(c_total * lane_col) / coarse_sum + 0.5 - own_col
        fine_out = dot((acc_fine / fine_sum).astype(BF16), weight[:channels])
        coarse_out = dot((acc_coarse / coarse_sum).astype(BF16), weight[channels:])
        mixed[pl.ds(first, tile), 0:128] = fine_out + fine_row * ow[0:1] + fine_col * ow[1:2]
        mixed[pl.ds(first, tile), 128:256] = coarse_out + coarse_row * ow[2:3] + coarse_col * ow[3:4]
        mixed[pl.ds(first, tile), 256:384] = jnp.where(
            iota((tile, 128), 1) < 64,
            peak_fine + jnp.log(fine_sum),
            peak_coarse + jnp.log(coarse_sum),
        )
        return carry

    lax.fori_loop(0, pixels // tile, one_tile, 0)
    start = pl.multiple_of(half * columns, 128)
    other = pl.multiple_of((1 - half) * columns, 128)
    for r in range(rows_per):
        wide[r, HALO : HALO + width, :] = mixed[r * width : (r + 1) * width, :]
        keep_ref[r] = wide[r, pl.ds(start, half_wide), :]
        send_ref[r] = wide[r, pl.ds(other, half_wide), :]


def combine_kernel(keep_ref, got_ref, out_ref):
    for r in range(keep_ref.shape[0]):
        keep, got = keep_ref[r], got_ref[r]
        gap = got[:, 256:384] - keep[:, 256:384]
        share = 1.0 / (1.0 + jnp.exp(gap))
        out_ref[r] = (
            got[:, 0:128]
            + (keep[:, 0:128] - got[:, 0:128]) * share[:, 0:1]
            + got[:, 128:256]
            + (keep[:, 128:256] - got[:, 128:256]) * share[:, 64:65]
        )


def merge_kernel(own, base_ref, term_ref, hidden_ref, out_ref):
    dests = out_ref.shape[0]
    for r in range(base_ref.shape[0]):
        base = base_ref[r] + term_ref[r]
        hidden = hidden_ref[r].astype(F32)
        for j in range(dests):
            out_ref[j, r * WIN : (r + 1) * WIN, 0:128] = base[j * own : j * own + WIN].astype(BF16)
            out_ref[j, r * WIN : (r + 1) * WIN, 128:256] = hidden[j * own : j * own + WIN].astype(BF16)


def sigmoid(x):
    return 0.5 * jnp.tanh(0.5 * x) + 0.5


def shifted(value, tap):
    return value if tap == 2 else pltpu.roll(value, (2 - tap) % TILE, 0)


def each_tile(count, body):
    def step(t, carry):
        body(pl.multiple_of(t * TILE, TILE))
        return carry

    lax.fori_loop(0, count // TILE, step, 0, unroll=count == TILE)


def fetch(copies, sems, first=0):
    handles = []
    for k, (source, target) in enumerate(copies):
        handles.append(pltpu.make_async_copy(source, target, sems.at[first + k]))
        handles[-1].start()
    return handles


def context_kernel(early_ref, gate_hbm, state_hbm, bias_ref, fixed_ref, gate_ref, state_ref, padded, taps, sems):
    handles = fetch(
        [
            (gate_hbm.at[:, :, pl.ds(128, 128), :], gate_ref),
            (state_hbm.at[:, :, pl.ds(128, 128), :], state_ref),
        ],
        sems,
    )
    dests = early_ref.shape[0]
    count = fixed_ref.shape[1]
    per_dest = count // dests
    first = early_ref.shape[1] - per_dest
    pad = 2 * WIN
    padded[0:pad, :] = jnp.zeros((pad, 128), BF16)
    padded[pad + count : pad + count + pad, :] = jnp.zeros((pad, 128), BF16)
    for j in range(dests):
        padded[pad + j * per_dest : pad + (j + 1) * per_dest, :] = early_ref[j, first : first + per_dest, :]
    for handle in handles:
        handle.wait()
    for p in range(2):

        def one(at):
            for tap in range(5):
                if p == 0:
                    value = shifted(padded[pl.ds(pad + at, TILE), :].astype(F32), tap).astype(BF16)
                else:
                    value = padded[pl.ds(at + tap * WIN, TILE), :]
                taps[:, tap * 128 : (tap + 1) * 128] = value
            gate = gate_ref[p].reshape(640, 256)
            state = state_ref[p].reshape(640, 128)
            fixed_ref[p, pl.ds(at, TILE), 0:256] = dot(taps[...], gate) + bias_ref[p : p + 1, 0:256]
            fixed_ref[p, pl.ds(at, TILE), 256:384] = dot(taps[...], state) + bias_ref[p : p + 1, 256:384]

        each_tile(count, one)


def update_kernel(
    own, width, got_ref, fixed_ref, ow_ref, gate_hbm, state_hbm, head_ref, delta_ref,
    out_ref, base, hidden, motions, states, resets, updates, taps, flow, flow_cols, gate_ref, state_ref,
    slim_taps, slim_states, slim_motions, slim_resets, slim_hidden, sems,
):
    handles = []
    for p in range(2):
        for source, target in ((gate_hbm, gate_ref), (state_hbm, state_ref)):
            parts = [
                (source.at[p, :, pl.ds(256 * k, 128), :], target.at[p, :, pl.ds(128 * k, 128), :]) for k in range(2)
            ]
            handles.append(fetch(parts, sems, 2 * len(handles)))

    def ready(k):
        for handle in handles[k]:
            handle.wait()

    me, half = lax.axis_index("rows"), lax.axis_index("loop")
    dests, per_dest, _ = got_ref.shape
    rows_per = per_dest // WIN
    count = dests * per_dest
    pad = 2 * WIN
    first_col = (half * dests + me) * own - HALO
    column = first_col + iota((TILE, 128), 0) % WIN
    inside = (column >= 0) & (column < width)
    mask = jnp.where(inside, 1.0, 0.0)
    ow = ow_ref[...]
    add_row = OFFSET_SCALE * (ow[4:5] - ow[0:1] - ow[2:3])
    add_col = OFFSET_SCALE * (ow[5:6] - ow[1:2] - ow[3:4])

    for ref in (motions, states, resets):
        ref[0:pad, :] = jnp.zeros((pad, 128), BF16)
        ref[pad + count : pad + count + pad, :] = jnp.zeros((pad, 128), BF16)
    slim_pad = 2 * SLIM
    for ref in (slim_motions, slim_states, slim_resets):
        ref[0:slim_pad, :] = jnp.zeros((slim_pad, 128), BF16)
        ref[slim_pad + count // 2 :, :] = jnp.zeros((slim_pad, 128), BF16)
    for j in range(dests):
        at = j * per_dest
        base[at : at + per_dest, :] = got_ref[j, :, 0:128]
        hidden[at : at + per_dest, :] = got_ref[j, :, 128:256].astype(F32)

    def finish(at, update, candidate):
        old = hidden[pl.ds(at, TILE), :]
        new = (old + update * (candidate - old)) * mask
        hidden[pl.ds(at, TILE), :] = new
        return new

    def slim(value):
        cube = value.reshape(TILE // WIN, WIN, value.shape[1])
        return cube[:, HALO : HALO + SLIM, :].reshape(SLIM_TILE, value.shape[1])

    for iteration in range(ITERS):
        last = iteration == ITERS - 1

        def columns_pass(at):
            motion = base[pl.ds(at, TILE), :].astype(F32)
            if iteration > 0:
                moved = flow_cols[pl.ds(at, TILE), :]
                motion = (motion + moved[:, 0:1] * add_row + moved[:, 1:2] * add_col) * mask
            motion = jnp.maximum(motion, 0.0)
            rounded = motion.astype(BF16)
            if not last:
                motions[pl.ds(pad + at, TILE), :] = rounded
            motion = rounded.astype(F32)
            state = hidden[pl.ds(at, TILE), :].astype(BF16).astype(F32)
            for tap in range(5):
                taps[:, tap * 256 : tap * 256 + 128] = shifted(state, tap).astype(BF16)
                taps[:, tap * 256 + 128 : tap * 256 + 256] = shifted(motion, tap).astype(BF16)
            if iteration == 0 and count == TILE:
                ready(0)
            gates = sigmoid(dot(taps[...], gate_ref[0].reshape(1280, 256)) + fixed_ref[0, pl.ds(at, TILE), 0:256])
            reset = (gates[:, 128:256] * state).astype(BF16).astype(F32)
            if last:
                to = pl.multiple_of(at // 2, SLIM_TILE)
                for tap in range(5):
                    slim_taps[:, tap * 256 : tap * 256 + 128] = slim(shifted(reset, tap)).astype(BF16)
                    slim_taps[:, tap * 256 + 128 : tap * 256 + 256] = slim(shifted(motion, tap)).astype(BF16)
                candidate = jnp.tanh(
                    dot(slim_taps[...], state_ref[0].reshape(1280, 128)) + slim(fixed_ref[0, pl.ds(at, TILE), 256:384])
                )
                old = slim(hidden[pl.ds(at, TILE), :])
                new = old + slim(gates[:, 0:128]) * (candidate - old)
                slim_hidden[pl.ds(to, SLIM_TILE), :] = new
                slim_states[pl.ds(slim_pad + to, SLIM_TILE), :] = new.astype(BF16)
                slim_motions[pl.ds(slim_pad + to, SLIM_TILE), :] = slim(motion).astype(BF16)
                return
            for tap in range(5):
                taps[:, tap * 256 : tap * 256 + 128] = shifted(reset, tap).astype(BF16)
            if iteration == 0 and count == TILE:
                ready(1)
            candidate = jnp.tanh(dot(taps[...], state_ref[0].reshape(1280, 128)) + fixed_ref[0, pl.ds(at, TILE), 256:384])
            states[pl.ds(pad + at, TILE), :] = finish(at, gates[:, 0:128], candidate).astype(BF16)

        def fill(out, first, second, at, stride, size):
            for tap in range(5):
                out[:, tap * 256 : tap * 256 + 128] = first[pl.ds(at + tap * stride, size), :]
                out[:, tap * 256 + 128 : tap * 256 + 256] = second[pl.ds(at + tap * stride, size), :]

        def gate_rows(at):
            fill(taps, states, motions, at, WIN, TILE)
            gates = sigmoid(dot(taps[...], gate_ref[1].reshape(1280, 256)) + fixed_ref[1, pl.ds(at, TILE), 0:256])
            updates[pl.ds(at, TILE), :] = gates[:, 0:128]
            resets[pl.ds(pad + at, TILE), :] = (
                gates[:, 128:256] * states[pl.ds(pad + at, TILE), :].astype(F32)
            ).astype(BF16)

        def head(new):
            lifted = jnp.maximum(dot(new.astype(BF16), head_ref[...]), 0.0).astype(BF16)
            return dot_nt(delta_ref[...], lifted)

        def state_rows(at):
            fill(taps, resets, motions, at, WIN, TILE)
            candidate = jnp.tanh(
                dot(taps[...], state_ref[1].reshape(1280, 128)) + fixed_ref[1, pl.ds(at, TILE), 256:384]
            )
            new = finish(at, updates[pl.ds(at, TILE), :], candidate)
            flow_cols[pl.ds(at, TILE), :] = head(new).T

        def slim_gate_rows(at):
            to = pl.multiple_of(at // 2, SLIM_TILE)
            fill(slim_taps, slim_states, slim_motions, to, SLIM, SLIM_TILE)
            gates = sigmoid(
                dot(slim_taps[...], gate_ref[1].reshape(1280, 256)) + slim(fixed_ref[1, pl.ds(at, TILE), 0:256])
            )
            updates[pl.ds(to, SLIM_TILE), :] = gates[:, 0:128]
            slim_resets[pl.ds(slim_pad + to, SLIM_TILE), :] = (
                gates[:, 128:256] * slim_states[pl.ds(slim_pad + to, SLIM_TILE), :].astype(F32)
            ).astype(BF16)

        def slim_state_rows(at):
            to = pl.multiple_of(at // 2, SLIM_TILE)
            fill(slim_taps, slim_resets, slim_motions, to, SLIM, SLIM_TILE)
            candidate = jnp.tanh(
                dot(slim_taps[...], state_ref[1].reshape(1280, 128)) + slim(fixed_ref[1, pl.ds(at, TILE), 256:384])
            )
            old = slim_hidden[pl.ds(to, SLIM_TILE), :]
            new = old + updates[pl.ds(to, SLIM_TILE), :] * (candidate - old)
            slim_hidden[pl.ds(to, SLIM_TILE), :] = new
            flow[:, pl.ds(to, SLIM_TILE)] = head(new) + slim(flow_cols[pl.ds(at, TILE), :]).T

        if iteration == 0 and count != TILE:
            ready(0)
            ready(1)
        each_tile(count, columns_pass)
        if iteration == 0:
            ready(2)
            ready(3)
            each_tile(count, gate_rows)
            each_tile(count, state_rows)
        else:
            each_tile(count, slim_gate_rows)
            each_tile(count, slim_state_rows)

    for j in range(dests):
        for r in range(rows_per):
            at = j * rows_per * SLIM + r * SLIM
            out_ref[j, r * own : (r + 1) * own, :] = slim_hidden[at : at + own, :]
        moved = flow[:, j * rows_per * SLIM : (j + 1) * rows_per * SLIM]
        out_ref[j, rows_per * own : rows_per * own + 8, :] = jnp.concatenate(
            [moved, jnp.zeros((8, 128 - rows_per * SLIM), F32)], axis=1
        )


def finish_kernel(own, mine_ref, other_ref, first_ref, hidden_ref, flow_ref):
    half = lax.axis_index("loop")
    rows_per, width, _ = hidden_ref.shape
    columns = width // 2
    dests = mine_ref.shape[0]
    for ref, side in ((mine_ref, half), (other_ref, 1 - half)):
        start = pl.multiple_of(side * columns, 128)
        for r in range(rows_per):
            cells = [ref[j, r * own : (r + 1) * own, :] for j in range(dests)]
            hidden_ref[r, pl.ds(start, columns), :] = jnp.concatenate(cells, axis=0)
            moved = jnp.concatenate(
                [ref[j, rows_per * own : rows_per * own + 8, r * SLIM : r * SLIM + own] for j in range(dests)], axis=1
            )
            at = pl.multiple_of(r * width + side * columns, 128)
            total = first_ref[:, pl.ds(at, columns)] + moved
            for k in range(2):
                flow_ref[k, r : r + 1, pl.ds(start, columns)] = total[k : k + 1]


def local(
    frame_one,
    frame_two,
    context,
    carry_hidden,
    carry_flow,
    slot_target,
    slot_count,
    match_weight,
    offset_weight,
    gate_weight,
    state_weight,
    gru_bias,
    head_weight,
    delta_weight,
):
    dests = lax.axis_size("rows")
    halves = lax.axis_size("loop")
    rows_per, width, channels = frame_one.shape
    columns = frame_two.shape[1]
    pixels = rows_per * width
    slots, hidden_size = carry_hidden.shape
    cap = -(-slots // (dests * halves))
    own = columns // dests
    half_wide = round_up(columns - own + WIN, 8)
    padded = columns + half_wide
    room = 16 if dests <= 8 else 56

    rows_hidden = round_up(cap, 16)
    rows_slot = rows_hidden + 8 * (-(-cap // 128))
    shard = frame_two.reshape(1, rows_per, columns, channels)
    if dests == 8:

        def swap(value, flip):
            return lax.ppermute(value, "rows", [(i, i ^ flip) for i in range(dests)])

        beside, near, wrap, across = (swap(shard, flip) for flip in (1, 2, 6, 4))
        near_beside, wrap_beside = (swap(beside, flip) for flip in (2, 6))
    else:
        beside = lax.all_gather(shard, "rows", axis=0, tiled=True)
    slot_target, beside = lax.optimization_barrier((slot_target, beside))
    packed = call(
        functools.partial(pack_kernel, dests, cap, pixels, own, half_wide),
        jax.ShapeDtypeStruct((dests, rows_slot + rows_per * WIN, hidden_size), BF16),
        [smem_spec()] + vmem_specs(4),
        [pltpu.VMEM((rows_per, padded, 128), F32)],
        (2 * slots * slots * 128, 1 << 20, 0),
        60,
        slot_count,
        slot_target.reshape(slots // 128, 128),
        carry_flow.T,
        carry_hidden,
        context,
    )
    if dests == 8:
        packed, across = lax.optimization_barrier((packed, across))
        across_beside = swap(across, 1)
        packed, near, wrap, near_beside, wrap_beside, across_beside = lax.optimization_barrier(
            (packed, near, wrap, near_beside, wrap_beside, across_beside)
        )
        keys = (shard, beside, near, near_beside, across, across_beside, wrap, wrap_beside)
    else:
        keys = (beside,)
    early = lax.all_to_all(packed, "rows", 0, 0, tiled=True)
    around = [(i, (i + 1) % halves) for i in range(halves)]
    early_other = lax.ppermute(early, "loop", around)
    ow = jnp.pad(offset_weight, ((0, 2), (0, 0)))
    hidden_part, flow_part = call(
        functools.partial(own_slots_kernel, cap),
        (jax.ShapeDtypeStruct((pixels, 128), F32), jax.ShapeDtypeStruct((8, pixels), F32)),
        vmem_specs(1),
        [],
        (slots * pixels * 128, 1 << 20, 0),
        room,
        early,
    )
    hidden_wide, flow_first, term = call(
        functools.partial(place_kernel, cap, half_wide, rows_per),
        (
            jax.ShapeDtypeStruct((rows_per, half_wide, 128), BF16),
            jax.ShapeDtypeStruct((8, pixels), F32),
            jax.ShapeDtypeStruct((rows_per, half_wide, 128), F32),
        ),
        vmem_specs(4),
        [pltpu.VMEM((rows_per, padded, 128), F32)] * 2,
        (slots * pixels * 128, 1 << 20, 0),
        room,
        early_other,
        hidden_part,
        flow_part,
        ow,
    )
    queries = frame_one.reshape(pixels, channels)
    chunks = dests // 2
    tile = 256 if dests <= 8 else 128
    keep, send = call(
        functools.partial(match_kernel, len(keys), len(keys) > 1, half_wide, rows_per),
        (jax.ShapeDtypeStruct((rows_per, half_wide, 384), F32),) * 2,
        vmem_specs(3 + len(keys)),
        [
            pltpu.VMEM((chunks, 4 * columns, channels), BF16),
            pltpu.VMEM((chunks, columns, channels), BF16),
            pltpu.VMEM((chunks, tile, 4 * columns), F32),
            pltpu.VMEM((pixels, 384), F32),
            pltpu.VMEM((rows_per, padded, 384), F32),
        ],
        (4 * pixels * chunks * 4 * columns * channels, 1 << 21, pixels * chunks * 5 * columns),
        room,
        queries,
        match_weight,
        ow,
        *keys,
    )
    other = lax.ppermute(send, "loop", around)
    combined = call(
        combine_kernel,
        jax.ShapeDtypeStruct((rows_per, half_wide, 128), F32),
        vmem_specs(2),
        [],
        (0, 1 << 20, 0),
        room,
        keep,
        other,
    )
    sending = call(
        functools.partial(merge_kernel, own),
        jax.ShapeDtypeStruct((dests, rows_per * WIN, 256), BF16),
        vmem_specs(3),
        [],
        (0, 1 << 20, 0),
        room,
        combined,
        term,
        hidden_wide,
    )
    arrived = lax.all_to_all(sending, "rows", 0, 0, tiled=True)
    count = dests * rows_per * WIN
    back_rows = rows_per * own + 8
    hbm = pl.BlockSpec(memory_space=pltpu.HBM)
    gate_weight = pltpu.with_memory_space_constraint(gate_weight, pltpu.HBM)
    state_weight = pltpu.with_memory_space_constraint(state_weight, pltpu.HBM)
    fixed = call(
        context_kernel,
        jax.ShapeDtypeStruct((2, count, 384), F32),
        [vmem_specs(1)[0], hbm, hbm, vmem_specs(1)[0]],
        [
            pltpu.VMEM((2, 5, 128, 256), BF16),
            pltpu.VMEM((2, 5, 128, 128), BF16),
            pltpu.VMEM((count + 4 * WIN, 128), BF16),
            pltpu.VMEM((TILE, 640), BF16),
            pltpu.SemaphoreType.DMA((2,)),
        ],
        (4 * count * 5 * 128 * 384, 1 << 22, 0),
        room,
        early,
        gate_weight,
        state_weight,
        gru_bias,
    )
    outgoing = call(
        functools.partial(update_kernel, own, width),
        jax.ShapeDtypeStruct((dests, back_rows, 128), F32),
        vmem_specs(3) + [hbm, hbm] + vmem_specs(2),
        [
            pltpu.VMEM((count, 128), BF16),
            pltpu.VMEM((count, 128), F32),
            pltpu.VMEM((count + 4 * WIN, 128), BF16),
            pltpu.VMEM((count + 4 * WIN, 128), BF16),
            pltpu.VMEM((count + 4 * WIN, 128), BF16),
            pltpu.VMEM((count, 128), F32),
            pltpu.VMEM((TILE, 1280), BF16),
            pltpu.VMEM((8, count // 2), F32),
            pltpu.VMEM((count, 8), F32),
            pltpu.VMEM((2, 5, 256, 256), BF16),
            pltpu.VMEM((2, 5, 256, 128), BF16),
            pltpu.VMEM((SLIM_TILE, 1280), BF16),
            pltpu.VMEM((count // 2 + 4 * SLIM, 128), BF16),
            pltpu.VMEM((count // 2 + 4 * SLIM, 128), BF16),
            pltpu.VMEM((count // 2 + 4 * SLIM, 128), BF16),
            pltpu.VMEM((count // 2, 128), F32),
            pltpu.SemaphoreType.DMA((8,)),
        ],
        (8 * count * 5 * 256 * 384, 1 << 22, 8 * count * 384),
        room,
        arrived,
        fixed,
        ow,
        gate_weight,
        state_weight,
        head_weight,
        jnp.pad(delta_weight, ((0, 6), (0, 0))),
    )
    back = lax.all_to_all(outgoing, "rows", 0, 0, tiled=True)
    hidden_out, flow_out = call(
        functools.partial(finish_kernel, own),
        (
            jax.ShapeDtypeStruct((rows_per, width, hidden_size), F32),
            jax.ShapeDtypeStruct((2, rows_per, width), F32),
        ),
        vmem_specs(3),
        [],
        (0, 1 << 20, 0),
        room,
        back,
        lax.ppermute(back, "loop", around),
        flow_first,
    )
    return (hidden_out, flow_out)


def solution(mesh):
    return jax.shard_map(
        local,
        mesh=mesh,
        in_specs=(
            P(("groups", "rows"), None, None),
            P(("groups", "rows"), "loop", None),
            P(("groups", "rows"), None, None),
            P(("groups", "rows"), None),
            P(("groups", "rows"), None),
            P(("groups", "rows")),
            P(("groups", "rows")),
            P(),
            P(),
            P(),
            P(),
            P(),
            P(),
            P(),
        ),
        out_specs=(P(("groups", "rows"), None, None), P(None, ("groups", "rows"), None)),
        check_vma=False,
    )
```
